32 devices in a mesh: pool: 8 (over z, x), tp: 4 (over y, core).
Axes of the slice: x: 2, y: 2, z: 4, core: 2. Of those that a mesh axis runs over, the one named last changes fastest.
Arguments:
- hidden_rows: bfloat16 [1024, 8192], P('pool', 'tp'), may hold values from -6 to 6
- kv_weight: bfloat16 [8192, 1024], P('tp', 'pool'), may hold values from -0.0625 to 0.0625
- queries: bfloat16 [1024, 4096], P('pool', 'tp'), may hold values from -5 to 5
- cache_table: bfloat16 [64, 128, 1024], P('pool', None, 'tp'), may hold values from -5 to 5
- retrieval: int32 [8, 4], P('pool'), may hold values from 0 to 63, as said below
- pattern: int32 [8, 2, 4], P('pool'), may hold values 0 or 1
Outputs:
- attended: bfloat16 [1024, 4096], P('pool', 'tp')
- fresh_kv: bfloat16 [1024, 1024], P('pool', 'tp')
The draws below stay inside these ranges and needn't reach their ends.
Inputs may be any that keep to these rules, and one draw needn't show every extreme that they name: `retrieval`: each request names 4 blocks held by 4 different devices (block b is held by device b // 8); one device, drawn from the seed, holds a block named by every request.
All inputs are finite; a program needn't handle non-finite values. No bound on the sum of `pattern` on one device may be relied on, other than what follows from the above.
Results may differ from the reference program's by a relative error of at most 0.025.
Values may be sent and summed in bfloat16 or wider, within the bound.
A program may use at most 192 MiB of HBM per device.

```python
import jax
import jax.numpy as jnp
from jax import lax

D = 8192
HD = 128
QH = 32
KVH = 4
BLK = 128
RBLK = 64
R_BLOCKS = 2
CACHE_DEV = 8
R_DEV = 128
TOKENS = 1024
FETCH = 4
KVW = 1024
BLOCKS = 64
N_POOL = 8


def draw_queries(key, part):
    shape = (TOKENS, QH * HD)
    first = jax.random.fold_in(key, 5)
    return jnp.clip(jax.random.normal(first, shape, jnp.float32), -5.0, 5.0).astype(jnp.bfloat16)


def draw_cache_table(key, part):
    shape = (BLOCKS, BLK, KVW)
    first = jax.random.fold_in(key, 3)
    return jnp.clip(jax.random.normal(first, shape, jnp.float32), -5.0, 5.0).astype(jnp.bfloat16)


def draw_retrieval(key, part):
    keys = jax.random.split(jax.random.fold_in(key, 11), 4)
    hot = jax.random.randint(keys[0], (), 0, N_POOL)
    columns = jnp.arange(N_POOL)[None, :]
    rows = jnp.arange(N_POOL)[:, None]
    raw = jax.random.randint(keys[1], (N_POOL, N_POOL), 0, 2 ** 20) * N_POOL + columns
    raw = jnp.where(columns == hot, -1, raw)
    raw = jnp.where((rows == 0) & (columns == 0), -2, raw)
    raw = jnp.where((rows == 1) & (columns == N_POOL - 1), -2, raw)
    owners = jnp.argsort(raw, axis=1)[:, :FETCH]
    mixing = jax.random.randint(keys[2], (N_POOL, FETCH), 0, 2 ** 20) * FETCH + jnp.arange(FETCH)[None, :]
    order = jnp.argsort(mixing, axis=1)
    owners = jnp.take_along_axis(owners, order, axis=1)
    local = jax.random.randint(keys[3], (N_POOL, FETCH), 0, CACHE_DEV)
    row_ids = jnp.arange(N_POOL)[:, None]
    local = jnp.where((row_ids == 0) & (owners == 0), 0, local)
    local = jnp.where((row_ids == 1) & (owners == N_POOL - 1), CACHE_DEV - 1, local)
    return (owners * CACHE_DEV + local).astype(jnp.int32)


def set_ends(drawn, rng, low, top_value):
    spot = [jax.random.randint(jax.random.fold_in(rng, axis), (), 0, length) for axis, length in enumerate(drawn.shape)]
    longest = drawn.shape.index(max(drawn.shape))
    neighbour = spot[:longest] + [(spot[longest] + 1) % drawn.shape[longest]] + spot[longest + 1:]
    return drawn.at[tuple(spot)].set(low).at[tuple(neighbour)].set(top_value)


def block_levels(stream_key, extent, cuts, low, top_value):
    def one(axis_at, blocks):
        draws = jax.random.uniform(jax.random.fold_in(jax.random.fold_in(stream_key, 6), axis_at), (blocks,), jnp.float32, low / len(cuts), top_value / len(cuts))
        return jnp.repeat(jnp.exp(draws), extent[axis_at] // blocks).reshape((-1,) + (1,) * (len(extent) - axis_at - 1))

    gain = one(*cuts[0])
    for cut in cuts[1:]:
        gain = gain * one(*cut)
    return gain


def normal_values(own_key, shape, scale, limit, pieces=(), kind=jnp.bfloat16):
    array = scale * jax.random.normal(own_key, shape, jnp.float32)
    if pieces:
        array = array * block_levels(own_key, shape, pieces, -0.22, 0.18)
    return jnp.clip(array, -limit, limit).astype(kind)


def setup_inputs(seed: int = 0) -> dict:
    arg_keys = jax.random.split(jax.random.key(seed), 7)
    hidden_rows = normal_values(arg_keys[0], (TOKENS, D), 1.0, 6.0, ((0, 8), (1, 4)))
    kv_weight = normal_values(arg_keys[1], (D, KVW), D ** -0.5, 0.0625, ((0, 4), (1, 8)))
    queries = draw_queries(jax.random.fold_in(arg_keys[6], 71), 0)
    cache_table = draw_cache_table(jax.random.fold_in(arg_keys[6], 71), 0)
    retrieval = draw_retrieval(jax.random.fold_in(arg_keys[6], 71), 0)
    pattern = set_ends((jax.random.randint(arg_keys[5], (N_POOL, R_BLOCKS, FETCH), 0, 2) < 1).astype(jnp.int32), jax.random.fold_in(arg_keys[5], 1), 0, 1)
    return {"hidden_rows": hidden_rows, "kv_weight": kv_weight, "queries": queries, "cache_table": cache_table, "retrieval": retrieval, "pattern": pattern}


def attend_request(q_rows, own_kv, fetched, pat):
    group = QH // KVH
    scale = float(HD) ** -0.5
    count = q_rows.shape[0]
    qh = q_rows.reshape(count, KVH, group, HD).astype(jnp.float32)
    far = fetched.reshape(FETCH * BLK, KVH, 2, HD)
    near = own_kv.reshape(count, KVH, 2, HD)
    keys = jnp.concatenate([far[:, :, 0], near[:, :, 0]], axis=0).astype(jnp.float32)
    vals = jnp.concatenate([far[:, :, 1], near[:, :, 1]], axis=0).astype(jnp.float32)
    scores = jnp.einsum("rhgd,shd->hgrs", qh, keys) * scale
    far_mask = jnp.repeat(jnp.repeat(pat != 0, RBLK, axis=0), BLK, axis=1)
    near_mask = jnp.arange(count)[:, None] >= jnp.arange(count)[None, :]
    mask = jnp.concatenate([far_mask, near_mask], axis=1)
    scores = jnp.where(mask[None, None], scores, -jnp.inf)
    top = jnp.max(scores, axis=-1, keepdims=True)
    weights = jnp.where(mask[None, None], jnp.exp(scores - top), 0.0)
    denom = jnp.sum(weights, axis=-1)
    rounded = weights.astype(jnp.bfloat16)
    rounded = lax.optimization_barrier(rounded).astype(jnp.float32)
    numer = jnp.einsum("hgrs,shd->rhgd", rounded, vals)
    result = numer / jnp.transpose(denom, (2, 0, 1))[:, :, :, None]
    return result.reshape(count, QH * HD).astype(jnp.bfloat16)


def reference(hidden_rows, kv_weight, queries, cache_table, retrieval, pattern):
    fresh_kv = jnp.dot(hidden_rows, kv_weight, preferred_element_type=jnp.float32).astype(jnp.bfloat16)

    def one_request(items):
        q_rows, own_kv, wanted, pat = items
        fetched = jnp.take(cache_table, wanted, axis=0)
        return attend_request(q_rows, own_kv, fetched, pat)

    attended = lax.map(one_request, (queries.reshape(N_POOL, R_DEV, QH * HD), fresh_kv.reshape(N_POOL, R_DEV, KVW), retrieval, pattern))
    return attended.reshape(TOKENS, QH * HD), fresh_kv
```

```python
import math

import jax
import jax.numpy as jnp
from jax import lax
from jax.experimental import pallas as pl
from jax.experimental.pallas import tpu as pltpu
from jax.sharding import PartitionSpec as P

HD = 128
QH = 32
KVH = 4
BLK = 128
RBLK = 64


def rows_by_keys(left, right):
    return lax.dot_general(
        left, right, (((1,), (1,)), ((), ())), preferred_element_type=jnp.float32
    )


def body(hidden_rows, kv_weight, queries, cache_table, retrieval, pattern):
    partial_kv = jnp.dot(
        hidden_rows,
        lax.all_gather(kv_weight, "pool", axis=1, tiled=True),
        preferred_element_type=jnp.float32,
    )
    fresh = lax.psum_scatter(partial_kv.astype(jnp.bfloat16), "tp", scatter_dimension=1, tiled=True)
    wanted = retrieval[0]
    blocks_dev = cache_table.shape[0]
    npool = lax.axis_size("pool")
    owners = wanted // blocks_dev
    local = wanted % blocks_dev
    hits = (owners[:, None] == jnp.arange(npool, dtype=jnp.int32)[None, :]).astype(jnp.int32)
    request = jnp.sum(hits * (local + 1)[:, None], axis=0)
    incoming = lax.all_to_all(
        request.reshape(npool, 1), "pool", split_axis=0, concat_axis=0, tiled=True
    ).reshape(npool)
    reply = jnp.zeros((npool,) + cache_table.shape[1:], jnp.bfloat16)
    for slot in range(blocks_dev):
        reply = jnp.where((incoming == slot + 1)[:, None, None], cache_table[slot][None], reply)
    arrived = lax.all_to_all(reply, "pool", split_axis=0, concat_axis=0, tiled=True)
    fetched = jnp.take(arrived, owners, axis=0)
    count = hidden_rows.shape[0]
    fetch_count = wanted.shape[0]
    group = QH // KVH
    scale = float(HD) ** (-0.5)
    local_heads = fresh.shape[1] // (2 * HD)
    width = fetched.shape[2]
    per_step = math.gcd(fetch_count, 8)
    steps_count = fetch_count // per_step
    grouped = fetched.reshape(steps_count, per_step * BLK, width)
    pat_steps = jnp.transpose(
        pattern[0].reshape(pattern.shape[1], steps_count, per_step), (1, 0, 2)
    )
    token_of_row = jnp.arange(count * group) // group
    block_of_row = token_of_row // RBLK
    row_blocks = block_of_row[:, None, None] == jnp.arange(pattern.shape[1])[None, :, None]
    near_mask = token_of_row[:, None] >= jnp.arange(count)[None, :]
    q_heads = queries.reshape(count, local_heads, group * HD)
    q_rows = q_heads[:, 0].reshape(count * group, HD)
    near_keys = fresh[:, 0:HD]
    near_vals = fresh[:, HD : 2 * HD]
    near_scores = rows_by_keys(q_rows, near_keys) * scale
    top = jnp.max(jnp.where(near_mask, near_scores, -1e30), axis=1)
    weights = jnp.where(near_mask, jnp.exp(near_scores - top[:, None]), 0.0)
    total = jnp.sum(weights, axis=1)
    numer = jnp.dot(weights.astype(jnp.bfloat16), near_vals, preferred_element_type=jnp.float32)

    def visit(carry, items):
        top_now, total_now, numer_now = carry
        block_rows, pat_now = items
        keys = block_rows[:, 0:HD]
        vals = block_rows[:, HD : 2 * HD]
        scores = rows_by_keys(q_rows, keys) * scale
        row_pat = jnp.any(row_blocks & (pat_now[None] != 0), axis=1)
        mask = jnp.repeat(row_pat, BLK, axis=1)
        top_new = jnp.maximum(top_now, jnp.max(jnp.where(mask, scores, -1e30), axis=1))
        weights_now = jnp.where(mask, jnp.exp(scores - top_new[:, None]), 0.0)
        factor = jnp.exp(top_now - top_new)
        total_new = total_now * factor + jnp.sum(weights_now, axis=1)
        numer_new = numer_now * factor[:, None] + jnp.dot(
            weights_now.astype(jnp.bfloat16), vals, preferred_element_type=jnp.float32
        )
        return ((top_new, total_new, numer_new), None)

    (top, total, numer), unused = lax.scan(visit, (top, total, numer), (grouped, pat_steps))
    results = (numer / total[:, None]).reshape(count, group * HD)
    attended = results.astype(jnp.bfloat16)
    return (attended, fresh)


MESH = pl.DeviceIdType.MESH


def kernel(hid, wgt, q_ref, cache, retr, pat, att, fresh, hbuf, wbuf, pbuf, part, msg_out, msg_in,
           reply, arrived, kcat, vcat, h_recv, h_send, w_recv, w_send, m_recv, m_send, f_recv, f_send,
           s_recv, s_send):
    npool = 8
    blocks_dev = cache.shape[0]
    fetch = retr.shape[1]
    rows = hid.shape[0]
    me = lax.axis_index("pool")
    t = lax.axis_index("tp")
    z, x = lax.div(me, 2), lax.rem(me, 2)
    a, b = lax.div(z, 2), lax.rem(z, 2)
    y = lax.div(t, 2)
    pair = (2 * a + 1 - b) * 2 + x
    other = z * 2 + 1 - x
    far = (2 - a) * 2 + x

    def remote(src, dst, ssem, rsem, pool, tp=None):
        where = {"pool": pool} if tp is None else {"pool": pool, "tp": tp}
        return pltpu.make_async_remote_copy(
            src_ref=src, dst_ref=dst, send_sem=ssem, recv_sem=rsem, device_id=where, device_id_type=MESH
        )

    def rows_at(slot, count=1):
        return pl.ds(pl.multiple_of(slot * rows, rows), count * rows)

    def cols_at(slot):
        return pl.ds(pl.multiple_of(slot * HD, HD), HD)

    own_slot = b * 2 + x
    pair_slot = (1 - b) * 2 + x
    own_h = pltpu.make_async_copy(hid, hbuf.at[rows_at(own_slot)], h_recv.at[own_slot])
    own_h.start()

    @pl.when(a == b)
    def _():
        pltpu.make_async_copy(wgt, wbuf.at[:, cols_at(b)], w_recv.at[b]).start()

    barrier = pltpu.get_barrier_semaphore()
    for k in range(1, npool):
        pl.semaphore_signal(barrier, inc=1, device_id={"pool": lax.rem(me + k, npool)}, device_id_type=MESH)
    for sx in range(2):
        for k in range(1, 4):
            pl.semaphore_signal(
                barrier, inc=1,
                device_id={"pool": (2 * a + y) * 2 + sx, "tp": lax.rem(t + k, 4)}, device_id_type=MESH,
            )
    pl.semaphore_wait(barrier, npool - 1 + jnp.where(y == b, 4, 8))

    h_pair = remote(hid, hbuf.at[rows_at(own_slot)], h_send.at[0], h_recv.at[own_slot], pair)
    h_other = remote(hid, hbuf.at[rows_at(own_slot)], h_send.at[1], h_recv.at[own_slot], other)
    w_far = remote(wgt, wbuf.at[:, cols_at(b)], w_send.at[0], w_recv.at[b], far)
    w_near = remote(wgt, wbuf.at[:, cols_at(b)], w_send.at[1], w_recv.at[b], pair)

    wanted = [retr[0, f] for f in range(fetch)]
    owners = [lax.div(v, blocks_dev) for v in wanted]
    locals_ = [lax.rem(v, blocks_dev) for v in wanted]

    def slot_at(owner):
        total = jnp.int32(0)
        for f in range(fetch):
            total = total + jnp.where(owners[f] == owner, locals_[f], 0)
        return total

    ask = []
    for k in range(1, npool):
        owner = lax.rem(me + k, npool)
        msg_out[k] = jnp.full((8, 128), slot_at(owner), jnp.int32)
        ask.append(remote(msg_out.at[k], msg_in.at[k], m_send.at[k], m_recv.at[k], owner))
        ask[-1].start()
    h_pair.start()
    h_other.start()

    @pl.when(a != b)
    def _():
        w_far.start()

    arrived[me] = cache[slot_at(me)]
    answers = []
    for k in range(1, npool):
        ask[k - 1].wait_recv()
        reply[k] = cache[jnp.max(msg_in[k])]
        answers.append(
            remote(reply.at[k], arrived.at[me], f_send.at[k], f_recv.at[k], lax.rem(me + npool - k, npool))
        )

    h_pair.wait_send()

    @pl.when(a == b)
    def _():
        w_far.start()

    @pl.when(a != b)
    def _():
        w_near.start()

    def h_wait(slot):
        pltpu.make_async_copy(hid, hbuf.at[rows_at(slot)], h_recv.at[slot]).wait()

    h_wait(pair_slot)
    h_fwd = remote(hbuf.at[rows_at(pair_slot)], hbuf.at[rows_at(pair_slot)], h_send.at[2], h_recv.at[pair_slot], other)
    h_fwd.start()
    w_far.wait_send()

    @pl.when(a != b)
    def _():
        w_near.wait_send()

    for k in (4, 3, 5, 2, 6, 1, 7):
        answers[k - 1].start()

    h_wait(own_slot)
    h_wait(b * 2 + 1 - x)
    for s in range(2):
        pltpu.make_async_copy(wgt, wbuf.at[:, pl.ds(s * HD, HD)], w_recv.at[s]).wait()

    def project(zl):
        block = jnp.dot(hbuf[rows_at(zl * 2, 2)], wbuf[...], preferred_element_type=jnp.float32)
        for sx in range(2):
            for i in range(2):
                j = zl * 2 + sx
                src = pbuf.at[j, i]
                src[...] = block[sx * rows:(sx + 1) * rows, i * HD:(i + 1) * HD].astype(jnp.bfloat16)
                mine = jnp.logical_and(4 * a + j == me, 2 * b + i == t)

                @pl.when(mine)
                def _():
                    pltpu.make_async_copy(src, part.at[x, t], s_recv.at[x, t]).start()

                @pl.when(jnp.logical_not(mine))
                def _():
                    remote(src, part.at[x, t], s_send.at[j, i], s_recv.at[x, t], 4 * a + j, 2 * b + i).start()

    project(b)
    h_wait((1 - b) * 2 + 1 - x)
    project(1 - b)

    for k in range(1, npool):
        answers[k - 1].wait_recv()
    for f in range(fetch):
        block = arrived[owners[f]]
        kcat[f * BLK:(f + 1) * BLK] = block[:, 0:HD]
        vcat[f * BLK:(f + 1) * BLK] = block[:, HD:2 * HD]

    for kind, cat in ((0, kcat), (1, vcat)):
        total = jnp.zeros((rows, HD), jnp.float32)
        for s in range(4):
            pltpu.make_async_copy(pbuf.at[0, 0], part.at[kind, s], s_recv.at[kind, s]).wait()
            total = total + part[kind, s].astype(jnp.float32)
        total = total.astype(jnp.bfloat16)
        cat[fetch * BLK:] = total
        fresh[:, kind * HD:(kind + 1) * HD] = total

    keys_count = fetch * BLK + rows
    token = lax.broadcasted_iota(jnp.int32, (rows, BLK), 0)
    key = lax.broadcasted_iota(jnp.int32, (rows, BLK), 1)
    scale = float(HD) ** (-0.5)

    @pl.loop(0, q_ref.shape[1] // (2 * HD))
    def _(step):
        masks = []
        for f in range(fetch):
            allowed = jnp.zeros((rows, BLK), jnp.int32)
            for r in range(pat.shape[1]):
                allowed = jnp.where(lax.div(token, RBLK) == r, pat[0, r, f], allowed)
            masks.append(allowed != 0)
        masks.append(token >= key)
        for half in range(2):
            at = pl.ds(pl.multiple_of(step * 2 * HD + half * HD, HD), HD)
            raw = rows_by_keys(q_ref[:, at], kcat[...]) * scale
            scores = [jnp.where(masks[n], raw[:, n * BLK:(n + 1) * BLK], -1e30) for n in range(fetch + 1)]
            top = scores[0]
            for n in range(1, fetch + 1):
                top = jnp.maximum(top, scores[n])
            top = jnp.max(top, axis=1, keepdims=True)
            weights = [jnp.exp(s - top) for s in scores]
            denom = weights[0]
            for n in range(1, fetch + 1):
                denom = denom + weights[n]
            denom = jnp.sum(denom, axis=1, keepdims=True)
            rounded = jnp.concatenate([w.astype(jnp.bfloat16) for w in weights], axis=1)
            numer = jnp.dot(rounded, vcat[...], preferred_element_type=jnp.float32)
            att[:, at] = (numer / denom).astype(jnp.bfloat16)

    h_other.wait_send()
    h_fwd.wait_send()
    for k in range(1, npool):
        ask[k - 1].wait_send()
        answers[k - 1].wait_send()
    for j in range(4):
        for i in range(2):
            mine = jnp.logical_and(4 * a + j == me, 2 * b + i == t)

            @pl.when(jnp.logical_not(mine))
            def _():
                remote(pbuf.at[j, i], part.at[x, t], s_send.at[j, i], s_recv.at[x, t], 4 * a + j, 2 * b + i).wait_send()


def fused(hidden_rows, kv_weight, queries, cache_table, retrieval, pattern):
    rows, depth = hidden_rows.shape
    cols = kv_weight.shape[1]
    blocks_dev, _, width = cache_table.shape
    keys_count = retrieval.shape[1] * BLK + rows
    dma = pltpu.SemaphoreType.DMA
    vmem = pl.BlockSpec(memory_space=pltpu.VMEM)
    smem = pl.BlockSpec(memory_space=pltpu.SMEM)
    anyw = pl.BlockSpec(memory_space=pl.ANY)
    bf = jnp.bfloat16
    return pl.pallas_call(
        kernel,
        out_shape=(
            jax.ShapeDtypeStruct(queries.shape, bf),
            jax.ShapeDtypeStruct((rows, width), bf),
        ),
        in_specs=[anyw, anyw, vmem, vmem, smem, smem],
        out_specs=(vmem, vmem),
        scratch_shapes=[
            pltpu.VMEM((4 * rows, depth), bf),
            pltpu.VMEM((depth, 2 * cols), bf),
            pltpu.VMEM((4, 2, rows, HD), bf),
            pltpu.VMEM((2, 4, rows, HD), bf),
            pltpu.VMEM((8, 8, 128), jnp.int32),
            pltpu.VMEM((8, 8, 128), jnp.int32),
            pltpu.VMEM((8, BLK, width), bf),
            pltpu.VMEM((8, BLK, width), bf),
            pltpu.VMEM((keys_count, HD), bf),
            pltpu.VMEM((keys_count, HD), bf),
            dma((4,)), dma((3,)), dma((2,)), dma((2,)), dma((8,)), dma((8,)), dma((8,)), dma((8,)),
            dma((2, 4)), dma((4, 2)),
        ],
        compiler_params=pltpu.CompilerParams(
            collective_id=0, has_side_effects=True, vmem_limit_bytes=32 * 1024 * 1024
        ),
        name="blend",
    )(hidden_rows, kv_weight, queries, cache_table, retrieval, pattern)


def fits(mesh, hidden_rows, kv_weight, cache_table, retrieval):
    return (
        mesh.shape["pool"] == 8
        and mesh.shape["tp"] == 4
        and hidden_rows.shape[0] == 8 * BLK
        and kv_weight.shape[1] == 8 * HD
        and cache_table.shape[2] == 8 * HD
        and retrieval.shape[1] <= 8
    )


def solution(mesh):
    placed = (
        P("pool", "tp"),
        P("tp", "pool"),
        P("pool", "tp"),
        P("pool", None, "tp"),
        P("pool", None),
        P("pool", None, None),
    )

    def run(hidden_rows, kv_weight, queries, cache_table, retrieval, pattern):
        small = fits(mesh, hidden_rows, kv_weight, cache_table, retrieval)
        return jax.shard_map(
            fused if small else body,
            mesh=mesh,
            in_specs=placed,
            out_specs=(P("pool", "tp"), P("pool", "tp")),
            check_vma=False,
        )(hidden_rows, kv_weight, queries, cache_table, retrieval, pattern)

    return run
```

```python
import math

import jax
import jax.numpy as jnp
from jax import lax
from jax.experimental import pallas as pl
from jax.experimental.pallas import tpu as pltpu
from jax.sharding import PartitionSpec as P

HD = 128
QH = 32
KVH = 4
BLK = 128
RBLK = 64


def rows_by_keys(left, right):
    return lax.dot_general(
        left, right, (((1,), (1,)), ((), ())), preferred_element_type=jnp.float32
    )


def body(hidden_rows, kv_weight, queries, cache_table, retrieval, pattern):
    partial_kv = jnp.dot(
        hidden_rows,
        lax.all_gather(kv_weight, "pool", axis=1, tiled=True),
        preferred_element_type=jnp.float32,
    )
    fresh = lax.psum_scatter(partial_kv.astype(jnp.bfloat16), "tp", scatter_dimension=1, tiled=True)
    wanted = retrieval[0]
    blocks_dev = cache_table.shape[0]
    npool = lax.axis_size("pool")
    owners = wanted // blocks_dev
    local = wanted % blocks_dev
    hits = (owners[:, None] == jnp.arange(npool, dtype=jnp.int32)[None, :]).astype(jnp.int32)
    request = jnp.sum(hits * (local + 1)[:, None], axis=0)
    incoming = lax.all_to_all(
        request.reshape(npool, 1), "pool", split_axis=0, concat_axis=0, tiled=True
    ).reshape(npool)
    reply = jnp.zeros((npool,) + cache_table.shape[1:], jnp.bfloat16)
    for slot in range(blocks_dev):
        reply = jnp.where((incoming == slot + 1)[:, None, None], cache_table[slot][None], reply)
    arrived = lax.all_to_all(reply, "pool", split_axis=0, concat_axis=0, tiled=True)
    fetched = jnp.take(arrived, owners, axis=0)
    count = hidden_rows.shape[0]
    fetch_count = wanted.shape[0]
    group = QH // KVH
    scale = float(HD) ** (-0.5)
    local_heads = fresh.shape[1] // (2 * HD)
    width = fetched.shape[2]
    per_step = math.gcd(fetch_count, 8)
    steps_count = fetch_count // per_step
    grouped = fetched.reshape(steps_count, per_step * BLK, width)
    pat_steps = jnp.transpose(
        pattern[0].reshape(pattern.shape[1], steps_count, per_step), (1, 0, 2)
    )
    token_of_row = jnp.arange(count * group) // group
    block_of_row = token_of_row // RBLK
    row_blocks = block_of_row[:, None, None] == jnp.arange(pattern.shape[1])[None, :, None]
    near_mask = token_of_row[:, None] >= jnp.arange(count)[None, :]
    q_heads = queries.reshape(count, local_heads, group * HD)
    q_rows = q_heads[:, 0].reshape(count * group, HD)
    near_keys = fresh[:, 0:HD]
    near_vals = fresh[:, HD : 2 * HD]
    near_scores = rows_by_keys(q_rows, near_keys) * scale
    top = jnp.max(jnp.where(near_mask, near_scores, -1e30), axis=1)
    weights = jnp.where(near_mask, jnp.exp(near_scores - top[:, None]), 0.0)
    total = jnp.sum(weights, axis=1)
    numer = jnp.dot(weights.astype(jnp.bfloat16), near_vals, preferred_element_type=jnp.float32)

    def visit(carry, items):
        top_now, total_now, numer_now = carry
        block_rows, pat_now = items
        keys = block_rows[:, 0:HD]
        vals = block_rows[:, HD : 2 * HD]
        scores = rows_by_keys(q_rows, keys) * scale
        row_pat = jnp.any(row_blocks & (pat_now[None] != 0), axis=1)
        mask = jnp.repeat(row_pat, BLK, axis=1)
        top_new = jnp.maximum(top_now, jnp.max(jnp.where(mask, scores, -1e30), axis=1))
        weights_now = jnp.where(mask, jnp.exp(scores - top_new[:, None]), 0.0)
        factor = jnp.exp(top_now - top_new)
        total_new = total_now * factor + jnp.sum(weights_now, axis=1)
        numer_new = numer_now * factor[:, None] + jnp.dot(
            weights_now.astype(jnp.bfloat16), vals, preferred_element_type=jnp.float32
        )
        return ((top_new, total_new, numer_new), None)

    (top, total, numer), unused = lax.scan(visit, (top, total, numer), (grouped, pat_steps))
    results = (numer / total[:, None]).reshape(count, group * HD)
    attended = results.astype(jnp.bfloat16)
    return (attended, fresh)


MESH = pl.DeviceIdType.MESH


def kernel(hid, wgt, q_hbm, cache_hbm, retr_hbm, pat_hbm, att_hbm, fresh_hbm, hbuf, wbuf, pbuf, part,
           msg_out, msg_in, reply, arrived, kcat, vcat, q_ref, cache, retr, pat, att, fresh,
           h_recv, p_send, x_send, f_send, w_recv, w_send, v_send, m_recv, m_send, a_recv, a_send,
           s_recv, s_send, load_sem, out_sem):
    npool = 8
    blocks_dev = cache.shape[0]
    fetch = retr.shape[1]
    rows, depth = hid.shape
    half_rows, half_depth = rows // 2, depth // 2
    loads = [
        pltpu.make_async_copy(src, dst, load_sem.at[n])
        for n, (src, dst) in enumerate(((retr_hbm, retr), (cache_hbm, cache), (q_hbm, q_ref), (pat_hbm, pat)))
    ]
    for load in loads:
        load.start()
    me = lax.axis_index("pool")
    t = lax.axis_index("tp")
    z, x = lax.div(me, 2), lax.rem(me, 2)
    a, b = lax.div(z, 2), lax.rem(z, 2)
    y = lax.div(t, 2)
    pair = (2 * a + 1 - b) * 2 + x
    other = z * 2 + 1 - x
    far = (2 - a) * 2 + x

    def peer(k):
        pa = 1 - a if k & 4 else a
        pb = 1 - b if k & 2 else b
        return (2 * pa + pb) * 2 + (1 - x if k & 1 else x)

    def remote(src, dst, ssem, rsem, pool, tp=None):
        where = {"pool": pool} if tp is None else {"pool": pool, "tp": tp}
        return pltpu.make_async_remote_copy(
            src_ref=src, dst_ref=dst, send_sem=ssem, recv_sem=rsem, device_id=where, device_id_type=MESH
        )

    def rows_at(slot, count=1):
        return pl.ds(pl.multiple_of(slot * rows, rows), count * rows)

    def half_at(slot, c):
        return pl.ds(pl.multiple_of(slot * rows + c * half_rows, half_rows), half_rows)

    def cols_at(slot):
        return pl.ds(pl.multiple_of(slot * HD, HD), HD)

    own_slot = b * 2 + x
    pair_slot = (1 - b) * 2 + x
    halves = (0, 1)
    h_part = [hid.at[pl.ds(c * half_rows, half_rows)] for c in halves]
    w_part = [wgt.at[pl.ds(c * half_depth, half_depth)] for c in halves]
    w_land = [wbuf.at[pl.ds(c * half_depth, half_depth), cols_at(b)] for c in halves]

    barrier = pltpu.get_barrier_semaphore()
    for k in range(1, npool):
        pl.semaphore_signal(barrier, inc=1, device_id={"pool": peer(k)}, device_id_type=MESH)
    for sx in range(2):
        for k in range(1, 4):
            pl.semaphore_signal(
                barrier, inc=1,
                device_id={"pool": (2 * a + y) * 2 + sx, "tp": lax.rem(t + k, 4)}, device_id_type=MESH,
            )
    own_h = [pltpu.make_async_copy(h_part[c], hbuf.at[half_at(own_slot, c)], h_recv.at[own_slot, c]) for c in halves]
    for c in halves:
        own_h[c].start()

    @pl.when(a == b)
    def _():
        for c in halves:
            pltpu.make_async_copy(w_part[c], w_land[c], w_recv.at[b, c]).start()

    pl.semaphore_wait(barrier, npool - 1 + jnp.where(y == b, 4, 8))

    h_pair = [remote(h_part[c], hbuf.at[half_at(own_slot, c)], p_send.at[c], h_recv.at[own_slot, c], pair) for c in halves]
    h_other = [remote(h_part[c], hbuf.at[half_at(own_slot, c)], x_send.at[c], h_recv.at[own_slot, c], other) for c in halves]
    h_fwd = [
        remote(hbuf.at[half_at(pair_slot, c)], hbuf.at[half_at(pair_slot, c)], f_send.at[c], h_recv.at[pair_slot, c], other)
        for c in halves
    ]
    w_far = [remote(w_part[c], w_land[c], w_send.at[c], w_recv.at[b, c], far) for c in halves]
    w_near = [remote(w_part[c], w_land[c], v_send.at[c], w_recv.at[b, c], pair) for c in halves]

    for c in halves:
        h_pair[c].start()
    for c in halves:
        h_other[c].start()

    @pl.when(a != b)
    def _():
        for c in halves:
            w_far[c].start()

    loads[0].wait()
    wanted = [retr[0, f] for f in range(fetch)]
    owners = [lax.div(v, blocks_dev) for v in wanted]
    locals_ = [lax.rem(v, blocks_dev) for v in wanted]

    def slot_at(owner):
        total = jnp.int32(0)
        for f in range(fetch):
            total = total + jnp.where(owners[f] == owner, locals_[f], 0)
        return total

    ask, answers = [None], [None]
    for k in range(1, npool):
        msg_out[k] = jnp.full((8, 128), slot_at(peer(k)), jnp.int32)
        ask.append(remote(msg_out.at[k], msg_in.at[k], m_send.at[k], m_recv.at[k], peer(k)))
        ask[k].start()
    loads[1].wait()
    arrived[me] = cache[slot_at(me)]
    for k in range(1, npool):
        ask[k].wait_recv()
        reply[k] = cache[jnp.max(msg_in[k])]
        answers.append(remote(reply.at[k], arrived.at[me], a_send.at[k], a_recv.at[k], peer(k)))

    def h_wait(slot, c):
        pltpu.make_async_copy(h_part[c], hbuf.at[half_at(slot, c)], h_recv.at[slot, c]).wait()

    for c in halves:
        h_pair[c].wait_send()

        @pl.when(a == b)
        def _():
            w_far[c].start()

        @pl.when(a != b)
        def _():
            w_near[c].start()

        h_wait(pair_slot, c)
        h_fwd[c].start()
    for c in halves:
        w_far[c].wait_send()

        @pl.when(a != b)
        def _():
            w_near[c].wait_send()

        for k in ((6, 7, 4, 5), (2, 3, 1))[c]:
            answers[k].start()

    for c in halves:
        h_wait(own_slot, c)
        h_wait(b * 2 + 1 - x, c)
        for s in range(2):
            pltpu.make_async_copy(w_part[c], wbuf.at[pl.ds(c * half_depth, half_depth), pl.ds(s * HD, HD)], w_recv.at[s, c]).wait()

    def project(zl):
        block = jnp.dot(hbuf[rows_at(zl * 2, 2)], wbuf[...], preferred_element_type=jnp.float32)
        for sx in range(2):
            for i in range(2):
                j = zl * 2 + sx
                src = pbuf.at[j, i]
                src[...] = block[sx * rows:(sx + 1) * rows, i * HD:(i + 1) * HD].astype(jnp.bfloat16)
                mine = jnp.logical_and(4 * a + j == me, 2 * b + i == t)

                @pl.when(mine)
                def _():
                    pltpu.make_async_copy(src, part.at[x, t], s_recv.at[x, t]).start()

                @pl.when(jnp.logical_not(mine))
                def _():
                    remote(src, part.at[x, t], s_send.at[j, i], s_recv.at[x, t], 4 * a + j, 2 * b + i).start()

    project(b)
    for c in halves:
        h_wait((1 - b) * 2 + 1 - x, c)
    project(1 - b)

    for k in range(1, npool):
        answers[k].wait_recv()
    for f in range(fetch):
        block = arrived[owners[f]]
        kcat[f * BLK:(f + 1) * BLK] = block[:, 0:HD]
        vcat[f * BLK:(f + 1) * BLK] = block[:, HD:2 * HD]

    for kind, cat in ((0, kcat), (1, vcat)):
        total = jnp.zeros((rows, HD), jnp.float32)
        for s in range(4):
            pltpu.make_async_copy(pbuf.at[0, 0], part.at[kind, s], s_recv.at[kind, s]).wait()
            total = total + part[kind, s].astype(jnp.float32)
        total = total.astype(jnp.bfloat16)
        cat[fetch * BLK:] = total
        fresh[:, kind * HD:(kind + 1) * HD] = total
    fresh_out = pltpu.make_async_copy(fresh, fresh_hbm, out_sem.at[0])
    fresh_out.start()
    loads[2].wait()
    loads[3].wait()

    keys_count = fetch * BLK + rows
    token = lax.broadcasted_iota(jnp.int32, (rows, BLK), 0)
    key = lax.broadcasted_iota(jnp.int32, (rows, BLK), 1)
    scale = float(HD) ** (-0.5)

    @pl.loop(0, q_ref.shape[1] // (2 * HD))
    def _(step):
        masks = []
        for f in range(fetch):
            allowed = jnp.zeros((rows, BLK), jnp.int32)
            for r in range(pat.shape[1]):
                allowed = jnp.where(lax.div(token, RBLK) == r, pat[0, r, f], allowed)
            masks.append(allowed != 0)
        masks.append(token >= key)
        for half in range(2):
            at = pl.ds(pl.multiple_of(step * 2 * HD + half * HD, HD), HD)
            raw = rows_by_keys(q_ref[:, at], kcat[...]) * scale
            scores = [jnp.where(masks[n], raw[:, n * BLK:(n + 1) * BLK], -1e30) for n in range(fetch + 1)]
            top = scores[0]
            for n in range(1, fetch + 1):
                top = jnp.maximum(top, scores[n])
            top = jnp.max(top, axis=1, keepdims=True)
            weights = [jnp.exp(s - top) for s in scores]
            denom = weights[0]
            for n in range(1, fetch + 1):
                denom = denom + weights[n]
            denom = jnp.sum(denom, axis=1, keepdims=True)
            rounded = jnp.concatenate([w.astype(jnp.bfloat16) for w in weights], axis=1)
            numer = jnp.dot(rounded, vcat[...], preferred_element_type=jnp.float32)
            att[:, at] = (numer / denom).astype(jnp.bfloat16)
        at = pl.ds(pl.multiple_of(step * 2 * HD, 2 * HD), 2 * HD)
        pltpu.make_async_copy(att.at[:, at], att_hbm.at[:, at], out_sem.at[1 + step]).start()

    for c in halves:
        h_other[c].wait_send()
        h_fwd[c].wait_send()
    for k in range(1, npool):
        ask[k].wait_send()
        answers[k].wait_send()
    fresh_out.wait()
    for n in range(4):
        at = pl.ds(n * 2 * HD, 2 * HD)
        pltpu.make_async_copy(att.at[:, at], att_hbm.at[:, at], out_sem.at[1 + n]).wait()
    for j in range(4):
        for i in range(2):
            mine = jnp.logical_and(4 * a + j == me, 2 * b + i == t)

            @pl.when(jnp.logical_not(mine))
            def _():
                remote(pbuf.at[j, i], part.at[x, t], s_send.at[j, i], s_recv.at[x, t], 4 * a + j, 2 * b + i).wait_send()


def fused(hidden_rows, kv_weight, queries, cache_table, retrieval, pattern):
    rows, depth = hidden_rows.shape
    cols = kv_weight.shape[1]
    blocks_dev, _, width = cache_table.shape
    keys_count = retrieval.shape[1] * BLK + rows
    dma = pltpu.SemaphoreType.DMA
    anyw = pl.BlockSpec(memory_space=pl.ANY)
    bf = jnp.bfloat16
    return pl.pallas_call(
        kernel,
        out_shape=(
            jax.ShapeDtypeStruct(queries.shape, bf),
            jax.ShapeDtypeStruct((rows, width), bf),
        ),
        in_specs=[anyw] * 6,
        out_specs=(anyw, anyw),
        scratch_shapes=[
            pltpu.VMEM((4 * rows, depth), bf),
            pltpu.VMEM((depth, 2 * cols), bf),
            pltpu.VMEM((4, 2, rows, HD), bf),
            pltpu.VMEM((2, 4, rows, HD), bf),
            pltpu.VMEM((8, 8, 128), jnp.int32),
            pltpu.VMEM((8, 8, 128), jnp.int32),
            pltpu.VMEM((8, BLK, width), bf),
            pltpu.VMEM((8, BLK, width), bf),
            pltpu.VMEM((keys_count, HD), bf),
            pltpu.VMEM((keys_count, HD), bf),
            pltpu.VMEM(queries.shape, bf),
            pltpu.VMEM(cache_table.shape, bf),
            pltpu.SMEM(retrieval.shape, jnp.int32),
            pltpu.SMEM(pattern.shape, jnp.int32),
            pltpu.VMEM(queries.shape, bf),
            pltpu.VMEM((rows, width), bf),
            dma((4, 2)), dma((2,)), dma((2,)), dma((2,)), dma((2, 2)), dma((2,)), dma((2,)),
            dma((8,)), dma((8,)), dma((8,)), dma((8,)), dma((2, 4)), dma((4, 2)), dma((4,)), dma((5,)),
        ],
        compiler_params=pltpu.CompilerParams(
            collective_id=0, has_side_effects=True, vmem_limit_bytes=60 * 1024 * 1024
        ),
        name="blend",
    )(hidden_rows, kv_weight, queries, cache_table, retrieval, pattern)


def fits(mesh, hidden_rows, kv_weight, cache_table, retrieval):
    return (
        mesh.shape["pool"] == 8
        and mesh.shape["tp"] == 4
        and hidden_rows.shape[0] == 8 * BLK
        and kv_weight.shape[1] == 8 * HD
        and cache_table.shape[2] == 8 * HD
        and retrieval.shape[1] <= 8
    )


def solution(mesh):
    placed = (
        P("pool", "tp"),
        P("tp", "pool"),
        P("pool", "tp"),
        P("pool", None, "tp"),
        P("pool", None),
        P("pool", None, None),
    )

    def run(hidden_rows, kv_weight, queries, cache_table, retrieval, pattern):
        small = fits(mesh, hidden_rows, kv_weight, cache_table, retrieval)
        return jax.shard_map(
            fused if small else body,
            mesh=mesh,
            in_specs=placed,
            out_specs=(P("pool", "tp"), P("pool", "tp")),
            check_vma=False,
        )(hidden_rows, kv_weight, queries, cache_table, retrieval, pattern)

    return run
```

```python
import math

import jax
import jax.numpy as jnp
from jax import lax
from jax.experimental import pallas as pl
from jax.experimental.pallas import tpu as pltpu
from jax.sharding import PartitionSpec as P

HD = 128
QH = 32
KVH = 4
BLK = 128
RBLK = 64


def rows_by_keys(left, right):
    return lax.dot_general(
        left, right, (((1,), (1,)), ((), ())), preferred_element_type=jnp.float32
    )


def body(hidden_rows, kv_weight, queries, cache_table, retrieval, pattern):
    partial_kv = jnp.dot(
        hidden_rows,
        lax.all_gather(kv_weight, "pool", axis=1, tiled=True),
        preferred_element_type=jnp.float32,
    )
    fresh = lax.psum_scatter(partial_kv.astype(jnp.bfloat16), "tp", scatter_dimension=1, tiled=True)
    wanted = retrieval[0]
    blocks_dev = cache_table.shape[0]
    npool = lax.axis_size("pool")
    owners = wanted // blocks_dev
    local = wanted % blocks_dev
    hits = (owners[:, None] == jnp.arange(npool, dtype=jnp.int32)[None, :]).astype(jnp.int32)
    request = jnp.sum(hits * (local + 1)[:, None], axis=0)
    incoming = lax.all_to_all(
        request.reshape(npool, 1), "pool", split_axis=0, concat_axis=0, tiled=True
    ).reshape(npool)
    reply = jnp.zeros((npool,) + cache_table.shape[1:], jnp.bfloat16)
    for slot in range(blocks_dev):
        reply = jnp.where((incoming == slot + 1)[:, None, None], cache_table[slot][None], reply)
    arrived = lax.all_to_all(reply, "pool", split_axis=0, concat_axis=0, tiled=True)
    fetched = jnp.take(arrived, owners, axis=0)
    count = hidden_rows.shape[0]
    fetch_count = wanted.shape[0]
    group = QH // KVH
    scale = float(HD) ** (-0.5)
    local_heads = fresh.shape[1] // (2 * HD)
    width = fetched.shape[2]
    per_step = math.gcd(fetch_count, 8)
    steps_count = fetch_count // per_step
    grouped = fetched.reshape(steps_count, per_step * BLK, width)
    pat_steps = jnp.transpose(
        pattern[0].reshape(pattern.shape[1], steps_count, per_step), (1, 0, 2)
    )
    token_of_row = jnp.arange(count * group) // group
    block_of_row = token_of_row // RBLK
    row_blocks = block_of_row[:, None, None] == jnp.arange(pattern.shape[1])[None, :, None]
    near_mask = token_of_row[:, None] >= jnp.arange(count)[None, :]
    q_heads = queries.reshape(count, local_heads, group * HD)
    q_rows = q_heads[:, 0].reshape(count * group, HD)
    near_keys = fresh[:, 0:HD]
    near_vals = fresh[:, HD : 2 * HD]
    near_scores = rows_by_keys(q_rows, near_keys) * scale
    top = jnp.max(jnp.where(near_mask, near_scores, -1e30), axis=1)
    weights = jnp.where(near_mask, jnp.exp(near_scores - top[:, None]), 0.0)
    total = jnp.sum(weights, axis=1)
    numer = jnp.dot(weights.astype(jnp.bfloat16), near_vals, preferred_element_type=jnp.float32)

    def visit(carry, items):
        top_now, total_now, numer_now = carry
        block_rows, pat_now = items
        keys = block_rows[:, 0:HD]
        vals = block_rows[:, HD : 2 * HD]
        scores = rows_by_keys(q_rows, keys) * scale
        row_pat = jnp.any(row_blocks & (pat_now[None] != 0), axis=1)
        mask = jnp.repeat(row_pat, BLK, axis=1)
        top_new = jnp.maximum(top_now, jnp.max(jnp.where(mask, scores, -1e30), axis=1))
        weights_now = jnp.where(mask, jnp.exp(scores - top_new[:, None]), 0.0)
        factor = jnp.exp(top_now - top_new)
        total_new = total_now * factor + jnp.sum(weights_now, axis=1)
        numer_new = numer_now * factor[:, None] + jnp.dot(
            weights_now.astype(jnp.bfloat16), vals, preferred_element_type=jnp.float32
        )
        return ((top_new, total_new, numer_new), None)

    (top, total, numer), unused = lax.scan(visit, (top, total, numer), (grouped, pat_steps))
    results = (numer / total[:, None]).reshape(count, group * HD)
    attended = results.astype(jnp.bfloat16)
    return (attended, fresh)


MESH = pl.DeviceIdType.MESH


def kernel(hid, wgt, q_hbm, cache_hbm, retr_hbm, pat_hbm, att, fresh, hbuf, wbuf, wsrc, pbuf, part,
           msg_out, msg_in, reply, arrived, kcat, vcat, q_ref, cache, retr, pat,
           h_recv, p_send, x_send, f_send, w_recv, w_send, v_send, m_recv, m_send, a_recv, a_send,
           s_recv, s_send, load_sem):
    npool = 8
    blocks_dev = cache.shape[0]
    fetch = retr.shape[1]
    rows, depth = hid.shape
    half_rows, half_depth = rows // 2, depth // 2
    loads = [
        pltpu.make_async_copy(src, dst, load_sem.at[n])
        for n, (src, dst) in enumerate(((retr_hbm, retr), (cache_hbm, cache), (q_hbm, q_ref), (pat_hbm, pat), (wgt, wsrc)))
    ]
    loads[0].start()
    loads[4].start()
    me = lax.axis_index("pool")
    t = lax.axis_index("tp")
    z, x = lax.div(me, 2), lax.rem(me, 2)
    a, b = lax.div(z, 2), lax.rem(z, 2)
    y = lax.div(t, 2)
    pair = (2 * a + 1 - b) * 2 + x
    other = z * 2 + 1 - x
    far = (2 - a) * 2 + x

    def peer(k):
        pa = 1 - a if k & 4 else a
        pb = 1 - b if k & 2 else b
        return (2 * pa + pb) * 2 + (1 - x if k & 1 else x)

    def remote(src, dst, ssem, rsem, pool, tp=None):
        where = {"pool": pool} if tp is None else {"pool": pool, "tp": tp}
        return pltpu.make_async_remote_copy(
            src_ref=src, dst_ref=dst, send_sem=ssem, recv_sem=rsem, device_id=where, device_id_type=MESH
        )

    def rows_at(slot, count=1):
        return pl.ds(pl.multiple_of(slot * rows, rows), count * rows)

    def half_at(slot, c):
        return pl.ds(pl.multiple_of(slot * rows + c * half_rows, half_rows), half_rows)

    def cols_at(slot):
        return pl.ds(pl.multiple_of(slot * HD, HD), HD)

    own_slot = b * 2 + x
    pair_slot = (1 - b) * 2 + x
    halves = (0, 1)
    h_in = [hid.at[pl.ds(c * half_rows, half_rows)] for c in halves]
    w_in = [wgt.at[pl.ds(c * half_depth, half_depth)] for c in halves]
    h_part = [hbuf.at[half_at(own_slot, c)] for c in halves]
    w_part = [wsrc.at[pl.ds(c * half_depth, half_depth)] for c in halves]
    w_land = [wbuf.at[pl.ds(c * half_depth, half_depth), cols_at(b)] for c in halves]

    own_h = [pltpu.make_async_copy(h_in[c], hbuf.at[half_at(own_slot, c)], h_recv.at[own_slot, c]) for c in halves]
    for c in halves:
        own_h[c].start()

    @pl.when(a == b)
    def _():
        for c in halves:
            pltpu.make_async_copy(w_in[c], w_land[c], w_recv.at[b, c]).start()

    for n in (1, 3, 2):
        loads[n].start()
    barrier = pltpu.get_barrier_semaphore()
    for k in range(1, npool):
        pl.semaphore_signal(barrier, inc=1, device_id={"pool": peer(k)}, device_id_type=MESH)
    for sx in range(2):
        for k in range(1, 4):
            pl.semaphore_signal(
                barrier, inc=1,
                device_id={"pool": (2 * a + y) * 2 + sx, "tp": lax.rem(t + k, 4)}, device_id_type=MESH,
            )
    for c in halves:
        own_h[c].wait()
    loads[4].wait()
    loads[0].wait()
    pl.semaphore_wait(barrier, npool - 1 + jnp.where(y == b, 4, 8))

    h_pair = [remote(h_part[c], hbuf.at[half_at(own_slot, c)], p_send.at[c], h_recv.at[own_slot, c], pair) for c in halves]
    h_other = [remote(h_part[c], hbuf.at[half_at(own_slot, c)], x_send.at[c], h_recv.at[own_slot, c], other) for c in halves]
    h_fwd = [
        remote(hbuf.at[half_at(pair_slot, c)], hbuf.at[half_at(pair_slot, c)], f_send.at[c], h_recv.at[pair_slot, c], other)
        for c in halves
    ]
    w_far = [remote(w_part[c], w_land[c], w_send.at[c], w_recv.at[b, c], far) for c in halves]
    w_near = [remote(w_part[c], w_land[c], v_send.at[c], w_recv.at[b, c], pair) for c in halves]

    for c in halves:
        h_pair[c].start()
    for c in halves:
        h_other[c].start()

    @pl.when(a != b)
    def _():
        for c in halves:
            w_far[c].start()

    wanted = [retr[0, f] for f in range(fetch)]
    owners = [lax.div(v, blocks_dev) for v in wanted]
    locals_ = [lax.rem(v, blocks_dev) for v in wanted]

    def slot_at(owner):
        total = jnp.int32(0)
        for f in range(fetch):
            total = total + jnp.where(owners[f] == owner, locals_[f], 0)
        return total

    ask, answers = [None], [None]
    for k in range(1, npool):
        msg_out[k] = jnp.full((8, 128), slot_at(peer(k)), jnp.int32)
        ask.append(remote(msg_out.at[k], msg_in.at[k], m_send.at[k], m_recv.at[k], peer(k)))
        ask[k].start()
    loads[1].wait()
    arrived[me] = cache[slot_at(me)]
    for k in range(1, npool):
        ask[k].wait_recv()
        reply[k] = cache[jnp.max(msg_in[k])]
        answers.append(remote(reply.at[k], arrived.at[me], a_send.at[k], a_recv.at[k], peer(k)))

    def h_wait(slot, c):
        pltpu.make_async_copy(h_in[c], hbuf.at[half_at(slot, c)], h_recv.at[slot, c]).wait()

    for c in halves:
        h_pair[c].wait_send()

        @pl.when(a == b)
        def _():
            w_far[c].start()

        @pl.when(a != b)
        def _():
            w_near[c].start()

        h_wait(pair_slot, c)
        h_fwd[c].start()
    for c in halves:
        w_far[c].wait_send()

        @pl.when(a != b)
        def _():
            w_near[c].wait_send()

        for k in ((6, 7, 4, 5), (2, 3, 1))[c]:
            answers[k].start()

    for c in halves:
        h_wait(b * 2 + 1 - x, c)
        for s in range(2):
            pltpu.make_async_copy(w_part[c], wbuf.at[pl.ds(c * half_depth, half_depth), pl.ds(s * HD, HD)], w_recv.at[s, c]).wait()

    def project(zl):
        block = jnp.dot(hbuf[rows_at(zl * 2, 2)], wbuf[...], preferred_element_type=jnp.float32)
        for sx in range(2):
            for i in range(2):
                j = zl * 2 + sx
                src = pbuf.at[j, i]
                src[...] = block[sx * rows:(sx + 1) * rows, i * HD:(i + 1) * HD].astype(jnp.bfloat16)
                mine = jnp.logical_and(4 * a + j == me, 2 * b + i == t)

                @pl.when(mine)
                def _():
                    pltpu.make_async_copy(src, part.at[x, t], s_recv.at[x, t]).start()

                @pl.when(jnp.logical_not(mine))
                def _():
                    remote(src, part.at[x, t], s_send.at[j, i], s_recv.at[x, t], 4 * a + j, 2 * b + i).start()

    project(b)
    for c in halves:
        h_wait((1 - b) * 2 + 1 - x, c)
    project(1 - b)

    for k in range(1, npool):
        answers[k].wait_recv()
    for f in range(fetch):
        block = arrived[owners[f]]
        kcat[f * BLK:(f + 1) * BLK] = block[:, 0:HD]
        vcat[f * BLK:(f + 1) * BLK] = block[:, HD:2 * HD]

    for kind, cat in ((0, kcat), (1, vcat)):
        total = jnp.zeros((rows, HD), jnp.float32)
        for s in range(4):
            pltpu.make_async_copy(pbuf.at[0, 0], part.at[kind, s], s_recv.at[kind, s]).wait()
            total = total + part[kind, s].astype(jnp.float32)
        total = total.astype(jnp.bfloat16)
        cat[fetch * BLK:] = total
        fresh[:, kind * HD:(kind + 1) * HD] = total
    loads[2].wait()
    loads[3].wait()

    keys_count = fetch * BLK + rows
    token = lax.broadcasted_iota(jnp.int32, (rows, BLK), 0)
    key = lax.broadcasted_iota(jnp.int32, (rows, BLK), 1)
    scale = float(HD) ** (-0.5)

    @pl.loop(0, q_ref.shape[1] // (2 * HD))
    def _(step):
        masks = []
        for f in range(fetch):
            allowed = jnp.zeros((rows, BLK), jnp.int32)
            for r in range(pat.shape[1]):
                allowed = jnp.where(lax.div(token, RBLK) == r, pat[0, r, f], allowed)
            masks.append(allowed != 0)
        masks.append(token >= key)
        for half in range(2):
            at = pl.ds(pl.multiple_of(step * 2 * HD + half * HD, HD), HD)
            raw = rows_by_keys(q_ref[:, at], kcat[...]) * scale
            scores = [jnp.where(masks[n], raw[:, n * BLK:(n + 1) * BLK], -1e30) for n in range(fetch + 1)]
            top = scores[0]
            for n in range(1, fetch + 1):
                top = jnp.maximum(top, scores[n])
            top = jnp.max(top, axis=1, keepdims=True)
            weights = [jnp.exp(s - top) for s in scores]
            denom = weights[0]
            for n in range(1, fetch + 1):
                denom = denom + weights[n]
            denom = jnp.sum(denom, axis=1, keepdims=True)
            rounded = jnp.concatenate([w.astype(jnp.bfloat16) for w in weights], axis=1)
            numer = jnp.dot(rounded, vcat[...], preferred_element_type=jnp.float32)
            att[:, at] = (numer / denom).astype(jnp.bfloat16)

    for c in halves:
        h_other[c].wait_send()
        h_fwd[c].wait_send()
    for k in range(1, npool):
        ask[k].wait_send()
        answers[k].wait_send()
    for j in range(4):
        for i in range(2):
            mine = jnp.logical_and(4 * a + j == me, 2 * b + i == t)

            @pl.when(jnp.logical_not(mine))
            def _():
                remote(pbuf.at[j, i], part.at[x, t], s_send.at[j, i], s_recv.at[x, t], 4 * a + j, 2 * b + i).wait_send()


def fused(hidden_rows, kv_weight, queries, cache_table, retrieval, pattern):
    rows, depth = hidden_rows.shape
    cols = kv_weight.shape[1]
    blocks_dev, _, width = cache_table.shape
    keys_count = retrieval.shape[1] * BLK + rows
    dma = pltpu.SemaphoreType.DMA
    hbm = pl.BlockSpec(memory_space=pltpu.HBM)
    vmem = pl.BlockSpec(memory_space=pltpu.VMEM)
    bf = jnp.bfloat16
    return pl.pallas_call(
        kernel,
        out_shape=(
            pltpu.VMEM(queries.shape, bf),
            pltpu.VMEM((rows, width), bf),
        ),
        in_specs=[hbm] * 6,
        out_specs=(vmem, vmem),
        scratch_shapes=[
            pltpu.VMEM((4 * rows, depth), bf),
            pltpu.VMEM((depth, 2 * cols), bf),
            pltpu.VMEM((depth, cols), bf),
            pltpu.VMEM((4, 2, rows, HD), bf),
            pltpu.VMEM((2, 4, rows, HD), bf),
            pltpu.VMEM((8, 8, 128), jnp.int32),
            pltpu.VMEM((8, 8, 128), jnp.int32),
            pltpu.VMEM((8, BLK, width), bf),
            pltpu.VMEM((8, BLK, width), bf),
            pltpu.VMEM((keys_count, HD), bf),
            pltpu.VMEM((keys_count, HD), bf),
            pltpu.VMEM(queries.shape, bf),
            pltpu.VMEM(cache_table.shape, bf),
            pltpu.SMEM(retrieval.shape, jnp.int32),
            pltpu.SMEM(pattern.shape, jnp.int32),
            dma((4, 2)), dma((2,)), dma((2,)), dma((2,)), dma((2, 2)), dma((2,)), dma((2,)),
            dma((8,)), dma((8,)), dma((8,)), dma((8,)), dma((2, 4)), dma((4, 2)), dma((5,)),
        ],
        compiler_params=pltpu.CompilerParams(
            collective_id=0, has_side_effects=True, vmem_limit_bytes=62 * 1024 * 1024
        ),
        name="blend",
    )(hidden_rows, kv_weight, queries, cache_table, retrieval, pattern)


def fits(mesh, hidden_rows, kv_weight, cache_table, retrieval):
    return (
        mesh.shape["pool"] == 8
        and mesh.shape["tp"] == 4
        and hidden_rows.shape[0] == 8 * BLK
        and kv_weight.shape[1] == 8 * HD
        and cache_table.shape[2] == 8 * HD
        and retrieval.shape[1] <= 8
    )


def solution(mesh):
    placed = (
        P("pool", "tp"),
        P("tp", "pool"),
        P("pool", "tp"),
        P("pool", None, "tp"),
        P("pool", None),
        P("pool", None, None),
    )

    def run(hidden_rows, kv_weight, queries, cache_table, retrieval, pattern):
        small = fits(mesh, hidden_rows, kv_weight, cache_table, retrieval)
        return jax.shard_map(
            fused if small else body,
            mesh=mesh,
            in_specs=placed,
            out_specs=(P("pool", "tp"), P("pool", "tp")),
            check_vma=False,
        )(hidden_rows, kv_weight, queries, cache_table, retrieval, pattern)

    return run
```

```python
import math

import jax
import jax.numpy as jnp
from jax import lax
from jax.experimental import pallas as pl
from jax.experimental.pallas import tpu as pltpu
from jax.sharding import PartitionSpec as P

HD = 128
QH = 32
KVH = 4
BLK = 128
RBLK = 64


def rows_by_keys(left, right):
    return lax.dot_general(
        left, right, (((1,), (1,)), ((), ())), preferred_element_type=jnp.float32
    )


def body(hidden_rows, kv_weight, queries, cache_table, retrieval, pattern):
    partial_kv = jnp.dot(
        hidden_rows,
        lax.all_gather(kv_weight, "pool", axis=1, tiled=True),
        preferred_element_type=jnp.float32,
    )
    fresh = lax.psum_scatter(partial_kv.astype(jnp.bfloat16), "tp", scatter_dimension=1, tiled=True)
    wanted = retrieval[0]
    blocks_dev = cache_table.shape[0]
    npool = lax.axis_size("pool")
    owners = wanted // blocks_dev
    local = wanted % blocks_dev
    hits = (owners[:, None] == jnp.arange(npool, dtype=jnp.int32)[None, :]).astype(jnp.int32)
    request = jnp.sum(hits * (local + 1)[:, None], axis=0)
    incoming = lax.all_to_all(
        request.reshape(npool, 1), "pool", split_axis=0, concat_axis=0, tiled=True
    ).reshape(npool)
    reply = jnp.zeros((npool,) + cache_table.shape[1:], jnp.bfloat16)
    for slot in range(blocks_dev):
        reply = jnp.where((incoming == slot + 1)[:, None, None], cache_table[slot][None], reply)
    arrived = lax.all_to_all(reply, "pool", split_axis=0, concat_axis=0, tiled=True)
    fetched = jnp.take(arrived, owners, axis=0)
    count = hidden_rows.shape[0]
    fetch_count = wanted.shape[0]
    group = QH // KVH
    scale = float(HD) ** (-0.5)
    local_heads = fresh.shape[1] // (2 * HD)
    width = fetched.shape[2]
    per_step = math.gcd(fetch_count, 8)
    steps_count = fetch_count // per_step
    grouped = fetched.reshape(steps_count, per_step * BLK, width)
    pat_steps = jnp.transpose(
        pattern[0].reshape(pattern.shape[1], steps_count, per_step), (1, 0, 2)
    )
    token_of_row = jnp.arange(count * group) // group
    block_of_row = token_of_row // RBLK
    row_blocks = block_of_row[:, None, None] == jnp.arange(pattern.shape[1])[None, :, None]
    near_mask = token_of_row[:, None] >= jnp.arange(count)[None, :]
    q_heads = queries.reshape(count, local_heads, group * HD)
    q_rows = q_heads[:, 0].reshape(count * group, HD)
    near_keys = fresh[:, 0:HD]
    near_vals = fresh[:, HD : 2 * HD]
    near_scores = rows_by_keys(q_rows, near_keys) * scale
    top = jnp.max(jnp.where(near_mask, near_scores, -1e30), axis=1)
    weights = jnp.where(near_mask, jnp.exp(near_scores - top[:, None]), 0.0)
    total = jnp.sum(weights, axis=1)
    numer = jnp.dot(weights.astype(jnp.bfloat16), near_vals, preferred_element_type=jnp.float32)

    def visit(carry, items):
        top_now, total_now, numer_now = carry
        block_rows, pat_now = items
        keys = block_rows[:, 0:HD]
        vals = block_rows[:, HD : 2 * HD]
        scores = rows_by_keys(q_rows, keys) * scale
        row_pat = jnp.any(row_blocks & (pat_now[None] != 0), axis=1)
        mask = jnp.repeat(row_pat, BLK, axis=1)
        top_new = jnp.maximum(top_now, jnp.max(jnp.where(mask, scores, -1e30), axis=1))
        weights_now = jnp.where(mask, jnp.exp(scores - top_new[:, None]), 0.0)
        factor = jnp.exp(top_now - top_new)
        total_new = total_now * factor + jnp.sum(weights_now, axis=1)
        numer_new = numer_now * factor[:, None] + jnp.dot(
            weights_now.astype(jnp.bfloat16), vals, preferred_element_type=jnp.float32
        )
        return ((top_new, total_new, numer_new), None)

    (top, total, numer), unused = lax.scan(visit, (top, total, numer), (grouped, pat_steps))
    results = (numer / total[:, None]).reshape(count, group * HD)
    attended = results.astype(jnp.bfloat16)
    return (attended, fresh)


MESH = pl.DeviceIdType.MESH


def kernel(hid, wgt, q_hbm, cache_hbm, retr_hbm, pat_hbm, att, fresh, hbuf, wbuf, wsrc, pbuf, part,
           msg_out, msg_in, reply, arrived, top_ref, sum_ref, acc_ref, q_ref, cache, retr, pat,
           h_recv, p_send, x_send, f_send, w_recv, w_send, v_send, m_recv, m_send, a_recv, a_send,
           s_recv, s_send, load_sem):
    npool = 8
    blocks_dev = cache.shape[0]
    fetch = retr.shape[1]
    rows, depth = hid.shape
    half_rows, half_depth = rows // 2, depth // 2
    loads = [
        pltpu.make_async_copy(src, dst, load_sem.at[n])
        for n, (src, dst) in enumerate(((retr_hbm, retr), (cache_hbm, cache), (q_hbm, q_ref), (pat_hbm, pat), (wgt, wsrc)))
    ]
    loads[0].start()
    loads[4].start()
    me = lax.axis_index("pool")
    t = lax.axis_index("tp")
    z, x = lax.div(me, 2), lax.rem(me, 2)
    a, b = lax.div(z, 2), lax.rem(z, 2)
    y = lax.div(t, 2)
    pair = (2 * a + 1 - b) * 2 + x
    other = z * 2 + 1 - x
    far = (2 - a) * 2 + x

    def peer(k):
        pa = 1 - a if k & 4 else a
        pb = 1 - b if k & 2 else b
        return (2 * pa + pb) * 2 + (1 - x if k & 1 else x)

    def remote(src, dst, ssem, rsem, pool, tp=None):
        where = {"pool": pool} if tp is None else {"pool": pool, "tp": tp}
        return pltpu.make_async_remote_copy(
            src_ref=src, dst_ref=dst, send_sem=ssem, recv_sem=rsem, device_id=where, device_id_type=MESH
        )

    def rows_at(slot, count=1):
        return pl.ds(pl.multiple_of(slot * rows, rows), count * rows)

    def half_at(slot, c):
        return pl.ds(pl.multiple_of(slot * rows + c * half_rows, half_rows), half_rows)

    def cols_at(slot):
        return pl.ds(pl.multiple_of(slot * HD, HD), HD)

    own_slot = b * 2 + x
    pair_slot = (1 - b) * 2 + x
    halves = (0, 1)
    h_in = [hid.at[pl.ds(c * half_rows, half_rows)] for c in halves]
    w_in = [wgt.at[pl.ds(c * half_depth, half_depth)] for c in halves]
    h_part = [hbuf.at[half_at(own_slot, c)] for c in halves]
    w_part = [wsrc.at[pl.ds(c * half_depth, half_depth)] for c in halves]
    w_land = [wbuf.at[pl.ds(c * half_depth, half_depth), cols_at(b)] for c in halves]

    own_h = [pltpu.make_async_copy(h_in[c], hbuf.at[half_at(own_slot, c)], h_recv.at[own_slot, c]) for c in halves]
    for c in halves:
        own_h[c].start()

    @pl.when(a == b)
    def _():
        for c in halves:
            pltpu.make_async_copy(w_in[c], w_land[c], w_recv.at[b, c]).start()

    for n in (1, 3, 2):
        loads[n].start()
    barrier = pltpu.get_barrier_semaphore()
    for k in range(1, npool):
        pl.semaphore_signal(barrier, inc=1, device_id={"pool": peer(k)}, device_id_type=MESH)
    for sx in range(2):
        for k in range(1, 4):
            pl.semaphore_signal(
                barrier, inc=1,
                device_id={"pool": (2 * a + y) * 2 + sx, "tp": lax.rem(t + k, 4)}, device_id_type=MESH,
            )
    for c in halves:
        own_h[c].wait()
    loads[4].wait()
    loads[0].wait()
    pl.semaphore_wait(barrier, npool - 1 + jnp.where(y == b, 4, 8))

    h_pair = [remote(h_part[c], hbuf.at[half_at(own_slot, c)], p_send.at[c], h_recv.at[own_slot, c], pair) for c in halves]
    h_other = [remote(h_part[c], hbuf.at[half_at(own_slot, c)], x_send.at[c], h_recv.at[own_slot, c], other) for c in halves]
    h_fwd = [
        remote(hbuf.at[half_at(pair_slot, c)], hbuf.at[half_at(pair_slot, c)], f_send.at[c], h_recv.at[pair_slot, c], other)
        for c in halves
    ]
    w_far = [remote(w_part[c], w_land[c], w_send.at[c], w_recv.at[b, c], far) for c in halves]
    w_near = [remote(w_part[c], w_land[c], v_send.at[c], w_recv.at[b, c], pair) for c in halves]

    for c in halves:
        h_pair[c].start()
    for c in halves:
        h_other[c].start()

    @pl.when(a != b)
    def _():
        for c in halves:
            w_far[c].start()

    wanted = [retr[0, f] for f in range(fetch)]
    owners = [lax.div(v, blocks_dev) for v in wanted]
    locals_ = [lax.rem(v, blocks_dev) for v in wanted]

    def slot_at(owner):
        total = jnp.int32(0)
        for f in range(fetch):
            total = total + jnp.where(owners[f] == owner, locals_[f], 0)
        return total

    ask, answers = [None], [None]
    for k in range(1, npool):
        msg_out[k] = jnp.full((8, 128), slot_at(peer(k)), jnp.int32)
        ask.append(remote(msg_out.at[k], msg_in.at[k], m_send.at[k], m_recv.at[k], peer(k)))
        ask[k].start()
    loads[1].wait()
    arrived[0] = cache[slot_at(me)]
    for k in range(1, npool):
        ask[k].wait_recv()
        reply[k] = cache[jnp.max(msg_in[k])]
        answers.append(remote(reply.at[k], arrived.at[k], a_send.at[k], a_recv.at[k], peer(k)))

    def h_wait(slot, c):
        pltpu.make_async_copy(h_in[c], hbuf.at[half_at(slot, c)], h_recv.at[slot, c]).wait()

    for c in halves:
        h_pair[c].wait_send()

        @pl.when(a == b)
        def _():
            w_far[c].start()

        @pl.when(a != b)
        def _():
            w_near[c].start()

        h_wait(pair_slot, c)
        h_fwd[c].start()
    for c in halves:
        w_far[c].wait_send()

        @pl.when(a != b)
        def _():
            w_near[c].wait_send()

        for k in ((6, 7), (2, 3, 1))[c]:
            answers[k].start()

    for c in halves:
        h_wait(b * 2 + 1 - x, c)
        for s in range(2):
            pltpu.make_async_copy(w_part[c], wbuf.at[pl.ds(c * half_depth, half_depth), pl.ds(s * HD, HD)], w_recv.at[s, c]).wait()

    def project(zl):
        block = jnp.dot(hbuf[rows_at(zl * 2, 2)], wbuf[...], preferred_element_type=jnp.float32)
        for sx in range(2):
            for i in range(2):
                j = zl * 2 + sx
                src = pbuf.at[j, i]
                src[...] = block[sx * rows:(sx + 1) * rows, i * HD:(i + 1) * HD].astype(jnp.bfloat16)
                mine = jnp.logical_and(4 * a + j == me, 2 * b + i == t)

                @pl.when(mine)
                def _():
                    pltpu.make_async_copy(src, part.at[x, t], s_recv.at[x, t]).start()

                @pl.when(jnp.logical_not(mine))
                def _():
                    remote(src, part.at[x, t], s_send.at[j, i], s_recv.at[x, t], 4 * a + j, 2 * b + i).start()

    project(b)
    for c in halves:
        h_wait((1 - b) * 2 + 1 - x, c)
    project(1 - b)

    for k, first in ((4, 6), (5, 7)):
        answers[first].wait_send()
        answers[k].start()

    for kind in range(2):
        total = jnp.zeros((rows, HD), jnp.float32)
        for n in range(4):
            pltpu.make_async_copy(pbuf.at[0, 0], part.at[kind, n], s_recv.at[kind, n]).wait()
            total = total + part[kind, n].astype(jnp.float32)
        fresh[:, kind * HD:(kind + 1) * HD] = total.astype(jnp.bfloat16)
    loads[2].wait()
    loads[3].wait()

    scale = float(HD) ** (-0.5)

    def allowed(k):
        owner = me if k == 0 else peer(k)
        token = lax.broadcasted_iota(jnp.int32, (rows, BLK), 0)
        mask = jnp.zeros((rows, BLK), jnp.int32)
        for r in range(pat.shape[1]):
            named = jnp.int32(0)
            for f in range(fetch):
                named = named + jnp.where(owners[f] == owner, pat[0, r, f], 0)
            mask = jnp.where(lax.div(token, RBLK) == r, named, mask)
        return mask != 0

    def stage(near, ks, last):
        @pl.loop(0, q_ref.shape[1] // HD, unroll=2)
        def _(head):
            at = pl.ds(pl.multiple_of(head * HD, HD), HD)
            masks = [allowed(k) for k in ks]
            keys = [arrived[k, :, 0:HD] for k in ks]
            vals = [arrived[k, :, HD:2 * HD] for k in ks]
            if near:
                token = lax.broadcasted_iota(jnp.int32, (rows, rows), 0)
                masks.append(token >= lax.broadcasted_iota(jnp.int32, (rows, rows), 1))
                keys.append(fresh[:, 0:HD])
                vals.append(fresh[:, HD:2 * HD])
            raw = rows_by_keys(q_ref[:, at], jnp.concatenate(keys, axis=0)) * scale
            scores = [jnp.where(m, raw[:, n * BLK:(n + 1) * BLK], -1e30) for n, m in enumerate(masks)]
            top = scores[0]
            for one in scores[1:]:
                top = jnp.maximum(top, one)
            top = jnp.max(top, axis=1, keepdims=True)
            if not near:
                before = top_ref[head]
                top = jnp.maximum(before, top)
                factor = jnp.exp(before - top)
            else:
                top = jnp.broadcast_to(top, (rows, HD))
            weights = [jnp.exp(one - top) for one in scores]
            denom = weights[0]
            for one in weights[1:]:
                denom = denom + one
            rounded = jnp.concatenate([w.astype(jnp.bfloat16) for w in weights], axis=1)
            numer = jnp.dot(rounded, jnp.concatenate(vals, axis=0), preferred_element_type=jnp.float32)
            if not near:
                denom = denom + factor * sum_ref[head]
                numer = numer + factor * acc_ref[head]
            if last:
                att[:, at] = (numer / jnp.sum(denom, axis=1, keepdims=True)).astype(jnp.bfloat16)
            else:
                top_ref[head] = top
                sum_ref[head] = denom
                acc_ref[head] = numer

    for near, ks, last in ((True, (0, 1, 2, 3), False), (False, (6, 7), False), (False, (4, 5), True)):
        for k in ks:
            if k:
                answers[k].wait_recv()
        stage(near, ks, last)

    for c in halves:
        h_other[c].wait_send()
        h_fwd[c].wait_send()
    for k in range(1, npool):
        ask[k].wait_send()
        if k not in (6, 7):
            answers[k].wait_send()
    for j in range(4):
        for i in range(2):
            mine = jnp.logical_and(4 * a + j == me, 2 * b + i == t)

            @pl.when(jnp.logical_not(mine))
            def _():
                remote(pbuf.at[j, i], part.at[x, t], s_send.at[j, i], s_recv.at[x, t], 4 * a + j, 2 * b + i).wait_send()


def fused(hidden_rows, kv_weight, queries, cache_table, retrieval, pattern):
    rows, depth = hidden_rows.shape
    cols = kv_weight.shape[1]
    blocks_dev, _, width = cache_table.shape
    dma = pltpu.SemaphoreType.DMA
    hbm = pl.BlockSpec(memory_space=pltpu.HBM)
    vmem = pl.BlockSpec(memory_space=pltpu.VMEM)
    bf = jnp.bfloat16
    return pl.pallas_call(
        kernel,
        out_shape=(
            pltpu.VMEM(queries.shape, bf),
            pltpu.VMEM((rows, width), bf),
        ),
        in_specs=[hbm] * 6,
        out_specs=(vmem, vmem),
        scratch_shapes=[
            pltpu.VMEM((4 * rows, depth), bf),
            pltpu.VMEM((depth, 2 * cols), bf),
            pltpu.VMEM((depth, cols), bf),
            pltpu.VMEM((4, 2, rows, HD), bf),
            pltpu.VMEM((2, 4, rows, HD), bf),
            pltpu.VMEM((8, 8, 128), jnp.int32),
            pltpu.VMEM((8, 8, 128), jnp.int32),
            pltpu.VMEM((8, BLK, width), bf),
            pltpu.VMEM((8, BLK, width), bf),
            pltpu.VMEM((queries.shape[1] // HD, rows, HD), jnp.float32),
            pltpu.VMEM((queries.shape[1] // HD, rows, HD), jnp.float32),
            pltpu.VMEM((queries.shape[1] // HD, rows, HD), jnp.float32),
            pltpu.VMEM(queries.shape, bf),
            pltpu.VMEM(cache_table.shape, bf),
            pltpu.SMEM(retrieval.shape, jnp.int32),
            pltpu.SMEM(pattern.shape, jnp.int32),
            dma((4, 2)), dma((2,)), dma((2,)), dma((2,)), dma((2, 2)), dma((2,)), dma((2,)),
            dma((8,)), dma((8,)), dma((8,)), dma((8,)), dma((2, 4)), dma((4, 2)), dma((5,)),
        ],
        compiler_params=pltpu.CompilerParams(
            collective_id=0, has_side_effects=True, vmem_limit_bytes=62 * 1024 * 1024
        ),
        name="blend",
    )(hidden_rows, kv_weight, queries, cache_table, retrieval, pattern)


def fits(mesh, hidden_rows, kv_weight, cache_table, retrieval):
    return (
        mesh.shape["pool"] == 8
        and mesh.shape["tp"] == 4
        and hidden_rows.shape[0] == 8 * BLK
        and kv_weight.shape[1] == 8 * HD
        and cache_table.shape[2] == 8 * HD
        and retrieval.shape[1] <= 8
    )


def solution(mesh):
    placed = (
        P("pool", "tp"),
        P("tp", "pool"),
        P("pool", "tp"),
        P("pool", None, "tp"),
        P("pool", None),
        P("pool", None, None),
    )

    def run(hidden_rows, kv_weight, queries, cache_table, retrieval, pattern):
        small = fits(mesh, hidden_rows, kv_weight, cache_table, retrieval)
        return jax.shard_map(
            fused if small else body,
            mesh=mesh,
            in_specs=placed,
            out_specs=(P("pool", "tp"), P("pool", "tp")),
            check_vma=False,
        )(hidden_rows, kv_weight, queries, cache_table, retrieval, pattern)

    return run
```

```python
import math

import jax
import jax.numpy as jnp
from jax import lax
from jax.experimental import pallas as pl
from jax.experimental.pallas import tpu as pltpu
from jax.sharding import PartitionSpec as P

HD = 128
QH = 32
KVH = 4
BLK = 128
RBLK = 64


def rows_by_keys(left, right):
    return lax.dot_general(
        left, right, (((1,), (1,)), ((), ())), preferred_element_type=jnp.float32
    )


def body(hidden_rows, kv_weight, queries, cache_table, retrieval, pattern):
    partial_kv = jnp.dot(
        hidden_rows,
        lax.all_gather(kv_weight, "pool", axis=1, tiled=True),
        preferred_element_type=jnp.float32,
    )
    fresh = lax.psum_scatter(partial_kv.astype(jnp.bfloat16), "tp", scatter_dimension=1, tiled=True)
    wanted = retrieval[0]
    blocks_dev = cache_table.shape[0]
    npool = lax.axis_size("pool")
    owners = wanted // blocks_dev
    local = wanted % blocks_dev
    hits = (owners[:, None] == jnp.arange(npool, dtype=jnp.int32)[None, :]).astype(jnp.int32)
    request = jnp.sum(hits * (local + 1)[:, None], axis=0)
    incoming = lax.all_to_all(
        request.reshape(npool, 1), "pool", split_axis=0, concat_axis=0, tiled=True
    ).reshape(npool)
    reply = jnp.zeros((npool,) + cache_table.shape[1:], jnp.bfloat16)
    for slot in range(blocks_dev):
        reply = jnp.where((incoming == slot + 1)[:, None, None], cache_table[slot][None], reply)
    arrived = lax.all_to_all(reply, "pool", split_axis=0, concat_axis=0, tiled=True)
    fetched = jnp.take(arrived, owners, axis=0)
    count = hidden_rows.shape[0]
    fetch_count = wanted.shape[0]
    group = QH // KVH
    scale = float(HD) ** (-0.5)
    local_heads = fresh.shape[1] // (2 * HD)
    width = fetched.shape[2]
    per_step = math.gcd(fetch_count, 8)
    steps_count = fetch_count // per_step
    grouped = fetched.reshape(steps_count, per_step * BLK, width)
    pat_steps = jnp.transpose(
        pattern[0].reshape(pattern.shape[1], steps_count, per_step), (1, 0, 2)
    )
    token_of_row = jnp.arange(count * group) // group
    block_of_row = token_of_row // RBLK
    row_blocks = block_of_row[:, None, None] == jnp.arange(pattern.shape[1])[None, :, None]
    near_mask = token_of_row[:, None] >= jnp.arange(count)[None, :]
    q_heads = queries.reshape(count, local_heads, group * HD)
    q_rows = q_heads[:, 0].reshape(count * group, HD)
    near_keys = fresh[:, 0:HD]
    near_vals = fresh[:, HD : 2 * HD]
    near_scores = rows_by_keys(q_rows, near_keys) * scale
    top = jnp.max(jnp.where(near_mask, near_scores, -1e30), axis=1)
    weights = jnp.where(near_mask, jnp.exp(near_scores - top[:, None]), 0.0)
    total = jnp.sum(weights, axis=1)
    numer = jnp.dot(weights.astype(jnp.bfloat16), near_vals, preferred_element_type=jnp.float32)

    def visit(carry, items):
        top_now, total_now, numer_now = carry
        block_rows, pat_now = items
        keys = block_rows[:, 0:HD]
        vals = block_rows[:, HD : 2 * HD]
        scores = rows_by_keys(q_rows, keys) * scale
        row_pat = jnp.any(row_blocks & (pat_now[None] != 0), axis=1)
        mask = jnp.repeat(row_pat, BLK, axis=1)
        top_new = jnp.maximum(top_now, jnp.max(jnp.where(mask, scores, -1e30), axis=1))
        weights_now = jnp.where(mask, jnp.exp(scores - top_new[:, None]), 0.0)
        factor = jnp.exp(top_now - top_new)
        total_new = total_now * factor + jnp.sum(weights_now, axis=1)
        numer_new = numer_now * factor[:, None] + jnp.dot(
            weights_now.astype(jnp.bfloat16), vals, preferred_element_type=jnp.float32
        )
        return ((top_new, total_new, numer_new), None)

    (top, total, numer), unused = lax.scan(visit, (top, total, numer), (grouped, pat_steps))
    results = (numer / total[:, None]).reshape(count, group * HD)
    attended = results.astype(jnp.bfloat16)
    return (attended, fresh)


MESH = pl.DeviceIdType.MESH


def kernel(hid, wgt, q_hbm, cache_hbm, retr_hbm, pat_hbm, att, fresh, hbuf, wbuf, wsrc, pbuf, part,
           msg_out, msg_in, reply, arrived, top_ref, acc_ref, near_bias, q_ref, cache, retr, pat,
           h_recv, p_send, x_send, f_send, w_recv, w_send, v_send, m_recv, m_send, a_recv, a_send,
           s_recv, s_send, load_sem):
    npool = 8
    blocks_dev = cache.shape[0]
    fetch = retr.shape[1]
    rows, depth = hid.shape
    half_rows, half_depth = rows // 2, depth // 2
    loads = [
        pltpu.make_async_copy(src, dst, load_sem.at[n])
        for n, (src, dst) in enumerate(((retr_hbm, retr), (cache_hbm, cache), (q_hbm, q_ref), (pat_hbm, pat), (wgt, wsrc)))
    ]
    loads[0].start()
    loads[4].start()
    me = lax.axis_index("pool")
    t = lax.axis_index("tp")
    z, x = lax.div(me, 2), lax.rem(me, 2)
    a, b = lax.div(z, 2), lax.rem(z, 2)
    y = lax.div(t, 2)
    pair = (2 * a + 1 - b) * 2 + x
    other = z * 2 + 1 - x
    far = (2 - a) * 2 + x

    def peer(k):
        pa = 1 - a if k & 4 else a
        pb = 1 - b if k & 2 else b
        return (2 * pa + pb) * 2 + (1 - x if k & 1 else x)

    def remote(src, dst, ssem, rsem, pool, tp=None):
        where = {"pool": pool} if tp is None else {"pool": pool, "tp": tp}
        return pltpu.make_async_remote_copy(
            src_ref=src, dst_ref=dst, send_sem=ssem, recv_sem=rsem, device_id=where, device_id_type=MESH
        )

    def rows_at(slot, count=1):
        return pl.ds(pl.multiple_of(slot * rows, rows), count * rows)

    def half_at(slot, c):
        return pl.ds(pl.multiple_of(slot * rows + c * half_rows, half_rows), half_rows)

    def cols_at(slot):
        return pl.ds(pl.multiple_of(slot * HD, HD), HD)

    own_slot = b * 2 + x
    pair_slot = (1 - b) * 2 + x
    halves = (0, 1)
    h_in = [hid.at[pl.ds(c * half_rows, half_rows)] for c in halves]
    w_in = [wgt.at[pl.ds(c * half_depth, half_depth)] for c in halves]
    h_part = [hbuf.at[half_at(own_slot, c)] for c in halves]
    w_part = [wsrc.at[pl.ds(c * half_depth, half_depth)] for c in halves]
    w_land = [wbuf.at[pl.ds(c * half_depth, half_depth), cols_at(b)] for c in halves]

    own_h = [pltpu.make_async_copy(h_in[c], hbuf.at[half_at(own_slot, c)], h_recv.at[own_slot, c]) for c in halves]
    for c in halves:
        own_h[c].start()

    @pl.when(a == b)
    def _():
        for c in halves:
            pltpu.make_async_copy(w_in[c], w_land[c], w_recv.at[b, c]).start()

    for n in (1, 3, 2):
        loads[n].start()
    barrier = pltpu.get_barrier_semaphore()
    for k in range(1, npool):
        pl.semaphore_signal(barrier, inc=1, device_id={"pool": peer(k)}, device_id_type=MESH)
    for sx in range(2):
        for k in range(1, 4):
            pl.semaphore_signal(
                barrier, inc=1,
                device_id={"pool": (2 * a + y) * 2 + sx, "tp": lax.rem(t + k, 4)}, device_id_type=MESH,
            )
    for c in halves:
        own_h[c].wait()
    loads[4].wait()
    loads[0].wait()
    pl.semaphore_wait(barrier, npool - 1 + jnp.where(y == b, 4, 8))

    h_pair = [remote(h_part[c], hbuf.at[half_at(own_slot, c)], p_send.at[c], h_recv.at[own_slot, c], pair) for c in halves]
    h_other = [remote(h_part[c], hbuf.at[half_at(own_slot, c)], x_send.at[c], h_recv.at[own_slot, c], other) for c in halves]
    h_fwd = [
        remote(hbuf.at[half_at(pair_slot, c)], hbuf.at[half_at(pair_slot, c)], f_send.at[c], h_recv.at[pair_slot, c], other)
        for c in halves
    ]
    w_far = [remote(w_part[c], w_land[c], w_send.at[c], w_recv.at[b, c], far) for c in halves]
    w_near = [remote(w_part[c], w_land[c], v_send.at[c], w_recv.at[b, c], pair) for c in halves]

    for c in halves:
        h_pair[c].start()
    for c in halves:
        h_other[c].start()

    @pl.when(a != b)
    def _():
        for c in halves:
            w_far[c].start()

    wanted = [retr[0, f] for f in range(fetch)]
    owners = [lax.div(v, blocks_dev) for v in wanted]
    locals_ = [lax.rem(v, blocks_dev) for v in wanted]

    def slot_at(owner):
        total = jnp.int32(0)
        for f in range(fetch):
            total = total + jnp.where(owners[f] == owner, locals_[f], 0)
        return total

    ask, answers = [None], [None]
    for k in range(1, npool):
        msg_out[k] = jnp.full((8, 128), slot_at(peer(k)), jnp.int32)
        ask.append(remote(msg_out.at[k], msg_in.at[k], m_send.at[k], m_recv.at[k], peer(k)))
        ask[k].start()
    loads[1].wait()
    arrived[0] = cache[slot_at(me)]
    for k in range(1, npool):
        ask[k].wait_recv()
        reply[k] = cache[jnp.max(msg_in[k])]
        answers.append(remote(reply.at[k], arrived.at[k], a_send.at[k], a_recv.at[k], peer(k)))

    def h_wait(slot, c):
        pltpu.make_async_copy(h_in[c], hbuf.at[half_at(slot, c)], h_recv.at[slot, c]).wait()

    for c in halves:
        h_pair[c].wait_send()

        @pl.when(a == b)
        def _():
            w_far[c].start()

        @pl.when(a != b)
        def _():
            w_near[c].start()

        h_wait(pair_slot, c)
        h_fwd[c].start()
    for c in halves:
        w_far[c].wait_send()

        @pl.when(a != b)
        def _():
            w_near[c].wait_send()

        for k in ((6, 7), (2, 3, 1, 4, 5))[c]:
            answers[k].start()

    for c in halves:
        h_wait(b * 2 + 1 - x, c)
        for s in range(2):
            pltpu.make_async_copy(w_part[c], wbuf.at[pl.ds(c * half_depth, half_depth), pl.ds(s * HD, HD)], w_recv.at[s, c]).wait()

    def project(zl):
        block = jnp.dot(hbuf[rows_at(zl * 2, 2)], wbuf[...], preferred_element_type=jnp.float32)
        for sx in range(2):
            for i in range(2):
                j = zl * 2 + sx
                src = pbuf.at[j, i]
                src[...] = block[sx * rows:(sx + 1) * rows, i * HD:(i + 1) * HD].astype(jnp.bfloat16)
                mine = jnp.logical_and(4 * a + j == me, 2 * b + i == t)

                @pl.when(mine)
                def _():
                    pltpu.make_async_copy(src, part.at[x, t], s_recv.at[x, t]).start()

                @pl.when(jnp.logical_not(mine))
                def _():
                    remote(src, part.at[x, t], s_send.at[j, i], s_recv.at[x, t], 4 * a + j, 2 * b + i).start()

    project(b)
    for c in halves:
        h_wait((1 - b) * 2 + 1 - x, c)
    project(1 - b)

    token = lax.broadcasted_iota(jnp.int32, (rows, rows), 0)
    near_bias[...] = jnp.where(token >= lax.broadcasted_iota(jnp.int32, (rows, rows), 1), 0.0, -1e30)
    for kind in range(2):
        total = jnp.zeros((rows, HD), jnp.float32)
        for n in range(4):
            pltpu.make_async_copy(pbuf.at[0, 0], part.at[kind, n], s_recv.at[kind, n]).wait()
            total = total + part[kind, n].astype(jnp.float32)
        fresh[:, kind * HD:(kind + 1) * HD] = total.astype(jnp.bfloat16)
    loads[2].wait()
    loads[3].wait()

    rate = float(HD) ** (-0.5) * math.log2(math.e)
    r_blocks = pat.shape[1]

    def bias_of(k, r):
        owner = me if k == 0 else peer(k)
        named = jnp.int32(0)
        for f in range(fetch):
            named = named + jnp.where(owners[f] == owner, pat[0, r, f], 0)
        return jnp.where(named != 0, jnp.float32(0.0), jnp.float32(-1e30))

    def stage(near, ks, last):
        biases = [[bias_of(k, r) for r in range(r_blocks)] for k in ks]

        @pl.loop(0, q_ref.shape[1] // (2 * HD), unroll=2)
        def _(step):
            ats = [pl.ds(pl.multiple_of(step * 2 * HD + h * HD, HD), HD) for h in range(2)]
            keys = [arrived[k, :, 0:HD] for k in ks]
            vals = [arrived[k, :, HD:2 * HD] for k in ks]
            if near:
                keys.append(fresh[:, 0:HD])
                vals.append(fresh[:, HD:2 * HD])
            keys = jnp.concatenate(keys, axis=0)
            vals = jnp.concatenate(vals, axis=0)
            vals = jnp.concatenate([vals, jnp.ones_like(vals)], axis=1)
            raw = rows_by_keys(jnp.concatenate([q_ref[:, at] for at in ats], axis=0), keys)
            rounded, factors = [], []
            for h in range(2):
                scores = []
                for n in range(len(ks)):
                    scores.append(jnp.concatenate([
                        raw[h * rows + r * RBLK:h * rows + (r + 1) * RBLK, n * BLK:(n + 1) * BLK] + biases[n][r]
                        for r in range(r_blocks)
                    ], axis=0))
                if near:
                    scores.append(raw[h * rows:(h + 1) * rows, len(ks) * BLK:] + near_bias[...])
                top = scores[0]
                for one in scores[1:]:
                    top = jnp.maximum(top, one)
                top = jnp.broadcast_to(jnp.max(top, axis=1, keepdims=True), (rows, HD))
                if not near:
                    before = top_ref[2 * step + h]
                    top = jnp.maximum(before, top)
                    factors.append(jnp.exp2((before - top) * rate))
                if not last:
                    top_ref[2 * step + h] = top
                rounded.append(jnp.concatenate(
                    [jnp.exp2((one - top) * rate).astype(jnp.bfloat16) for one in scores], axis=1
                ))
            both = jnp.dot(jnp.concatenate(rounded, axis=0), vals, preferred_element_type=jnp.float32)
            for h in range(2):
                numer = both[h * rows:(h + 1) * rows, 0:HD]
                denom = both[h * rows:(h + 1) * rows, HD:2 * HD]
                if not near:
                    numer = numer + factors[h] * acc_ref[2 * step + h, :, 0:HD]
                    denom = denom + factors[h] * acc_ref[2 * step + h, :, HD:2 * HD]
                if last:
                    att[:, ats[h]] = (numer / denom).astype(jnp.bfloat16)
                else:
                    acc_ref[2 * step + h, :, 0:HD] = numer
                    acc_ref[2 * step + h, :, HD:2 * HD] = denom

    for near, ks, last in ((True, (0, 1, 2, 3), False), (False, (6, 7), False), (False, (4, 5), True)):
        for k in ks:
            if k:
                answers[k].wait_recv()
        stage(near, ks, last)

    for c in halves:
        h_other[c].wait_send()
        h_fwd[c].wait_send()
    for k in range(1, npool):
        ask[k].wait_send()
        answers[k].wait_send()
    for j in range(4):
        for i in range(2):
            mine = jnp.logical_and(4 * a + j == me, 2 * b + i == t)

            @pl.when(jnp.logical_not(mine))
            def _():
                remote(pbuf.at[j, i], part.at[x, t], s_send.at[j, i], s_recv.at[x, t], 4 * a + j, 2 * b + i).wait_send()


def fused(hidden_rows, kv_weight, queries, cache_table, retrieval, pattern):
    rows, depth = hidden_rows.shape
    cols = kv_weight.shape[1]
    blocks_dev, _, width = cache_table.shape
    dma = pltpu.SemaphoreType.DMA
    hbm = pl.BlockSpec(memory_space=pltpu.HBM)
    vmem = pl.BlockSpec(memory_space=pltpu.VMEM)
    bf = jnp.bfloat16
    return pl.pallas_call(
        kernel,
        out_shape=(
            pltpu.VMEM(queries.shape, bf),
            pltpu.VMEM((rows, width), bf),
        ),
        in_specs=[hbm] * 6,
        out_specs=(vmem, vmem),
        scratch_shapes=[
            pltpu.VMEM((4 * rows, depth), bf),
            pltpu.VMEM((depth, 2 * cols), bf),
            pltpu.VMEM((depth, cols), bf),
            pltpu.VMEM((4, 2, rows, HD), bf),
            pltpu.VMEM((2, 4, rows, HD), bf),
            pltpu.VMEM((8, 8, 128), jnp.int32),
            pltpu.VMEM((8, 8, 128), jnp.int32),
            pltpu.VMEM((8, BLK, width), bf),
            pltpu.VMEM((8, BLK, width), bf),
            pltpu.VMEM((queries.shape[1] // HD, rows, HD), jnp.float32),
            pltpu.VMEM((queries.shape[1] // HD, rows, 2 * HD), jnp.float32),
            pltpu.VMEM((rows, rows), jnp.float32),
            pltpu.VMEM(queries.shape, bf),
            pltpu.VMEM(cache_table.shape, bf),
            pltpu.SMEM(retrieval.shape, jnp.int32),
            pltpu.SMEM(pattern.shape, jnp.int32),
            dma((4, 2)), dma((2,)), dma((2,)), dma((2,)), dma((2, 2)), dma((2,)), dma((2,)),
            dma((8,)), dma((8,)), dma((8,)), dma((8,)), dma((2, 4)), dma((4, 2)), dma((5,)),
        ],
        compiler_params=pltpu.CompilerParams(
            collective_id=0, has_side_effects=True, vmem_limit_bytes=62 * 1024 * 1024
        ),
        name="blend",
    )(hidden_rows, kv_weight, queries, cache_table, retrieval, pattern)


def fits(mesh, hidden_rows, kv_weight, cache_table, retrieval):
    return (
        mesh.shape["pool"] == 8
        and mesh.shape["tp"] == 4
        and hidden_rows.shape[0] == 8 * BLK
        and kv_weight.shape[1] == 8 * HD
        and cache_table.shape[2] == 8 * HD
        and retrieval.shape[1] <= 8
    )


def solution(mesh):
    placed = (
        P("pool", "tp"),
        P("tp", "pool"),
        P("pool", "tp"),
        P("pool", None, "tp"),
        P("pool", None),
        P("pool", None, None),
    )

    def run(hidden_rows, kv_weight, queries, cache_table, retrieval, pattern):
        small = fits(mesh, hidden_rows, kv_weight, cache_table, retrieval)
        return jax.shard_map(
            fused if small else body,
            mesh=mesh,
            in_specs=placed,
            out_specs=(P("pool", "tp"), P("pool", "tp")),
            check_vma=False,
        )(hidden_rows, kv_weight, queries, cache_table, retrieval, pattern)

    return run
```

```python
import math

import jax
import jax.numpy as jnp
from jax import lax
from jax.experimental import pallas as pl
from jax.experimental.pallas import tpu as pltpu
from jax.sharding import PartitionSpec as P

HD = 128
QH = 32
KVH = 4
BLK = 128
RBLK = 64


def rows_by_keys(left, right):
    return lax.dot_general(
        left, right, (((1,), (1,)), ((), ())), preferred_element_type=jnp.float32
    )


def body(hidden_rows, kv_weight, queries, cache_table, retrieval, pattern):
    partial_kv = jnp.dot(
        hidden_rows,
        lax.all_gather(kv_weight, "pool", axis=1, tiled=True),
        preferred_element_type=jnp.float32,
    )
    fresh = lax.psum_scatter(partial_kv.astype(jnp.bfloat16), "tp", scatter_dimension=1, tiled=True)
    wanted = retrieval[0]
    blocks_dev = cache_table.shape[0]
    npool = lax.axis_size("pool")
    owners = wanted // blocks_dev
    local = wanted % blocks_dev
    hits = (owners[:, None] == jnp.arange(npool, dtype=jnp.int32)[None, :]).astype(jnp.int32)
    request = jnp.sum(hits * (local + 1)[:, None], axis=0)
    incoming = lax.all_to_all(
        request.reshape(npool, 1), "pool", split_axis=0, concat_axis=0, tiled=True
    ).reshape(npool)
    reply = jnp.zeros((npool,) + cache_table.shape[1:], jnp.bfloat16)
    for slot in range(blocks_dev):
        reply = jnp.where((incoming == slot + 1)[:, None, None], cache_table[slot][None], reply)
    arrived = lax.all_to_all(reply, "pool", split_axis=0, concat_axis=0, tiled=True)
    fetched = jnp.take(arrived, owners, axis=0)
    count = hidden_rows.shape[0]
    fetch_count = wanted.shape[0]
    group = QH // KVH
    scale = float(HD) ** (-0.5)
    local_heads = fresh.shape[1] // (2 * HD)
    width = fetched.shape[2]
    per_step = math.gcd(fetch_count, 8)
    steps_count = fetch_count // per_step
    grouped = fetched.reshape(steps_count, per_step * BLK, width)
    pat_steps = jnp.transpose(
        pattern[0].reshape(pattern.shape[1], steps_count, per_step), (1, 0, 2)
    )
    token_of_row = jnp.arange(count * group) // group
    block_of_row = token_of_row // RBLK
    row_blocks = block_of_row[:, None, None] == jnp.arange(pattern.shape[1])[None, :, None]
    near_mask = token_of_row[:, None] >= jnp.arange(count)[None, :]
    q_heads = queries.reshape(count, local_heads, group * HD)
    q_rows = q_heads[:, 0].reshape(count * group, HD)
    near_keys = fresh[:, 0:HD]
    near_vals = fresh[:, HD : 2 * HD]
    near_scores = rows_by_keys(q_rows, near_keys) * scale
    top = jnp.max(jnp.where(near_mask, near_scores, -1e30), axis=1)
    weights = jnp.where(near_mask, jnp.exp(near_scores - top[:, None]), 0.0)
    total = jnp.sum(weights, axis=1)
    numer = jnp.dot(weights.astype(jnp.bfloat16), near_vals, preferred_element_type=jnp.float32)

    def visit(carry, items):
        top_now, total_now, numer_now = carry
        block_rows, pat_now = items
        keys = block_rows[:, 0:HD]
        vals = block_rows[:, HD : 2 * HD]
        scores = rows_by_keys(q_rows, keys) * scale
        row_pat = jnp.any(row_blocks & (pat_now[None] != 0), axis=1)
        mask = jnp.repeat(row_pat, BLK, axis=1)
        top_new = jnp.maximum(top_now, jnp.max(jnp.where(mask, scores, -1e30), axis=1))
        weights_now = jnp.where(mask, jnp.exp(scores - top_new[:, None]), 0.0)
        factor = jnp.exp(top_now - top_new)
        total_new = total_now * factor + jnp.sum(weights_now, axis=1)
        numer_new = numer_now * factor[:, None] + jnp.dot(
            weights_now.astype(jnp.bfloat16), vals, preferred_element_type=jnp.float32
        )
        return ((top_new, total_new, numer_new), None)

    (top, total, numer), unused = lax.scan(visit, (top, total, numer), (grouped, pat_steps))
    results = (numer / total[:, None]).reshape(count, group * HD)
    attended = results.astype(jnp.bfloat16)
    return (attended, fresh)


MESH = pl.DeviceIdType.MESH


def kernel(hid, wgt, q_hbm, cache_hbm, retr_hbm, pat_hbm, att, fresh, hbuf, wbuf, wsrc, pbuf, part,
           msg_out, msg_in, reply, arrived, top_ref, acc_ref, near_bias, q_ref, cache, retr, pat,
           h_recv, p_send, x_send, f_send, w_recv, w_send, v_send, m_recv, m_send, a_recv, a_send,
           s_recv, s_send, load_sem):
    npool = 8
    blocks_dev = cache.shape[0]
    fetch = retr.shape[1]
    rows, depth = hid.shape
    half_rows, half_depth = rows // 2, depth // 2
    loads = [
        pltpu.make_async_copy(src, dst, load_sem.at[n])
        for n, (src, dst) in enumerate(((retr_hbm, retr), (cache_hbm, cache), (q_hbm, q_ref), (pat_hbm, pat), (wgt, wsrc)))
    ]
    loads[0].start()
    loads[4].start()
    me = lax.axis_index("pool")
    t = lax.axis_index("tp")
    z, x = lax.div(me, 2), lax.rem(me, 2)
    a, b = lax.div(z, 2), lax.rem(z, 2)
    y = lax.div(t, 2)
    pair = (2 * a + 1 - b) * 2 + x
    other = z * 2 + 1 - x
    far = (2 - a) * 2 + x

    def peer(k):
        pa = 1 - a if k & 4 else a
        pb = 1 - b if k & 2 else b
        return (2 * pa + pb) * 2 + (1 - x if k & 1 else x)

    def remote(src, dst, ssem, rsem, pool, tp=None):
        where = {"pool": pool} if tp is None else {"pool": pool, "tp": tp}
        return pltpu.make_async_remote_copy(
            src_ref=src, dst_ref=dst, send_sem=ssem, recv_sem=rsem, device_id=where, device_id_type=MESH
        )

    def rows_at(slot, count=1):
        return pl.ds(pl.multiple_of(slot * rows, rows), count * rows)

    def half_at(slot, c):
        return pl.ds(pl.multiple_of(slot * rows + c * half_rows, half_rows), half_rows)

    def cols_at(slot):
        return pl.ds(pl.multiple_of(slot * HD, HD), HD)

    own_slot = b * 2 + x
    pair_slot = (1 - b) * 2 + x
    halves = (0, 1)
    h_in = [hid.at[pl.ds(c * half_rows, half_rows)] for c in halves]
    w_in = [wgt.at[pl.ds(c * half_depth, half_depth)] for c in halves]
    h_part = [hbuf.at[half_at(own_slot, c)] for c in halves]
    w_part = [wsrc.at[pl.ds(c * half_depth, half_depth)] for c in halves]
    w_land = [wbuf.at[pl.ds(c * half_depth, half_depth), cols_at(b)] for c in halves]

    own_h = [pltpu.make_async_copy(h_in[c], hbuf.at[half_at(own_slot, c)], h_recv.at[own_slot, c]) for c in halves]
    for c in halves:
        own_h[c].start()

    @pl.when(a == b)
    def _():
        for c in halves:
            pltpu.make_async_copy(w_in[c], w_land[c], w_recv.at[b, c]).start()

    for n in (1, 3, 2):
        loads[n].start()
    barrier = pltpu.get_barrier_semaphore()
    for k in range(1, npool):
        pl.semaphore_signal(barrier, inc=1, device_id={"pool": peer(k)}, device_id_type=MESH)
    for sx in range(2):
        for k in range(1, 4):
            pl.semaphore_signal(
                barrier, inc=1,
                device_id={"pool": (2 * a + y) * 2 + sx, "tp": lax.rem(t + k, 4)}, device_id_type=MESH,
            )
    loads[0].wait()

    wanted = [retr[0, f] for f in range(fetch)]
    owners = [lax.div(v, blocks_dev) for v in wanted]
    locals_ = [lax.rem(v, blocks_dev) for v in wanted]

    def slot_at(owner):
        total = jnp.int32(0)
        for f in range(fetch):
            total = total + jnp.where(owners[f] == owner, locals_[f], 0)
        return total

    ask, answers = [None], [None]
    for k in range(1, npool):
        msg_out[k] = jnp.full((8, 128), slot_at(peer(k)), jnp.int32)
        ask.append(remote(msg_out.at[k], msg_in.at[k], m_send.at[k], m_recv.at[k], peer(k)))
    for c in halves:
        own_h[c].wait()
    loads[4].wait()
    pl.semaphore_wait(barrier, npool - 1 + jnp.where(y == b, 4, 8))

    h_pair = [remote(h_part[c], hbuf.at[half_at(own_slot, c)], p_send.at[c], h_recv.at[own_slot, c], pair) for c in halves]
    h_other = [remote(h_part[c], hbuf.at[half_at(own_slot, c)], x_send.at[c], h_recv.at[own_slot, c], other) for c in halves]
    h_fwd = [
        remote(hbuf.at[half_at(pair_slot, c)], hbuf.at[half_at(pair_slot, c)], f_send.at[c], h_recv.at[pair_slot, c], other)
        for c in halves
    ]
    w_far = [remote(w_part[c], w_land[c], w_send.at[c], w_recv.at[b, c], far) for c in halves]
    w_near = [remote(w_part[c], w_land[c], v_send.at[c], w_recv.at[b, c], pair) for c in halves]

    for k in range(1, npool):
        ask[k].start()
    for c in halves:
        h_pair[c].start()
    for c in halves:
        h_other[c].start()

    @pl.when(a != b)
    def _():
        for c in halves:
            w_far[c].start()

    def h_wait(slot, c):
        pltpu.make_async_copy(h_in[c], hbuf.at[half_at(slot, c)], h_recv.at[slot, c]).wait()

    for c in halves:
        h_pair[c].wait_send()

        @pl.when(a == b)
        def _():
            w_far[c].start()

        @pl.when(a != b)
        def _():
            w_near[c].start()

        h_wait(pair_slot, c)
        h_fwd[c].start()
        if c == 0:
            loads[1].wait()
            arrived[0] = cache[slot_at(me)]
            for k in range(1, npool):
                ask[k].wait_recv()
                reply[k] = cache[jnp.max(msg_in[k])]
                answers.append(remote(reply.at[k], arrived.at[k], a_send.at[k], a_recv.at[k], peer(k)))
    for c in halves:
        w_far[c].wait_send()

        @pl.when(a != b)
        def _():
            w_near[c].wait_send()

        for k in ((6, 7), (2, 3, 1))[c]:
            answers[k].start()

    def w_wait(c):
        for n in range(2):
            pltpu.make_async_copy(
                w_in[c], wbuf.at[pl.ds(c * half_depth, half_depth), pl.ds(n * HD, HD)], w_recv.at[n, c]
            ).wait()

    def product(zl, c):
        at = pl.ds(c * half_depth, half_depth)
        return jnp.dot(hbuf[rows_at(zl * 2, 2), at], wbuf[at, :], preferred_element_type=jnp.float32)

    def hand_out(zl, block):
        for sx in range(2):
            for i in range(2):
                j = zl * 2 + sx
                src = pbuf.at[j, i]
                src[...] = block[sx * rows:(sx + 1) * rows, i * HD:(i + 1) * HD].astype(jnp.bfloat16)
                mine = jnp.logical_and(4 * a + j == me, 2 * b + i == t)

                @pl.when(mine)
                def _():
                    pltpu.make_async_copy(src, part.at[x, t], s_recv.at[x, t]).start()

                @pl.when(jnp.logical_not(mine))
                def _():
                    remote(src, part.at[x, t], s_send.at[j, i], s_recv.at[x, t], 4 * a + j, 2 * b + i).start()

    for c in halves:
        h_wait(b * 2 + 1 - x, c)
    w_wait(0)
    first = product(b, 0)
    w_wait(1)
    hand_out(b, first + product(b, 1))
    for c in halves:
        h_wait((1 - b) * 2 + 1 - x, c)
    hand_out(1 - b, product(1 - b, 0) + product(1 - b, 1))
    for k in (4, 5):
        answers[k].start()

    token = lax.broadcasted_iota(jnp.int32, (rows, rows), 0)
    near_bias[...] = jnp.where(token >= lax.broadcasted_iota(jnp.int32, (rows, rows), 1), 0.0, -1e30)
    loads[2].wait()
    loads[3].wait()

    rate = float(HD) ** (-0.5) * math.log2(math.e)
    r_blocks = pat.shape[1]

    def bias_of(k, r):
        owner = me if k == 0 else peer(k)
        named = jnp.int32(0)
        for f in range(fetch):
            named = named + jnp.where(owners[f] == owner, pat[0, r, f], 0)
        return jnp.where(named != 0, jnp.float32(0.0), jnp.float32(-1e30))

    def stage(first, near, ks, last):
        biases = [[bias_of(k, r) for r in range(r_blocks)] for k in ks]

        @pl.loop(0, q_ref.shape[1] // (2 * HD), unroll=2)
        def _(step):
            ats = [pl.ds(pl.multiple_of(step * 2 * HD + h * HD, HD), HD) for h in range(2)]
            keys = [arrived[k, :, 0:HD] for k in ks]
            vals = [arrived[k, :, HD:2 * HD] for k in ks]
            if near:
                keys.append(fresh[:, 0:HD])
                vals.append(fresh[:, HD:2 * HD])
            keys = jnp.concatenate(keys, axis=0)
            vals = jnp.concatenate(vals, axis=0)
            vals = jnp.concatenate([vals, jnp.ones_like(vals)], axis=1)
            raw = rows_by_keys(jnp.concatenate([q_ref[:, at] for at in ats], axis=0), keys)
            rounded, factors = [], []
            for h in range(2):
                scores = []
                for n in range(len(ks)):
                    scores.append(jnp.concatenate([
                        raw[h * rows + r * RBLK:h * rows + (r + 1) * RBLK, n * BLK:(n + 1) * BLK] + biases[n][r]
                        for r in range(r_blocks)
                    ], axis=0))
                if near:
                    scores.append(raw[h * rows:(h + 1) * rows, len(ks) * BLK:] + near_bias[...])
                top = scores[0]
                for one in scores[1:]:
                    top = jnp.maximum(top, one)
                top = jnp.broadcast_to(jnp.max(top, axis=1, keepdims=True), (rows, HD))
                if not first:
                    before = top_ref[2 * step + h]
                    top = jnp.maximum(before, top)
                    factors.append(jnp.exp2((before - top) * rate))
                if not last:
                    top_ref[2 * step + h] = top
                rounded.append(jnp.concatenate(
                    [jnp.exp2((one - top) * rate).astype(jnp.bfloat16) for one in scores], axis=1
                ))
            both = jnp.dot(jnp.concatenate(rounded, axis=0), vals, preferred_element_type=jnp.float32)
            for h in range(2):
                numer = both[h * rows:(h + 1) * rows, 0:HD]
                denom = both[h * rows:(h + 1) * rows, HD:2 * HD]
                if not first:
                    numer = numer + factors[h] * acc_ref[2 * step + h, :, 0:HD]
                    denom = denom + factors[h] * acc_ref[2 * step + h, :, HD:2 * HD]
                if last:
                    att[:, ats[h]] = (numer / denom).astype(jnp.bfloat16)
                else:
                    acc_ref[2 * step + h, :, 0:HD] = numer
                    acc_ref[2 * step + h, :, HD:2 * HD] = denom

    for k in (1, 2, 3):
        answers[k].wait_recv()
    stage(True, False, (0, 1, 2, 3), False)
    for kind in range(2):
        total = jnp.zeros((rows, HD), jnp.float32)
        for n in range(4):
            pltpu.make_async_copy(pbuf.at[0, 0], part.at[kind, n], s_recv.at[kind, n]).wait()
            total = total + part[kind, n].astype(jnp.float32)
        fresh[:, kind * HD:(kind + 1) * HD] = total.astype(jnp.bfloat16)
    for k in (6, 7):
        answers[k].wait_recv()
    stage(False, True, (6, 7), False)
    for k in (4, 5):
        answers[k].wait_recv()
    stage(False, False, (4, 5), True)

    for c in halves:
        h_other[c].wait_send()
        h_fwd[c].wait_send()
    for k in range(1, npool):
        ask[k].wait_send()
        answers[k].wait_send()
    for j in range(4):
        for i in range(2):
            mine = jnp.logical_and(4 * a + j == me, 2 * b + i == t)

            @pl.when(jnp.logical_not(mine))
            def _():
                remote(pbuf.at[j, i], part.at[x, t], s_send.at[j, i], s_recv.at[x, t], 4 * a + j, 2 * b + i).wait_send()


def fused(hidden_rows, kv_weight, queries, cache_table, retrieval, pattern):
    rows, depth = hidden_rows.shape
    cols = kv_weight.shape[1]
    blocks_dev, _, width = cache_table.shape
    dma = pltpu.SemaphoreType.DMA
    hbm = pl.BlockSpec(memory_space=pltpu.HBM)
    vmem = pl.BlockSpec(memory_space=pltpu.VMEM)
    bf = jnp.bfloat16
    return pl.pallas_call(
        kernel,
        out_shape=(
            pltpu.VMEM(queries.shape, bf),
            pltpu.VMEM((rows, width), bf),
        ),
        in_specs=[hbm] * 6,
        out_specs=(vmem, vmem),
        scratch_shapes=[
            pltpu.VMEM((4 * rows, depth), bf),
            pltpu.VMEM((depth, 2 * cols), bf),
            pltpu.VMEM((depth, cols), bf),
            pltpu.VMEM((4, 2, rows, HD), bf),
            pltpu.VMEM((2, 4, rows, HD), bf),
            pltpu.VMEM((8, 8, 128), jnp.int32),
            pltpu.VMEM((8, 8, 128), jnp.int32),
            pltpu.VMEM((8, BLK, width), bf),
            pltpu.VMEM((8, BLK, width), bf),
            pltpu.VMEM((queries.shape[1] // HD, rows, HD), jnp.float32),
            pltpu.VMEM((queries.shape[1] // HD, rows, 2 * HD), jnp.float32),
            pltpu.VMEM((rows, rows), jnp.float32),
            pltpu.VMEM(queries.shape, bf),
            pltpu.VMEM(cache_table.shape, bf),
            pltpu.SMEM(retrieval.shape, jnp.int32),
            pltpu.SMEM(pattern.shape, jnp.int32),
            dma((4, 2)), dma((2,)), dma((2,)), dma((2,)), dma((2, 2)), dma((2,)), dma((2,)),
            dma((8,)), dma((8,)), dma((8,)), dma((8,)), dma((2, 4)), dma((4, 2)), dma((5,)),
        ],
        compiler_params=pltpu.CompilerParams(
            collective_id=0, has_side_effects=True, vmem_limit_bytes=62 * 1024 * 1024
        ),
        name="blend",
    )(hidden_rows, kv_weight, queries, cache_table, retrieval, pattern)


def fits(mesh, hidden_rows, kv_weight, cache_table, retrieval):
    return (
        mesh.shape["pool"] == 8
        and mesh.shape["tp"] == 4
        and hidden_rows.shape[0] == 8 * BLK
        and kv_weight.shape[1] == 8 * HD
        and cache_table.shape[2] == 8 * HD
        and retrieval.shape[1] <= 8
    )


def solution(mesh):
    placed = (
        P("pool", "tp"),
        P("tp", "pool"),
        P("pool", "tp"),
        P("pool", None, "tp"),
        P("pool", None),
        P("pool", None, None),
    )

    def run(hidden_rows, kv_weight, queries, cache_table, retrieval, pattern):
        small = fits(mesh, hidden_rows, kv_weight, cache_table, retrieval)
        return jax.shard_map(
            fused if small else body,
            mesh=mesh,
            in_specs=placed,
            out_specs=(P("pool", "tp"), P("pool", "tp")),
            check_vma=False,
        )(hidden_rows, kv_weight, queries, cache_table, retrieval, pattern)

    return run
```

```python
import math

import jax
import jax.numpy as jnp
from jax import lax
from jax.experimental import pallas as pl
from jax.experimental.pallas import tpu as pltpu
from jax.sharding import PartitionSpec as P

HD = 128
QH = 32
KVH = 4
BLK = 128
RBLK = 64


def rows_by_keys(left, right):
    return lax.dot_general(
        left, right, (((1,), (1,)), ((), ())), preferred_element_type=jnp.float32
    )


def body(hidden_rows, kv_weight, queries, cache_table, retrieval, pattern):
    partial_kv = jnp.dot(
        hidden_rows,
        lax.all_gather(kv_weight, "pool", axis=1, tiled=True),
        preferred_element_type=jnp.float32,
    )
    fresh = lax.psum_scatter(partial_kv.astype(jnp.bfloat16), "tp", scatter_dimension=1, tiled=True)
    wanted = retrieval[0]
    blocks_dev = cache_table.shape[0]
    npool = lax.axis_size("pool")
    owners = wanted // blocks_dev
    local = wanted % blocks_dev
    hits = (owners[:, None] == jnp.arange(npool, dtype=jnp.int32)[None, :]).astype(jnp.int32)
    request = jnp.sum(hits * (local + 1)[:, None], axis=0)
    incoming = lax.all_to_all(
        request.reshape(npool, 1), "pool", split_axis=0, concat_axis=0, tiled=True
    ).reshape(npool)
    reply = jnp.zeros((npool,) + cache_table.shape[1:], jnp.bfloat16)
    for slot in range(blocks_dev):
        reply = jnp.where((incoming == slot + 1)[:, None, None], cache_table[slot][None], reply)
    arrived = lax.all_to_all(reply, "pool", split_axis=0, concat_axis=0, tiled=True)
    fetched = jnp.take(arrived, owners, axis=0)
    count = hidden_rows.shape[0]
    fetch_count = wanted.shape[0]
    group = QH // KVH
    scale = float(HD) ** (-0.5)
    local_heads = fresh.shape[1] // (2 * HD)
    width = fetched.shape[2]
    per_step = math.gcd(fetch_count, 8)
    steps_count = fetch_count // per_step
    grouped = fetched.reshape(steps_count, per_step * BLK, width)
    pat_steps = jnp.transpose(
        pattern[0].reshape(pattern.shape[1], steps_count, per_step), (1, 0, 2)
    )
    token_of_row = jnp.arange(count * group) // group
    block_of_row = token_of_row // RBLK
    row_blocks = block_of_row[:, None, None] == jnp.arange(pattern.shape[1])[None, :, None]
    near_mask = token_of_row[:, None] >= jnp.arange(count)[None, :]
    q_heads = queries.reshape(count, local_heads, group * HD)
    q_rows = q_heads[:, 0].reshape(count * group, HD)
    near_keys = fresh[:, 0:HD]
    near_vals = fresh[:, HD : 2 * HD]
    near_scores = rows_by_keys(q_rows, near_keys) * scale
    top = jnp.max(jnp.where(near_mask, near_scores, -1e30), axis=1)
    weights = jnp.where(near_mask, jnp.exp(near_scores - top[:, None]), 0.0)
    total = jnp.sum(weights, axis=1)
    numer = jnp.dot(weights.astype(jnp.bfloat16), near_vals, preferred_element_type=jnp.float32)

    def visit(carry, items):
        top_now, total_now, numer_now = carry
        block_rows, pat_now = items
        keys = block_rows[:, 0:HD]
        vals = block_rows[:, HD : 2 * HD]
        scores = rows_by_keys(q_rows, keys) * scale
        row_pat = jnp.any(row_blocks & (pat_now[None] != 0), axis=1)
        mask = jnp.repeat(row_pat, BLK, axis=1)
        top_new = jnp.maximum(top_now, jnp.max(jnp.where(mask, scores, -1e30), axis=1))
        weights_now = jnp.where(mask, jnp.exp(scores - top_new[:, None]), 0.0)
        factor = jnp.exp(top_now - top_new)
        total_new = total_now * factor + jnp.sum(weights_now, axis=1)
        numer_new = numer_now * factor[:, None] + jnp.dot(
            weights_now.astype(jnp.bfloat16), vals, preferred_element_type=jnp.float32
        )
        return ((top_new, total_new, numer_new), None)

    (top, total, numer), unused = lax.scan(visit, (top, total, numer), (grouped, pat_steps))
    results = (numer / total[:, None]).reshape(count, group * HD)
    attended = results.astype(jnp.bfloat16)
    return (attended, fresh)


MESH = pl.DeviceIdType.MESH


def kernel(hid, wgt, q_hbm, cache_hbm, retr_hbm, pat_hbm, att, fresh, hbuf, wbuf, wsrc, pbuf, part,
           msg_out, msg_in, reply, arrived, top_ref, acc_ref, near_bias, q_ref, cache, retr, pat,
           h_recv, p_send, x_send, f_send, w_recv, w_send, v_send, m_recv, m_send, a_recv, a_send,
           s_recv, s_send, load_sem):
    npool = 8
    blocks_dev = cache.shape[0]
    fetch = retr.shape[1]
    rows, depth = hid.shape
    half_rows, half_depth = rows // 2, depth // 2
    loads = [
        pltpu.make_async_copy(src, dst, load_sem.at[n])
        for n, (src, dst) in enumerate(((retr_hbm, retr), (cache_hbm, cache), (q_hbm, q_ref), (pat_hbm, pat), (wgt, wsrc)))
    ]
    loads[0].start()
    loads[4].start()
    me = lax.axis_index("pool")
    t = lax.axis_index("tp")
    z, x = lax.div(me, 2), lax.rem(me, 2)
    a, b = lax.div(z, 2), lax.rem(z, 2)
    y = lax.div(t, 2)
    pair = (2 * a + 1 - b) * 2 + x
    other = z * 2 + 1 - x
    far = (2 - a) * 2 + x

    def peer(k):
        pa = 1 - a if k & 4 else a
        pb = 1 - b if k & 2 else b
        return (2 * pa + pb) * 2 + (1 - x if k & 1 else x)

    def remote(src, dst, ssem, rsem, pool, tp=None):
        where = {"pool": pool} if tp is None else {"pool": pool, "tp": tp}
        return pltpu.make_async_remote_copy(
            src_ref=src, dst_ref=dst, send_sem=ssem, recv_sem=rsem, device_id=where, device_id_type=MESH
        )

    def rows_at(slot, count=1):
        return pl.ds(pl.multiple_of(slot * rows, rows), count * rows)

    def half_at(slot, c):
        return pl.ds(pl.multiple_of(slot * rows + c * half_rows, half_rows), half_rows)

    def cols_at(slot):
        return pl.ds(pl.multiple_of(slot * HD, HD), HD)

    own_slot = b * 2 + x
    pair_slot = (1 - b) * 2 + x
    halves = (0, 1)
    h_in = [hid.at[pl.ds(c * half_rows, half_rows)] for c in halves]
    w_in = [wgt.at[pl.ds(c * half_depth, half_depth)] for c in halves]
    h_part = [hbuf.at[half_at(own_slot, c)] for c in halves]
    w_part = [wsrc.at[pl.ds(c * half_depth, half_depth)] for c in halves]
    w_land = [wbuf.at[pl.ds(c * half_depth, half_depth), cols_at(b)] for c in halves]

    own_h = [pltpu.make_async_copy(h_in[c], hbuf.at[half_at(own_slot, c)], h_recv.at[own_slot, c]) for c in halves]
    for c in halves:
        own_h[c].start()

    @pl.when(a == b)
    def _():
        for c in halves:
            pltpu.make_async_copy(w_in[c], w_land[c], w_recv.at[b, c]).start()

    for n in (1, 3, 2):
        loads[n].start()
    barrier = pltpu.get_barrier_semaphore()
    for k in range(1, npool):
        pl.semaphore_signal(barrier, inc=1, device_id={"pool": peer(k)}, device_id_type=MESH)
    for sx in range(2):
        for k in range(1, 4):
            pl.semaphore_signal(
                barrier, inc=1,
                device_id={"pool": (2 * a + y) * 2 + sx, "tp": lax.rem(t + k, 4)}, device_id_type=MESH,
            )
    loads[0].wait()

    wanted = [retr[0, f] for f in range(fetch)]
    owners = [lax.div(v, blocks_dev) for v in wanted]
    locals_ = [lax.rem(v, blocks_dev) for v in wanted]

    def slot_at(owner):
        total = jnp.int32(0)
        for f in range(fetch):
            total = total + jnp.where(owners[f] == owner, locals_[f], 0)
        return total

    ask, answers = [None], [None]
    for k in range(1, npool):
        msg_out[k] = jnp.full((8, 128), slot_at(peer(k)), jnp.int32)
        ask.append(remote(msg_out.at[k], msg_in.at[k], m_send.at[k], m_recv.at[k], peer(k)))
    for c in halves:
        own_h[c].wait()
    loads[4].wait()
    pl.semaphore_wait(barrier, npool - 1 + jnp.where(y == b, 4, 8))

    h_pair = [remote(h_part[c], hbuf.at[half_at(own_slot, c)], p_send.at[c], h_recv.at[own_slot, c], pair) for c in halves]
    h_other = [remote(h_part[c], hbuf.at[half_at(own_slot, c)], x_send.at[c], h_recv.at[own_slot, c], other) for c in halves]
    h_fwd = [
        remote(hbuf.at[half_at(pair_slot, c)], hbuf.at[half_at(pair_slot, c)], f_send.at[c], h_recv.at[pair_slot, c], other)
        for c in halves
    ]
    w_far = [remote(w_part[c], w_land[c], w_send.at[c], w_recv.at[b, c], far) for c in halves]
    w_near = [remote(w_part[c], w_land[c], v_send.at[c], w_recv.at[b, c], pair) for c in halves]

    for k in range(1, npool):
        ask[k].start()
    for c in halves:
        h_pair[c].start()
    for c in halves:
        h_other[c].start()

    @pl.when(a != b)
    def _():
        for c in halves:
            w_far[c].start()

    def h_wait(slot, c):
        pltpu.make_async_copy(h_in[c], hbuf.at[half_at(slot, c)], h_recv.at[slot, c]).wait()

    for c in halves:
        h_pair[c].wait_send()

        @pl.when(a == b)
        def _():
            w_far[c].start()

        @pl.when(a != b)
        def _():
            w_near[c].start()

        h_wait(pair_slot, c)
        h_fwd[c].start()
        if c == 0:
            loads[1].wait()
            arrived[0] = cache[slot_at(me)]
            for k in range(1, npool):
                ask[k].wait_recv()
                reply[k] = cache[jnp.max(msg_in[k])]
                answers.append(remote(reply.at[k], arrived.at[k], a_send.at[k], a_recv.at[k], peer(k)))
    for c in halves:
        w_far[c].wait_send()

        @pl.when(a != b)
        def _():
            w_near[c].wait_send()

        for k in ((6,), (4, 2))[c]:
            answers[k].start()

    def w_wait(c):
        for n in range(2):
            pltpu.make_async_copy(
                w_in[c], wbuf.at[pl.ds(c * half_depth, half_depth), pl.ds(n * HD, HD)], w_recv.at[n, c]
            ).wait()

    def product(zl, c):
        at = pl.ds(c * half_depth, half_depth)
        return jnp.dot(hbuf[rows_at(zl * 2, 2), at], wbuf[at, :], preferred_element_type=jnp.float32)

    def hand_out(zl, block):
        for sx in range(2):
            for i in range(2):
                j = zl * 2 + sx
                src = pbuf.at[j, i]
                src[...] = block[sx * rows:(sx + 1) * rows, i * HD:(i + 1) * HD].astype(jnp.bfloat16)
                mine = jnp.logical_and(4 * a + j == me, 2 * b + i == t)

                @pl.when(mine)
                def _():
                    pltpu.make_async_copy(src, part.at[x, t], s_recv.at[x, t]).start()

                @pl.when(jnp.logical_not(mine))
                def _():
                    remote(src, part.at[x, t], s_send.at[j, i], s_recv.at[x, t], 4 * a + j, 2 * b + i).start()

    for c in halves:
        h_wait(b * 2 + 1 - x, c)
    w_wait(0)
    first = product(b, 0)
    w_wait(1)
    hand_out(b, first + product(b, 1))
    for c in halves:
        h_wait((1 - b) * 2 + 1 - x, c)
    hand_out(1 - b, product(1 - b, 0) + product(1 - b, 1))
    for k in (7, 5, 3, 1):
        answers[k].start()

    token = lax.broadcasted_iota(jnp.int32, (rows, rows), 0)
    near_bias[...] = jnp.where(token >= lax.broadcasted_iota(jnp.int32, (rows, rows), 1), 0.0, -1e30)
    loads[2].wait()
    loads[3].wait()

    rate = float(HD) ** (-0.5) * math.log2(math.e)
    r_blocks = pat.shape[1]

    def bias_of(k, r):
        owner = me if k == 0 else peer(k)
        named = jnp.int32(0)
        for f in range(fetch):
            named = named + jnp.where(owners[f] == owner, pat[0, r, f], 0)
        return jnp.where(named != 0, jnp.float32(0.0), jnp.float32(-1e30))

    def stage(first, near, ks, last):
        biases = [[bias_of(k, r) for r in range(r_blocks)] for k in ks]

        @pl.loop(0, q_ref.shape[1] // (2 * HD), unroll=2)
        def _(step):
            ats = [pl.ds(pl.multiple_of(step * 2 * HD + h * HD, HD), HD) for h in range(2)]
            keys = [arrived[k, :, 0:HD] for k in ks]
            vals = [arrived[k, :, HD:2 * HD] for k in ks]
            if near:
                keys.append(fresh[:, 0:HD])
                vals.append(fresh[:, HD:2 * HD])
            keys = jnp.concatenate(keys, axis=0)
            vals = jnp.concatenate(vals, axis=0)
            vals = jnp.concatenate([vals, jnp.ones_like(vals)], axis=1)
            raw = rows_by_keys(jnp.concatenate([q_ref[:, at] for at in ats], axis=0), keys)
            rounded, factors = [], []
            for h in range(2):
                scores = []
                for n in range(len(ks)):
                    scores.append(jnp.concatenate([
                        raw[h * rows + r * RBLK:h * rows + (r + 1) * RBLK, n * BLK:(n + 1) * BLK] + biases[n][r]
                        for r in range(r_blocks)
                    ], axis=0))
                if near:
                    scores.append(raw[h * rows:(h + 1) * rows, len(ks) * BLK:] + near_bias[...])
                top = scores[0]
                for one in scores[1:]:
                    top = jnp.maximum(top, one)
                top = jnp.broadcast_to(jnp.max(top, axis=1, keepdims=True), (rows, HD))
                if not first:
                    before = top_ref[2 * step + h]
                    top = jnp.maximum(before, top)
                    factors.append(jnp.exp2((before - top) * rate))
                if not last:
                    top_ref[2 * step + h] = top
                rounded.append(jnp.concatenate(
                    [jnp.exp2((one - top) * rate).astype(jnp.bfloat16) for one in scores], axis=1
                ))
            both = jnp.dot(jnp.concatenate(rounded, axis=0), vals, preferred_element_type=jnp.float32)
            for h in range(2):
                numer = both[h * rows:(h + 1) * rows, 0:HD]
                denom = both[h * rows:(h + 1) * rows, HD:2 * HD]
                if not first:
                    numer = numer + factors[h] * acc_ref[2 * step + h, :, 0:HD]
                    denom = denom + factors[h] * acc_ref[2 * step + h, :, HD:2 * HD]
                if last:
                    att[:, ats[h]] = (numer / denom).astype(jnp.bfloat16)
                else:
                    acc_ref[2 * step + h, :, 0:HD] = numer
                    acc_ref[2 * step + h, :, HD:2 * HD] = denom

    for k in (2, 6, 4):
        answers[k].wait_recv()
    stage(True, False, (0, 2, 6, 4), False)
    for kind in range(2):
        total = jnp.zeros((rows, HD), jnp.float32)
        for n in range(4):
            pltpu.make_async_copy(pbuf.at[0, 0], part.at[kind, n], s_recv.at[kind, n]).wait()
            total = total + part[kind, n].astype(jnp.float32)
        fresh[:, kind * HD:(kind + 1) * HD] = total.astype(jnp.bfloat16)
    for k in (1, 3):
        answers[k].wait_recv()
    stage(False, True, (1, 3), False)
    for k in (7, 5):
        answers[k].wait_recv()
    stage(False, False, (7, 5), True)

    for c in halves:
        h_other[c].wait_send()
        h_fwd[c].wait_send()
    for k in range(1, npool):
        ask[k].wait_send()
        answers[k].wait_send()
    for j in range(4):
        for i in range(2):
            mine = jnp.logical_and(4 * a + j == me, 2 * b + i == t)

            @pl.when(jnp.logical_not(mine))
            def _():
                remote(pbuf.at[j, i], part.at[x, t], s_send.at[j, i], s_recv.at[x, t], 4 * a + j, 2 * b + i).wait_send()


def fused(hidden_rows, kv_weight, queries, cache_table, retrieval, pattern):
    rows, depth = hidden_rows.shape
    cols = kv_weight.shape[1]
    blocks_dev, _, width = cache_table.shape
    dma = pltpu.SemaphoreType.DMA
    hbm = pl.BlockSpec(memory_space=pltpu.HBM)
    vmem = pl.BlockSpec(memory_space=pltpu.VMEM)
    bf = jnp.bfloat16
    return pl.pallas_call(
        kernel,
        out_shape=(
            pltpu.VMEM(queries.shape, bf),
            pltpu.VMEM((rows, width), bf),
        ),
        in_specs=[hbm] * 6,
        out_specs=(vmem, vmem),
        scratch_shapes=[
            pltpu.VMEM((4 * rows, depth), bf),
            pltpu.VMEM((depth, 2 * cols), bf),
            pltpu.VMEM((depth, cols), bf),
            pltpu.VMEM((4, 2, rows, HD), bf),
            pltpu.VMEM((2, 4, rows, HD), bf),
            pltpu.VMEM((8, 8, 128), jnp.int32),
            pltpu.VMEM((8, 8, 128), jnp.int32),
            pltpu.VMEM((8, BLK, width), bf),
            pltpu.VMEM((8, BLK, width), bf),
            pltpu.VMEM((queries.shape[1] // HD, rows, HD), jnp.float32),
            pltpu.VMEM((queries.shape[1] // HD, rows, 2 * HD), jnp.float32),
            pltpu.VMEM((rows, rows), jnp.float32),
            pltpu.VMEM(queries.shape, bf),
            pltpu.VMEM(cache_table.shape, bf),
            pltpu.SMEM(retrieval.shape, jnp.int32),
            pltpu.SMEM(pattern.shape, jnp.int32),
            dma((4, 2)), dma((2,)), dma((2,)), dma((2,)), dma((2, 2)), dma((2,)), dma((2,)),
            dma((8,)), dma((8,)), dma((8,)), dma((8,)), dma((2, 4)), dma((4, 2)), dma((5,)),
        ],
        compiler_params=pltpu.CompilerParams(
            collective_id=0, has_side_effects=True, vmem_limit_bytes=62 * 1024 * 1024
        ),
        name="blend",
    )(hidden_rows, kv_weight, queries, cache_table, retrieval, pattern)


def fits(mesh, hidden_rows, kv_weight, cache_table, retrieval):
    return (
        mesh.shape["pool"] == 8
        and mesh.shape["tp"] == 4
        and hidden_rows.shape[0] == 8 * BLK
        and kv_weight.shape[1] == 8 * HD
        and cache_table.shape[2] == 8 * HD
        and retrieval.shape[1] <= 8
    )


def solution(mesh):
    placed = (
        P("pool", "tp"),
        P("tp", "pool"),
        P("pool", "tp"),
        P("pool", None, "tp"),
        P("pool", None),
        P("pool", None, None),
    )

    def run(hidden_rows, kv_weight, queries, cache_table, retrieval, pattern):
        small = fits(mesh, hidden_rows, kv_weight, cache_table, retrieval)
        return jax.shard_map(
            fused if small else body,
            mesh=mesh,
            in_specs=placed,
            out_specs=(P("pool", "tp"), P("pool", "tp")),
            check_vma=False,
        )(hidden_rows, kv_weight, queries, cache_table, retrieval, pattern)

    return run
```

```python
import math

import jax
import jax.numpy as jnp
from jax import lax
from jax.experimental import pallas as pl
from jax.experimental.pallas import tpu as pltpu
from jax.sharding import PartitionSpec as P

HD = 128
QH = 32
KVH = 4
BLK = 128
RBLK = 64


def rows_by_keys(left, right):
    return lax.dot_general(
        left, right, (((1,), (1,)), ((), ())), preferred_element_type=jnp.float32
    )


def body(hidden_rows, kv_weight, queries, cache_table, retrieval, pattern):
    partial_kv = jnp.dot(
        hidden_rows,
        lax.all_gather(kv_weight, "pool", axis=1, tiled=True),
        preferred_element_type=jnp.float32,
    )
    fresh = lax.psum_scatter(partial_kv.astype(jnp.bfloat16), "tp", scatter_dimension=1, tiled=True)
    wanted = retrieval[0]
    blocks_dev = cache_table.shape[0]
    npool = lax.axis_size("pool")
    owners = wanted // blocks_dev
    local = wanted % blocks_dev
    hits = (owners[:, None] == jnp.arange(npool, dtype=jnp.int32)[None, :]).astype(jnp.int32)
    request = jnp.sum(hits * (local + 1)[:, None], axis=0)
    incoming = lax.all_to_all(
        request.reshape(npool, 1), "pool", split_axis=0, concat_axis=0, tiled=True
    ).reshape(npool)
    reply = jnp.zeros((npool,) + cache_table.shape[1:], jnp.bfloat16)
    for slot in range(blocks_dev):
        reply = jnp.where((incoming == slot + 1)[:, None, None], cache_table[slot][None], reply)
    arrived = lax.all_to_all(reply, "pool", split_axis=0, concat_axis=0, tiled=True)
    fetched = jnp.take(arrived, owners, axis=0)
    count = hidden_rows.shape[0]
    fetch_count = wanted.shape[0]
    group = QH // KVH
    scale = float(HD) ** (-0.5)
    local_heads = fresh.shape[1] // (2 * HD)
    width = fetched.shape[2]
    per_step = math.gcd(fetch_count, 8)
    steps_count = fetch_count // per_step
    grouped = fetched.reshape(steps_count, per_step * BLK, width)
    pat_steps = jnp.transpose(
        pattern[0].reshape(pattern.shape[1], steps_count, per_step), (1, 0, 2)
    )
    token_of_row = jnp.arange(count * group) // group
    block_of_row = token_of_row // RBLK
    row_blocks = block_of_row[:, None, None] == jnp.arange(pattern.shape[1])[None, :, None]
    near_mask = token_of_row[:, None] >= jnp.arange(count)[None, :]
    q_heads = queries.reshape(count, local_heads, group * HD)
    q_rows = q_heads[:, 0].reshape(count * group, HD)
    near_keys = fresh[:, 0:HD]
    near_vals = fresh[:, HD : 2 * HD]
    near_scores = rows_by_keys(q_rows, near_keys) * scale
    top = jnp.max(jnp.where(near_mask, near_scores, -1e30), axis=1)
    weights = jnp.where(near_mask, jnp.exp(near_scores - top[:, None]), 0.0)
    total = jnp.sum(weights, axis=1)
    numer = jnp.dot(weights.astype(jnp.bfloat16), near_vals, preferred_element_type=jnp.float32)

    def visit(carry, items):
        top_now, total_now, numer_now = carry
        block_rows, pat_now = items
        keys = block_rows[:, 0:HD]
        vals = block_rows[:, HD : 2 * HD]
        scores = rows_by_keys(q_rows, keys) * scale
        row_pat = jnp.any(row_blocks & (pat_now[None] != 0), axis=1)
        mask = jnp.repeat(row_pat, BLK, axis=1)
        top_new = jnp.maximum(top_now, jnp.max(jnp.where(mask, scores, -1e30), axis=1))
        weights_now = jnp.where(mask, jnp.exp(scores - top_new[:, None]), 0.0)
        factor = jnp.exp(top_now - top_new)
        total_new = total_now * factor + jnp.sum(weights_now, axis=1)
        numer_new = numer_now * factor[:, None] + jnp.dot(
            weights_now.astype(jnp.bfloat16), vals, preferred_element_type=jnp.float32
        )
        return ((top_new, total_new, numer_new), None)

    (top, total, numer), unused = lax.scan(visit, (top, total, numer), (grouped, pat_steps))
    results = (numer / total[:, None]).reshape(count, group * HD)
    attended = results.astype(jnp.bfloat16)
    return (attended, fresh)


MESH = pl.DeviceIdType.MESH


def kernel(hid, wgt, q_hbm, cache_hbm, retr_hbm, pat_hbm, att, fresh, hbuf, wbuf, wsrc, pbuf, part,
           msg_out, msg_in, reply, arrived, top_ref, acc_ref, near_bias, q_ref, cache, retr, pat,
           h_recv, p_send, x_send, f_send, w_recv, w_send, v_send, m_recv, m_send, a_recv, a_send,
           s_recv, s_send, load_sem):
    npool = 8
    blocks_dev = cache.shape[0]
    fetch = retr.shape[1]
    rows, depth = hid.shape
    half_rows, half_depth = rows // 2, depth // 2
    loads = [
        pltpu.make_async_copy(src, dst, load_sem.at[n])
        for n, (src, dst) in enumerate(((retr_hbm, retr), (cache_hbm, cache), (q_hbm, q_ref), (pat_hbm, pat), (wgt, wsrc)))
    ]
    loads[0].start()
    loads[4].start()
    me = lax.axis_index("pool")
    t = lax.axis_index("tp")
    z, x = lax.div(me, 2), lax.rem(me, 2)
    a, b = lax.div(z, 2), lax.rem(z, 2)
    y = lax.div(t, 2)
    pair = (2 * a + 1 - b) * 2 + x
    other = z * 2 + 1 - x
    far = (2 - a) * 2 + x

    def peer(k):
        pa = 1 - a if k & 4 else a
        pb = 1 - b if k & 2 else b
        return (2 * pa + pb) * 2 + (1 - x if k & 1 else x)

    def remote(src, dst, ssem, rsem, pool, tp=None):
        where = {"pool": pool} if tp is None else {"pool": pool, "tp": tp}
        return pltpu.make_async_remote_copy(
            src_ref=src, dst_ref=dst, send_sem=ssem, recv_sem=rsem, device_id=where, device_id_type=MESH
        )

    def rows_at(slot, count=1):
        return pl.ds(pl.multiple_of(slot * rows, rows), count * rows)

    def half_at(slot, c):
        return pl.ds(pl.multiple_of(slot * rows + c * half_rows, half_rows), half_rows)

    def cols_at(slot):
        return pl.ds(pl.multiple_of(slot * HD, HD), HD)

    own_slot = b * 2 + x
    pair_slot = (1 - b) * 2 + x
    halves = (0, 1)
    h_in = [hid.at[pl.ds(c * half_rows, half_rows)] for c in halves]
    w_in = [wgt.at[pl.ds(c * half_depth, half_depth)] for c in halves]
    h_part = [hbuf.at[half_at(own_slot, c)] for c in halves]
    w_part = [wsrc.at[pl.ds(c * half_depth, half_depth)] for c in halves]
    w_land = [wbuf.at[pl.ds(c * half_depth, half_depth), cols_at(b)] for c in halves]

    own_h = [pltpu.make_async_copy(h_in[c], hbuf.at[half_at(own_slot, c)], h_recv.at[own_slot, c]) for c in halves]
    for c in halves:
        own_h[c].start()

    @pl.when(a == b)
    def _():
        for c in halves:
            pltpu.make_async_copy(w_in[c], w_land[c], w_recv.at[b, c]).start()

    for n in (1, 3, 2):
        loads[n].start()
    barrier = pltpu.get_barrier_semaphore()
    for k in range(1, npool):
        pl.semaphore_signal(barrier, inc=1, device_id={"pool": peer(k)}, device_id_type=MESH)
    for sx in range(2):
        for k in range(1, 4):
            pl.semaphore_signal(
                barrier, inc=1,
                device_id={"pool": (2 * a + y) * 2 + sx, "tp": lax.rem(t + k, 4)}, device_id_type=MESH,
            )
    loads[0].wait()

    wanted = [retr[0, f] for f in range(fetch)]
    owners = [lax.div(v, blocks_dev) for v in wanted]
    locals_ = [lax.rem(v, blocks_dev) for v in wanted]

    def slot_at(owner):
        total = jnp.int32(0)
        for f in range(fetch):
            total = total + jnp.where(owners[f] == owner, locals_[f], 0)
        return total

    ask, answers = [None], [None]
    for k in range(1, npool):
        msg_out[k] = jnp.full((8, 128), slot_at(peer(k)), jnp.int32)
        ask.append(remote(msg_out.at[k], msg_in.at[k], m_send.at[k], m_recv.at[k], peer(k)))
    for c in halves:
        own_h[c].wait()
    loads[4].wait()
    pl.semaphore_wait(barrier, npool - 1 + jnp.where(y == b, 4, 8))

    h_pair = [remote(h_part[c], hbuf.at[half_at(own_slot, c)], p_send.at[c], h_recv.at[own_slot, c], pair) for c in halves]
    h_other = [remote(h_part[c], hbuf.at[half_at(own_slot, c)], x_send.at[c], h_recv.at[own_slot, c], other) for c in halves]
    h_fwd = [
        remote(hbuf.at[half_at(pair_slot, c)], hbuf.at[half_at(pair_slot, c)], f_send.at[c], h_recv.at[pair_slot, c], other)
        for c in halves
    ]
    w_far = [remote(w_part[c], w_land[c], w_send.at[c], w_recv.at[b, c], far) for c in halves]
    w_near = [remote(w_part[c], w_land[c], v_send.at[c], w_recv.at[b, c], pair) for c in halves]

    for k in range(1, npool):
        ask[k].start()
    for c in halves:
        h_pair[c].start()
    for c in halves:
        h_other[c].start()

    @pl.when(a != b)
    def _():
        for c in halves:
            w_far[c].start()

    def h_wait(slot, c):
        pltpu.make_async_copy(h_in[c], hbuf.at[half_at(slot, c)], h_recv.at[slot, c]).wait()

    for c in halves:
        h_pair[c].wait_send()

        @pl.when(a == b)
        def _():
            w_far[c].start()

        @pl.when(a != b)
        def _():
            w_near[c].start()

        h_wait(pair_slot, c)
        h_fwd[c].start()
        if c == 0:
            loads[1].wait()
            arrived[0] = cache[slot_at(me)]
            for k in range(1, npool):
                ask[k].wait_recv()
                reply[k] = cache[jnp.max(msg_in[k])]
                answers.append(remote(reply.at[k], arrived.at[k], a_send.at[k], a_recv.at[k], peer(k)))
    for c in halves:
        w_far[c].wait_send()

        @pl.when(a != b)
        def _():
            w_near[c].wait_send()

        for k in ((6, 7), (2, 3, 1, 4))[c]:
            answers[k].start()

    def w_wait(c):
        for n in range(2):
            pltpu.make_async_copy(
                w_in[c], wbuf.at[pl.ds(c * half_depth, half_depth), pl.ds(n * HD, HD)], w_recv.at[n, c]
            ).wait()

    def product(zl, c):
        at = pl.ds(c * half_depth, half_depth)
        return jnp.dot(hbuf[rows_at(zl * 2, 2), at], wbuf[at, :], preferred_element_type=jnp.float32)

    def hand_out(zl, block):
        for sx in range(2):
            for i in range(2):
                j = zl * 2 + sx
                src = pbuf.at[j, i]
                src[...] = block[sx * rows:(sx + 1) * rows, i * HD:(i + 1) * HD].astype(jnp.bfloat16)
                mine = jnp.logical_and(4 * a + j == me, 2 * b + i == t)

                @pl.when(mine)
                def _():
                    pltpu.make_async_copy(src, part.at[x, t], s_recv.at[x, t]).start()

                @pl.when(jnp.logical_not(mine))
                def _():
                    remote(src, part.at[x, t], s_send.at[j, i], s_recv.at[x, t], 4 * a + j, 2 * b + i).start()

    for c in halves:
        h_wait(b * 2 + 1 - x, c)
    w_wait(0)
    first = product(b, 0)
    w_wait(1)
    hand_out(b, first + product(b, 1))
    for c in halves:
        h_wait((1 - b) * 2 + 1 - x, c)
    hand_out(1 - b, product(1 - b, 0) + product(1 - b, 1))
    answers[5].start()

    token = lax.broadcasted_iota(jnp.int32, (rows, rows), 0)
    near_bias[...] = jnp.where(token >= lax.broadcasted_iota(jnp.int32, (rows, rows), 1), 0.0, -1e30)
    loads[2].wait()
    loads[3].wait()

    rate = float(HD) ** (-0.5) * math.log2(math.e)
    r_blocks = pat.shape[1]

    def bias_of(k, r):
        owner = me if k == 0 else peer(k)
        named = jnp.int32(0)
        for f in range(fetch):
            named = named + jnp.where(owners[f] == owner, pat[0, r, f], 0)
        return jnp.where(named != 0, jnp.float32(0.0), jnp.float32(-1e30))

    def stage(first, near, ks, last):
        biases = [[bias_of(k, r) for r in range(r_blocks)] for k in ks]

        @pl.loop(0, q_ref.shape[1] // (2 * HD), unroll=2)
        def _(step):
            ats = [pl.ds(pl.multiple_of(step * 2 * HD + h * HD, HD), HD) for h in range(2)]
            keys = [arrived[k, :, 0:HD] for k in ks]
            vals = [arrived[k, :, HD:2 * HD] for k in ks]
            if near:
                keys.append(fresh[:, 0:HD])
                vals.append(fresh[:, HD:2 * HD])
            keys = jnp.concatenate(keys, axis=0)
            vals = jnp.concatenate(vals, axis=0)
            vals = jnp.concatenate([vals, jnp.ones_like(vals)], axis=1)
            raw = rows_by_keys(jnp.concatenate([q_ref[:, at] for at in ats], axis=0), keys)
            rounded, factors = [], []
            for h in range(2):
                scores = []
                for n in range(len(ks)):
                    scores.append(jnp.concatenate([
                        raw[h * rows + r * RBLK:h * rows + (r + 1) * RBLK, n * BLK:(n + 1) * BLK] + biases[n][r]
                        for r in range(r_blocks)
                    ], axis=0))
                if near:
                    scores.append(raw[h * rows:(h + 1) * rows, len(ks) * BLK:] + near_bias[...])
                top = scores[0]
                for one in scores[1:]:
                    top = jnp.maximum(top, one)
                top = jnp.broadcast_to(jnp.max(top, axis=1, keepdims=True), (rows, HD))
                if not first:
                    before = top_ref[2 * step + h]
                    top = jnp.maximum(before, top)
                    factors.append(jnp.exp2((before - top) * rate))
                if not last:
                    top_ref[2 * step + h] = top
                rounded.append(jnp.concatenate(
                    [jnp.exp2((one - top) * rate).astype(jnp.bfloat16) for one in scores], axis=1
                ))
            both = jnp.dot(jnp.concatenate(rounded, axis=0), vals, preferred_element_type=jnp.float32)
            for h in range(2):
                numer = both[h * rows:(h + 1) * rows, 0:HD]
                denom = both[h * rows:(h + 1) * rows, HD:2 * HD]
                if not first:
                    numer = numer + factors[h] * acc_ref[2 * step + h, :, 0:HD]
                    denom = denom + factors[h] * acc_ref[2 * step + h, :, HD:2 * HD]
                if last:
                    att[:, ats[h]] = (numer / denom).astype(jnp.bfloat16)
                else:
                    acc_ref[2 * step + h, :, 0:HD] = numer
                    acc_ref[2 * step + h, :, HD:2 * HD] = denom

    for k in (1, 2, 3):
        answers[k].wait_recv()
    stage(True, False, (0, 1, 2, 3), False)
    for kind in range(2):
        total = jnp.zeros((rows, HD), jnp.float32)
        for n in range(4):
            pltpu.make_async_copy(pbuf.at[0, 0], part.at[kind, n], s_recv.at[kind, n]).wait()
            total = total + part[kind, n].astype(jnp.float32)
        fresh[:, kind * HD:(kind + 1) * HD] = total.astype(jnp.bfloat16)
    for k in (6, 7, 4):
        answers[k].wait_recv()
    stage(False, True, (6, 7, 4), False)
    answers[5].wait_recv()
    stage(False, False, (5,), True)

    for c in halves:
        h_other[c].wait_send()
        h_fwd[c].wait_send()
    for k in range(1, npool):
        ask[k].wait_send()
        answers[k].wait_send()
    for j in range(4):
        for i in range(2):
            mine = jnp.logical_and(4 * a + j == me, 2 * b + i == t)

            @pl.when(jnp.logical_not(mine))
            def _():
                remote(pbuf.at[j, i], part.at[x, t], s_send.at[j, i], s_recv.at[x, t], 4 * a + j, 2 * b + i).wait_send()


def fused(hidden_rows, kv_weight, queries, cache_table, retrieval, pattern):
    rows, depth = hidden_rows.shape
    cols = kv_weight.shape[1]
    blocks_dev, _, width = cache_table.shape
    dma = pltpu.SemaphoreType.DMA
    hbm = pl.BlockSpec(memory_space=pltpu.HBM)
    vmem = pl.BlockSpec(memory_space=pltpu.VMEM)
    bf = jnp.bfloat16
    return pl.pallas_call(
        kernel,
        out_shape=(
            pltpu.VMEM(queries.shape, bf),
            pltpu.VMEM((rows, width), bf),
        ),
        in_specs=[hbm] * 6,
        out_specs=(vmem, vmem),
        scratch_shapes=[
            pltpu.VMEM((4 * rows, depth), bf),
            pltpu.VMEM((depth, 2 * cols), bf),
            pltpu.VMEM((depth, cols), bf),
            pltpu.VMEM((4, 2, rows, HD), bf),
            pltpu.VMEM((2, 4, rows, HD), bf),
            pltpu.VMEM((8, 8, 128), jnp.int32),
            pltpu.VMEM((8, 8, 128), jnp.int32),
            pltpu.VMEM((8, BLK, width), bf),
            pltpu.VMEM((8, BLK, width), bf),
            pltpu.VMEM((queries.shape[1] // HD, rows, HD), jnp.float32),
            pltpu.VMEM((queries.shape[1] // HD, rows, 2 * HD), jnp.float32),
            pltpu.VMEM((rows, rows), jnp.float32),
            pltpu.VMEM(queries.shape, bf),
            pltpu.VMEM(cache_table.shape, bf),
            pltpu.SMEM(retrieval.shape, jnp.int32),
            pltpu.SMEM(pattern.shape, jnp.int32),
            dma((4, 2)), dma((2,)), dma((2,)), dma((2,)), dma((2, 2)), dma((2,)), dma((2,)),
            dma((8,)), dma((8,)), dma((8,)), dma((8,)), dma((2, 4)), dma((4, 2)), dma((5,)),
        ],
        compiler_params=pltpu.CompilerParams(
            collective_id=0, has_side_effects=True, vmem_limit_bytes=62 * 1024 * 1024
        ),
        name="blend",
    )(hidden_rows, kv_weight, queries, cache_table, retrieval, pattern)


def fits(mesh, hidden_rows, kv_weight, cache_table, retrieval):
    return (
        mesh.shape["pool"] == 8
        and mesh.shape["tp"] == 4
        and hidden_rows.shape[0] == 8 * BLK
        and kv_weight.shape[1] == 8 * HD
        and cache_table.shape[2] == 8 * HD
        and retrieval.shape[1] <= 8
    )


def solution(mesh):
    placed = (
        P("pool", "tp"),
        P("tp", "pool"),
        P("pool", "tp"),
        P("pool", None, "tp"),
        P("pool", None),
        P("pool", None, None),
    )

    def run(hidden_rows, kv_weight, queries, cache_table, retrieval, pattern):
        small = fits(mesh, hidden_rows, kv_weight, cache_table, retrieval)
        return jax.shard_map(
            fused if small else body,
            mesh=mesh,
            in_specs=placed,
            out_specs=(P("pool", "tp"), P("pool", "tp")),
            check_vma=False,
        )(hidden_rows, kv_weight, queries, cache_table, retrieval, pattern)

    return run
```

```python
import math

import jax
import jax.numpy as jnp
from jax import lax
from jax.experimental import pallas as pl
from jax.experimental.pallas import tpu as pltpu
from jax.sharding import PartitionSpec as P

HD = 128
QH = 32
KVH = 4
BLK = 128
RBLK = 64


def rows_by_keys(left, right):
    return lax.dot_general(
        left, right, (((1,), (1,)), ((), ())), preferred_element_type=jnp.float32
    )


def body(hidden_rows, kv_weight, queries, cache_table, retrieval, pattern):
    partial_kv = jnp.dot(
        hidden_rows,
        lax.all_gather(kv_weight, "pool", axis=1, tiled=True),
        preferred_element_type=jnp.float32,
    )
    fresh = lax.psum_scatter(partial_kv.astype(jnp.bfloat16), "tp", scatter_dimension=1, tiled=True)
    wanted = retrieval[0]
    blocks_dev = cache_table.shape[0]
    npool = lax.axis_size("pool")
    owners = wanted // blocks_dev
    local = wanted % blocks_dev
    hits = (owners[:, None] == jnp.arange(npool, dtype=jnp.int32)[None, :]).astype(jnp.int32)
    request = jnp.sum(hits * (local + 1)[:, None], axis=0)
    incoming = lax.all_to_all(
        request.reshape(npool, 1), "pool", split_axis=0, concat_axis=0, tiled=True
    ).reshape(npool)
    reply = jnp.zeros((npool,) + cache_table.shape[1:], jnp.bfloat16)
    for slot in range(blocks_dev):
        reply = jnp.where((incoming == slot + 1)[:, None, None], cache_table[slot][None], reply)
    arrived = lax.all_to_all(reply, "pool", split_axis=0, concat_axis=0, tiled=True)
    fetched = jnp.take(arrived, owners, axis=0)
    count = hidden_rows.shape[0]
    fetch_count = wanted.shape[0]
    group = QH // KVH
    scale = float(HD) ** (-0.5)
    local_heads = fresh.shape[1] // (2 * HD)
    width = fetched.shape[2]
    per_step = math.gcd(fetch_count, 8)
    steps_count = fetch_count // per_step
    grouped = fetched.reshape(steps_count, per_step * BLK, width)
    pat_steps = jnp.transpose(
        pattern[0].reshape(pattern.shape[1], steps_count, per_step), (1, 0, 2)
    )
    token_of_row = jnp.arange(count * group) // group
    block_of_row = token_of_row // RBLK
    row_blocks = block_of_row[:, None, None] == jnp.arange(pattern.shape[1])[None, :, None]
    near_mask = token_of_row[:, None] >= jnp.arange(count)[None, :]
    q_heads = queries.reshape(count, local_heads, group * HD)
    q_rows = q_heads[:, 0].reshape(count * group, HD)
    near_keys = fresh[:, 0:HD]
    near_vals = fresh[:, HD : 2 * HD]
    near_scores = rows_by_keys(q_rows, near_keys) * scale
    top = jnp.max(jnp.where(near_mask, near_scores, -1e30), axis=1)
    weights = jnp.where(near_mask, jnp.exp(near_scores - top[:, None]), 0.0)
    total = jnp.sum(weights, axis=1)
    numer = jnp.dot(weights.astype(jnp.bfloat16), near_vals, preferred_element_type=jnp.float32)

    def visit(carry, items):
        top_now, total_now, numer_now = carry
        block_rows, pat_now = items
        keys = block_rows[:, 0:HD]
        vals = block_rows[:, HD : 2 * HD]
        scores = rows_by_keys(q_rows, keys) * scale
        row_pat = jnp.any(row_blocks & (pat_now[None] != 0), axis=1)
        mask = jnp.repeat(row_pat, BLK, axis=1)
        top_new = jnp.maximum(top_now, jnp.max(jnp.where(mask, scores, -1e30), axis=1))
        weights_now = jnp.where(mask, jnp.exp(scores - top_new[:, None]), 0.0)
        factor = jnp.exp(top_now - top_new)
        total_new = total_now * factor + jnp.sum(weights_now, axis=1)
        numer_new = numer_now * factor[:, None] + jnp.dot(
            weights_now.astype(jnp.bfloat16), vals, preferred_element_type=jnp.float32
        )
        return ((top_new, total_new, numer_new), None)

    (top, total, numer), unused = lax.scan(visit, (top, total, numer), (grouped, pat_steps))
    results = (numer / total[:, None]).reshape(count, group * HD)
    attended = results.astype(jnp.bfloat16)
    return (attended, fresh)


MESH = pl.DeviceIdType.MESH


def kernel(hid, wgt, q_hbm, cache_hbm, retr_hbm, pat_hbm, att, fresh, hbuf, wbuf, wsrc, pbuf, part,
           msg_out, msg_in, reply, arrived, top_ref, acc_ref, near_bias, q_ref, cache, retr, pat,
           h_recv, p_send, x_send, f_send, w_recv, w_send, v_send, m_recv, m_send, a_recv, a_send,
           s_recv, s_send, load_sem):
    npool = 8
    blocks_dev = cache.shape[0]
    fetch = retr.shape[1]
    rows, depth = hid.shape
    half_rows, half_depth = rows // 2, depth // 2
    loads = [
        pltpu.make_async_copy(src, dst, load_sem.at[n])
        for n, (src, dst) in enumerate(((retr_hbm, retr), (cache_hbm, cache), (q_hbm, q_ref), (pat_hbm, pat), (wgt, wsrc)))
    ]
    loads[0].start()
    loads[4].start()
    me = lax.axis_index("pool")
    t = lax.axis_index("tp")
    z, x = lax.div(me, 2), lax.rem(me, 2)
    a, b = lax.div(z, 2), lax.rem(z, 2)
    y = lax.div(t, 2)
    pair = (2 * a + 1 - b) * 2 + x
    other = z * 2 + 1 - x
    far = (2 - a) * 2 + x

    def peer(k):
        pa = 1 - a if k & 4 else a
        pb = 1 - b if k & 2 else b
        return (2 * pa + pb) * 2 + (1 - x if k & 1 else x)

    def remote(src, dst, ssem, rsem, pool, tp=None):
        where = {"pool": pool} if tp is None else {"pool": pool, "tp": tp}
        return pltpu.make_async_remote_copy(
            src_ref=src, dst_ref=dst, send_sem=ssem, recv_sem=rsem, device_id=where, device_id_type=MESH
        )

    def rows_at(slot, count=1):
        return pl.ds(pl.multiple_of(slot * rows, rows), count * rows)

    def half_at(slot, c):
        return pl.ds(pl.multiple_of(slot * rows + c * half_rows, half_rows), half_rows)

    def cols_at(slot):
        return pl.ds(pl.multiple_of(slot * HD, HD), HD)

    own_slot = b * 2 + x
    pair_slot = (1 - b) * 2 + x
    halves = (0, 1)
    h_in = [hid.at[pl.ds(c * half_rows, half_rows)] for c in halves]
    w_in = [wgt.at[pl.ds(c * half_depth, half_depth)] for c in halves]
    h_part = [hbuf.at[half_at(own_slot, c)] for c in halves]
    w_part = [wsrc.at[pl.ds(c * half_depth, half_depth)] for c in halves]
    w_land = [wbuf.at[pl.ds(c * half_depth, half_depth), cols_at(b)] for c in halves]

    own_h = [pltpu.make_async_copy(h_in[c], hbuf.at[half_at(own_slot, c)], h_recv.at[own_slot, c]) for c in halves]
    for c in halves:
        own_h[c].start()

    @pl.when(a == b)
    def _():
        for c in halves:
            pltpu.make_async_copy(w_in[c], w_land[c], w_recv.at[b, c]).start()

    for n in (1, 3, 2):
        loads[n].start()
    barrier = pltpu.get_barrier_semaphore()
    for k in range(1, npool):
        pl.semaphore_signal(barrier, inc=1, device_id={"pool": peer(k)}, device_id_type=MESH)
    for sx in range(2):
        for k in range(1, 4):
            pl.semaphore_signal(
                barrier, inc=1,
                device_id={"pool": (2 * a + y) * 2 + sx, "tp": lax.rem(t + k, 4)}, device_id_type=MESH,
            )
    loads[0].wait()

    wanted = [retr[0, f] for f in range(fetch)]
    owners = [lax.div(v, blocks_dev) for v in wanted]
    locals_ = [lax.rem(v, blocks_dev) for v in wanted]

    def slot_at(owner):
        total = jnp.int32(0)
        for f in range(fetch):
            total = total + jnp.where(owners[f] == owner, locals_[f], 0)
        return total

    ask, answers = [None], [None]
    for k in range(1, npool):
        msg_out[k] = jnp.full((8, 128), slot_at(peer(k)), jnp.int32)
        ask.append(remote(msg_out.at[k], msg_in.at[k], m_send.at[k], m_recv.at[k], peer(k)))
    for c in halves:
        own_h[c].wait()
    loads[4].wait()
    pl.semaphore_wait(barrier, npool - 1 + jnp.where(y == b, 4, 8))

    h_pair = [remote(h_part[c], hbuf.at[half_at(own_slot, c)], p_send.at[c], h_recv.at[own_slot, c], pair) for c in halves]
    h_other = [remote(h_part[c], hbuf.at[half_at(own_slot, c)], x_send.at[c], h_recv.at[own_slot, c], other) for c in halves]
    h_fwd = [
        remote(hbuf.at[half_at(pair_slot, c)], hbuf.at[half_at(pair_slot, c)], f_send.at[c], h_recv.at[pair_slot, c], other)
        for c in halves
    ]
    w_far = [remote(w_part[c], w_land[c], w_send.at[c], w_recv.at[b, c], far) for c in halves]
    w_near = [remote(w_part[c], w_land[c], v_send.at[c], w_recv.at[b, c], pair) for c in halves]

    for k in range(1, npool):
        ask[k].start()
    for c in halves:
        h_pair[c].start()
    for c in halves:
        h_other[c].start()

    @pl.when(a != b)
    def _():
        for c in halves:
            w_far[c].start()

    def h_wait(slot, c):
        pltpu.make_async_copy(h_in[c], hbuf.at[half_at(slot, c)], h_recv.at[slot, c]).wait()

    for c in halves:
        h_pair[c].wait_send()

        @pl.when(a == b)
        def _():
            w_far[c].start()

        @pl.when(a != b)
        def _():
            w_near[c].start()

        h_wait(pair_slot, c)
        h_fwd[c].start()
        if c == 0:
            loads[1].wait()
            arrived[0] = cache[slot_at(me)]
            for k in range(1, npool):
                ask[k].wait_recv()
                reply[k] = cache[jnp.max(msg_in[k])]
                answers.append(remote(reply.at[k], arrived.at[k], a_send.at[k], a_recv.at[k], peer(k)))
    for c in halves:
        w_far[c].wait_send()

        @pl.when(a != b)
        def _():
            w_near[c].wait_send()

        for k in ((), (6, 7, 1))[c]:
            answers[k].start()

    def w_wait(c):
        for n in range(2):
            pltpu.make_async_copy(
                w_in[c], wbuf.at[pl.ds(c * half_depth, half_depth), pl.ds(n * HD, HD)], w_recv.at[n, c]
            ).wait()

    def product(zl, c):
        at = pl.ds(c * half_depth, half_depth)
        return jnp.dot(hbuf[rows_at(zl * 2, 2), at], wbuf[at, :], preferred_element_type=jnp.float32)

    def hand_out(zl, block):
        for sx in range(2):
            for i in range(2):
                j = zl * 2 + sx
                src = pbuf.at[j, i]
                src[...] = block[sx * rows:(sx + 1) * rows, i * HD:(i + 1) * HD].astype(jnp.bfloat16)
                mine = jnp.logical_and(4 * a + j == me, 2 * b + i == t)

                @pl.when(mine)
                def _():
                    pltpu.make_async_copy(src, part.at[x, t], s_recv.at[x, t]).start()

                @pl.when(jnp.logical_not(mine))
                def _():
                    remote(src, part.at[x, t], s_send.at[j, i], s_recv.at[x, t], 4 * a + j, 2 * b + i).start()

    for c in halves:
        h_wait(b * 2 + 1 - x, c)
    w_wait(0)
    first = product(b, 0)
    w_wait(1)
    for c in halves:
        h_wait((1 - b) * 2 + 1 - x, c)
    hand_out(1 - b, product(1 - b, 0) + product(1 - b, 1))
    hand_out(b, first + product(b, 1))
    for k in (2, 3, 4, 5):
        answers[k].start()

    token = lax.broadcasted_iota(jnp.int32, (rows, rows), 0)
    near_bias[...] = jnp.where(token >= lax.broadcasted_iota(jnp.int32, (rows, rows), 1), 0.0, -1e30)
    loads[2].wait()
    loads[3].wait()

    rate = float(HD) ** (-0.5) * math.log2(math.e)
    r_blocks = pat.shape[1]

    def bias_of(k, r):
        owner = me if k == 0 else peer(k)
        named = jnp.int32(0)
        for f in range(fetch):
            named = named + jnp.where(owners[f] == owner, pat[0, r, f], 0)
        return jnp.where(named != 0, jnp.float32(0.0), jnp.float32(-1e30))

    def stage(first, near, ks, last):
        biases = [[bias_of(k, r) for r in range(r_blocks)] for k in ks]

        @pl.loop(0, q_ref.shape[1] // (2 * HD), unroll=2)
        def _(step):
            ats = [pl.ds(pl.multiple_of(step * 2 * HD + h * HD, HD), HD) for h in range(2)]
            keys = [arrived[k, :, 0:HD] for k in ks]
            vals = [arrived[k, :, HD:2 * HD] for k in ks]
            if near:
                keys.append(fresh[:, 0:HD])
                vals.append(fresh[:, HD:2 * HD])
            keys = jnp.concatenate(keys, axis=0)
            vals = jnp.concatenate(vals, axis=0)
            vals = jnp.concatenate([vals, jnp.ones_like(vals)], axis=1)
            raw = rows_by_keys(jnp.concatenate([q_ref[:, at] for at in ats], axis=0), keys)
            rounded, factors = [], []
            for h in range(2):
                scores = []
                for n in range(len(ks)):
                    scores.append(jnp.concatenate([
                        raw[h * rows + r * RBLK:h * rows + (r + 1) * RBLK, n * BLK:(n + 1) * BLK] + biases[n][r]
                        for r in range(r_blocks)
                    ], axis=0))
                if near:
                    scores.append(raw[h * rows:(h + 1) * rows, len(ks) * BLK:] + near_bias[...])
                top = scores[0]
                for one in scores[1:]:
                    top = jnp.maximum(top, one)
                top = jnp.broadcast_to(jnp.max(top, axis=1, keepdims=True), (rows, HD))
                if not first:
                    before = top_ref[2 * step + h]
                    top = jnp.maximum(before, top)
                    factors.append(jnp.exp2((before - top) * rate))
                if not last:
                    top_ref[2 * step + h] = top
                rounded.append(jnp.concatenate(
                    [jnp.exp2((one - top) * rate).astype(jnp.bfloat16) for one in scores], axis=1
                ))
            both = jnp.dot(jnp.concatenate(rounded, axis=0), vals, preferred_element_type=jnp.float32)
            for h in range(2):
                numer = both[h * rows:(h + 1) * rows, 0:HD]
                denom = both[h * rows:(h + 1) * rows, HD:2 * HD]
                if not first:
                    numer = numer + factors[h] * acc_ref[2 * step + h, :, 0:HD]
                    denom = denom + factors[h] * acc_ref[2 * step + h, :, HD:2 * HD]
                if last:
                    att[:, ats[h]] = (numer / denom).astype(jnp.bfloat16)
                else:
                    acc_ref[2 * step + h, :, 0:HD] = numer
                    acc_ref[2 * step + h, :, HD:2 * HD] = denom

    for k in (1, 6, 7):
        answers[k].wait_recv()
    stage(True, False, (0, 1, 6, 7), False)
    for kind in range(2):
        total = jnp.zeros((rows, HD), jnp.float32)
        for n in range(4):
            pltpu.make_async_copy(pbuf.at[0, 0], part.at[kind, n], s_recv.at[kind, n]).wait()
            total = total + part[kind, n].astype(jnp.float32)
        fresh[:, kind * HD:(kind + 1) * HD] = total.astype(jnp.bfloat16)
    for k in (2, 3):
        answers[k].wait_recv()
    stage(False, True, (2, 3), False)
    for k in (4, 5):
        answers[k].wait_recv()
    stage(False, False, (4, 5), True)

    for c in halves:
        h_other[c].wait_send()
        h_fwd[c].wait_send()
    for k in range(1, npool):
        ask[k].wait_send()
        answers[k].wait_send()
    for j in range(4):
        for i in range(2):
            mine = jnp.logical_and(4 * a + j == me, 2 * b + i == t)

            @pl.when(jnp.logical_not(mine))
            def _():
                remote(pbuf.at[j, i], part.at[x, t], s_send.at[j, i], s_recv.at[x, t], 4 * a + j, 2 * b + i).wait_send()


def fused(hidden_rows, kv_weight, queries, cache_table, retrieval, pattern):
    rows, depth = hidden_rows.shape
    cols = kv_weight.shape[1]
    blocks_dev, _, width = cache_table.shape
    dma = pltpu.SemaphoreType.DMA
    hbm = pl.BlockSpec(memory_space=pltpu.HBM)
    vmem = pl.BlockSpec(memory_space=pltpu.VMEM)
    bf = jnp.bfloat16
    return pl.pallas_call(
        kernel,
        out_shape=(
            pltpu.VMEM(queries.shape, bf),
            pltpu.VMEM((rows, width), bf),
        ),
        in_specs=[hbm] * 6,
        out_specs=(vmem, vmem),
        scratch_shapes=[
            pltpu.VMEM((4 * rows, depth), bf),
            pltpu.VMEM((depth, 2 * cols), bf),
            pltpu.VMEM((depth, cols), bf),
            pltpu.VMEM((4, 2, rows, HD), bf),
            pltpu.VMEM((2, 4, rows, HD), bf),
            pltpu.VMEM((8, 8, 128), jnp.int32),
            pltpu.VMEM((8, 8, 128), jnp.int32),
            pltpu.VMEM((8, BLK, width), bf),
            pltpu.VMEM((8, BLK, width), bf),
            pltpu.VMEM((queries.shape[1] // HD, rows, HD), jnp.float32),
            pltpu.VMEM((queries.shape[1] // HD, rows, 2 * HD), jnp.float32),
            pltpu.VMEM((rows, rows), jnp.float32),
            pltpu.VMEM(queries.shape, bf),
            pltpu.VMEM(cache_table.shape, bf),
            pltpu.SMEM(retrieval.shape, jnp.int32),
            pltpu.SMEM(pattern.shape, jnp.int32),
            dma((4, 2)), dma((2,)), dma((2,)), dma((2,)), dma((2, 2)), dma((2,)), dma((2,)),
            dma((8,)), dma((8,)), dma((8,)), dma((8,)), dma((2, 4)), dma((4, 2)), dma((5,)),
        ],
        compiler_params=pltpu.CompilerParams(
            collective_id=0, has_side_effects=True, vmem_limit_bytes=62 * 1024 * 1024
        ),
        name="blend",
    )(hidden_rows, kv_weight, queries, cache_table, retrieval, pattern)


def fits(mesh, hidden_rows, kv_weight, cache_table, retrieval):
    return (
        mesh.shape["pool"] == 8
        and mesh.shape["tp"] == 4
        and hidden_rows.shape[0] == 8 * BLK
        and kv_weight.shape[1] == 8 * HD
        and cache_table.shape[2] == 8 * HD
        and retrieval.shape[1] <= 8
    )


def solution(mesh):
    placed = (
        P("pool", "tp"),
        P("tp", "pool"),
        P("pool", "tp"),
        P("pool", None, "tp"),
        P("pool", None),
        P("pool", None, None),
    )

    def run(hidden_rows, kv_weight, queries, cache_table, retrieval, pattern):
        small = fits(mesh, hidden_rows, kv_weight, cache_table, retrieval)
        return jax.shard_map(
            fused if small else body,
            mesh=mesh,
            in_specs=placed,
            out_specs=(P("pool", "tp"), P("pool", "tp")),
            check_vma=False,
        )(hidden_rows, kv_weight, queries, cache_table, retrieval, pattern)

    return run
```

```python
import math

import jax
import jax.numpy as jnp
from jax import lax
from jax.experimental import pallas as pl
from jax.experimental.pallas import tpu as pltpu
from jax.sharding import PartitionSpec as P

HD = 128
QH = 32
KVH = 4
BLK = 128
RBLK = 64


def rows_by_keys(left, right):
    return lax.dot_general(
        left, right, (((1,), (1,)), ((), ())), preferred_element_type=jnp.float32
    )


def body(hidden_rows, kv_weight, queries, cache_table, retrieval, pattern):
    partial_kv = jnp.dot(
        hidden_rows,
        lax.all_gather(kv_weight, "pool", axis=1, tiled=True),
        preferred_element_type=jnp.float32,
    )
    fresh = lax.psum_scatter(partial_kv.astype(jnp.bfloat16), "tp", scatter_dimension=1, tiled=True)
    wanted = retrieval[0]
    blocks_dev = cache_table.shape[0]
    npool = lax.axis_size("pool")
    owners = wanted // blocks_dev
    local = wanted % blocks_dev
    hits = (owners[:, None] == jnp.arange(npool, dtype=jnp.int32)[None, :]).astype(jnp.int32)
    request = jnp.sum(hits * (local + 1)[:, None], axis=0)
    incoming = lax.all_to_all(
        request.reshape(npool, 1), "pool", split_axis=0, concat_axis=0, tiled=True
    ).reshape(npool)
    reply = jnp.zeros((npool,) + cache_table.shape[1:], jnp.bfloat16)
    for slot in range(blocks_dev):
        reply = jnp.where((incoming == slot + 1)[:, None, None], cache_table[slot][None], reply)
    arrived = lax.all_to_all(reply, "pool", split_axis=0, concat_axis=0, tiled=True)
    fetched = jnp.take(arrived, owners, axis=0)
    count = hidden_rows.shape[0]
    fetch_count = wanted.shape[0]
    group = QH // KVH
    scale = float(HD) ** (-0.5)
    local_heads = fresh.shape[1] // (2 * HD)
    width = fetched.shape[2]
    per_step = math.gcd(fetch_count, 8)
    steps_count = fetch_count // per_step
    grouped = fetched.reshape(steps_count, per_step * BLK, width)
    pat_steps = jnp.transpose(
        pattern[0].reshape(pattern.shape[1], steps_count, per_step), (1, 0, 2)
    )
    token_of_row = jnp.arange(count * group) // group
    block_of_row = token_of_row // RBLK
    row_blocks = block_of_row[:, None, None] == jnp.arange(pattern.shape[1])[None, :, None]
    near_mask = token_of_row[:, None] >= jnp.arange(count)[None, :]
    q_heads = queries.reshape(count, local_heads, group * HD)
    q_rows = q_heads[:, 0].reshape(count * group, HD)
    near_keys = fresh[:, 0:HD]
    near_vals = fresh[:, HD : 2 * HD]
    near_scores = rows_by_keys(q_rows, near_keys) * scale
    top = jnp.max(jnp.where(near_mask, near_scores, -1e30), axis=1)
    weights = jnp.where(near_mask, jnp.exp(near_scores - top[:, None]), 0.0)
    total = jnp.sum(weights, axis=1)
    numer = jnp.dot(weights.astype(jnp.bfloat16), near_vals, preferred_element_type=jnp.float32)

    def visit(carry, items):
        top_now, total_now, numer_now = carry
        block_rows, pat_now = items
        keys = block_rows[:, 0:HD]
        vals = block_rows[:, HD : 2 * HD]
        scores = rows_by_keys(q_rows, keys) * scale
        row_pat = jnp.any(row_blocks & (pat_now[None] != 0), axis=1)
        mask = jnp.repeat(row_pat, BLK, axis=1)
        top_new = jnp.maximum(top_now, jnp.max(jnp.where(mask, scores, -1e30), axis=1))
        weights_now = jnp.where(mask, jnp.exp(scores - top_new[:, None]), 0.0)
        factor = jnp.exp(top_now - top_new)
        total_new = total_now * factor + jnp.sum(weights_now, axis=1)
        numer_new = numer_now * factor[:, None] + jnp.dot(
            weights_now.astype(jnp.bfloat16), vals, preferred_element_type=jnp.float32
        )
        return ((top_new, total_new, numer_new), None)

    (top, total, numer), unused = lax.scan(visit, (top, total, numer), (grouped, pat_steps))
    results = (numer / total[:, None]).reshape(count, group * HD)
    attended = results.astype(jnp.bfloat16)
    return (attended, fresh)


MESH = pl.DeviceIdType.MESH


def kernel(hid, wgt, q_hbm, cache_hbm, retr_hbm, pat_hbm, att, fresh, hbuf, wbuf, wsrc, pbuf, part,
           msg_out, msg_in, reply, arrived, top_ref, acc_ref, near_bias, q_ref, cache, retr, pat,
           h_recv, p_send, x_send, f_send, w_recv, w_send, v_send, m_recv, m_send, a_recv, a_send,
           s_recv, s_send, load_sem):
    npool = 8
    blocks_dev = cache.shape[0]
    fetch = retr.shape[1]
    rows, depth = hid.shape
    half_rows, half_depth = rows // 2, depth // 2
    loads = [
        pltpu.make_async_copy(src, dst, load_sem.at[n])
        for n, (src, dst) in enumerate(((retr_hbm, retr), (cache_hbm, cache), (q_hbm, q_ref), (pat_hbm, pat), (wgt, wsrc)))
    ]
    loads[0].start()
    loads[4].start()
    me = lax.axis_index("pool")
    t = lax.axis_index("tp")
    z, x = lax.div(me, 2), lax.rem(me, 2)
    a, b = lax.div(z, 2), lax.rem(z, 2)
    y = lax.div(t, 2)
    pair = (2 * a + 1 - b) * 2 + x
    other = z * 2 + 1 - x
    far = (2 - a) * 2 + x

    def peer(k):
        pa = 1 - a if k & 4 else a
        pb = 1 - b if k & 2 else b
        return (2 * pa + pb) * 2 + (1 - x if k & 1 else x)

    def remote(src, dst, ssem, rsem, pool, tp=None):
        where = {"pool": pool} if tp is None else {"pool": pool, "tp": tp}
        return pltpu.make_async_remote_copy(
            src_ref=src, dst_ref=dst, send_sem=ssem, recv_sem=rsem, device_id=where, device_id_type=MESH
        )

    def rows_at(slot, count=1):
        return pl.ds(pl.multiple_of(slot * rows, rows), count * rows)

    def half_at(slot, c):
        return pl.ds(pl.multiple_of(slot * rows + c * half_rows, half_rows), half_rows)

    def cols_at(slot):
        return pl.ds(pl.multiple_of(slot * HD, HD), HD)

    own_slot = b * 2 + x
    pair_slot = (1 - b) * 2 + x
    halves = (0, 1)
    h_in = [hid.at[pl.ds(c * half_rows, half_rows)] for c in halves]
    w_in = [wgt.at[pl.ds(c * half_depth, half_depth)] for c in halves]
    h_part = [hbuf.at[half_at(own_slot, c)] for c in halves]
    w_part = [wsrc.at[pl.ds(c * half_depth, half_depth)] for c in halves]
    w_land = [wbuf.at[pl.ds(c * half_depth, half_depth), cols_at(b)] for c in halves]

    own_h = [pltpu.make_async_copy(h_in[c], hbuf.at[half_at(own_slot, c)], h_recv.at[own_slot, c]) for c in halves]
    for c in halves:
        own_h[c].start()

    @pl.when(a == b)
    def _():
        for c in halves:
            pltpu.make_async_copy(w_in[c], w_land[c], w_recv.at[b, c]).start()

    for n in (1, 3, 2):
        loads[n].start()
    barrier = pltpu.get_barrier_semaphore()
    for k in range(1, npool):
        pl.semaphore_signal(barrier, inc=1, device_id={"pool": peer(k)}, device_id_type=MESH)
    for sx in range(2):
        for k in range(1, 4):
            pl.semaphore_signal(
                barrier, inc=1,
                device_id={"pool": (2 * a + y) * 2 + sx, "tp": lax.rem(t + k, 4)}, device_id_type=MESH,
            )
    loads[0].wait()

    wanted = [retr[0, f] for f in range(fetch)]
    owners = [lax.div(v, blocks_dev) for v in wanted]
    locals_ = [lax.rem(v, blocks_dev) for v in wanted]

    def slot_at(owner):
        total = jnp.int32(0)
        for f in range(fetch):
            total = total + jnp.where(owners[f] == owner, locals_[f], 0)
        return total

    ask, answers = [None], [None]
    for k in range(1, npool):
        msg_out[k] = jnp.full((8, 128), slot_at(peer(k)), jnp.int32)
        ask.append(remote(msg_out.at[k], msg_in.at[k], m_send.at[k], m_recv.at[k], peer(k)))
    for c in halves:
        own_h[c].wait()
    loads[4].wait()
    pl.semaphore_wait(barrier, npool - 1 + jnp.where(y == b, 4, 8))

    h_pair = [remote(h_part[c], hbuf.at[half_at(own_slot, c)], p_send.at[c], h_recv.at[own_slot, c], pair) for c in halves]
    h_other = [remote(h_part[c], hbuf.at[half_at(own_slot, c)], x_send.at[c], h_recv.at[own_slot, c], other) for c in halves]
    h_fwd = [
        remote(hbuf.at[half_at(pair_slot, c)], hbuf.at[half_at(pair_slot, c)], f_send.at[c], h_recv.at[pair_slot, c], other)
        for c in halves
    ]
    w_far = [remote(w_part[c], w_land[c], w_send.at[c], w_recv.at[b, c], far) for c in halves]
    w_near = [remote(w_part[c], w_land[c], v_send.at[c], w_recv.at[b, c], pair) for c in halves]

    for k in range(1, npool):
        ask[k].start()
    for c in halves:
        h_pair[c].start()
    for c in halves:
        h_other[c].start()

    @pl.when(a != b)
    def _():
        for c in halves:
            w_far[c].start()

    def h_wait(slot, c):
        pltpu.make_async_copy(h_in[c], hbuf.at[half_at(slot, c)], h_recv.at[slot, c]).wait()

    for c in halves:
        h_pair[c].wait_send()

        @pl.when(a == b)
        def _():
            w_far[c].start()

        @pl.when(a != b)
        def _():
            w_near[c].start()

        h_wait(pair_slot, c)
        h_fwd[c].start()
        if c == 0:
            loads[1].wait()
            arrived[0] = cache[slot_at(me)]
            for k in range(1, npool):
                ask[k].wait_recv()
                reply[k] = cache[jnp.max(msg_in[k])]
                answers.append(remote(reply.at[k], arrived.at[k], a_send.at[k], a_recv.at[k], peer(k)))
    for c in halves:
        w_far[c].wait_send()

        @pl.when(a != b)
        def _():
            w_near[c].wait_send()

        for k in ((6, 7), (2, 3, 1, 4))[c]:
            answers[k].start()

    def w_wait(c):
        for n in range(2):
            pltpu.make_async_copy(
                w_in[c], wbuf.at[pl.ds(c * half_depth, half_depth), pl.ds(n * HD, HD)], w_recv.at[n, c]
            ).wait()

    def product(zl, c):
        at = pl.ds(c * half_depth, half_depth)
        return jnp.dot(hbuf[rows_at(zl * 2, 2), at], wbuf[at, :], preferred_element_type=jnp.float32)

    def hand_out(zl, block):
        for sx in range(2):
            for i in range(2):
                j = zl * 2 + sx
                src = pbuf.at[j, i]
                src[...] = block[sx * rows:(sx + 1) * rows, i * HD:(i + 1) * HD].astype(jnp.bfloat16)
                mine = jnp.logical_and(4 * a + j == me, 2 * b + i == t)

                @pl.when(mine)
                def _():
                    pltpu.make_async_copy(src, part.at[x, t], s_recv.at[x, t]).start()

                @pl.when(jnp.logical_not(mine))
                def _():
                    remote(src, part.at[x, t], s_send.at[j, i], s_recv.at[x, t], 4 * a + j, 2 * b + i).start()

    for c in halves:
        h_wait(b * 2 + 1 - x, c)
    w_wait(0)
    first = product(b, 0)
    w_wait(1)
    hand_out(b, first + product(b, 1))
    for c in halves:
        h_wait((1 - b) * 2 + 1 - x, c)
    hand_out(1 - b, product(1 - b, 0) + product(1 - b, 1))
    answers[5].start()

    token = lax.broadcasted_iota(jnp.int32, (rows, rows), 0)
    near_bias[...] = jnp.where(token >= lax.broadcasted_iota(jnp.int32, (rows, rows), 1), 0.0, -1e30)
    loads[2].wait()
    loads[3].wait()

    rate = float(HD) ** (-0.5) * math.log2(math.e)
    r_blocks = pat.shape[1]

    def bias_of(k, r):
        owner = me if k == 0 else peer(k)
        named = jnp.int32(0)
        for f in range(fetch):
            named = named + jnp.where(owners[f] == owner, pat[0, r, f], 0)
        return jnp.where(named != 0, jnp.float32(0.0), jnp.float32(-1e30))

    def stage(first, near, ks, last):
        biases = [[bias_of(k, r) for r in range(r_blocks)] for k in ks]

        @pl.loop(0, q_ref.shape[1] // (2 * HD), unroll=2)
        def _(step):
            ats = [pl.ds(pl.multiple_of(step * 2 * HD + h * HD, HD), HD) for h in range(2)]
            keys = [arrived[k, :, 0:HD] for k in ks]
            vals = [arrived[k, :, HD:2 * HD] for k in ks]
            if near:
                keys.append(fresh[:, 0:HD])
                vals.append(fresh[:, HD:2 * HD])
            keys = jnp.concatenate(keys, axis=0)
            vals = jnp.concatenate(vals, axis=0)
            vals = jnp.concatenate([vals, jnp.ones_like(vals)], axis=1)
            raw = rows_by_keys(jnp.concatenate([q_ref[:, at] for at in ats], axis=0), keys)
            rounded, factors = [], []
            for h in range(2):
                scores = []
                for n in range(len(ks)):
                    scores.append(jnp.concatenate([
                        raw[h * rows + r * RBLK:h * rows + (r + 1) * RBLK, n * BLK:(n + 1) * BLK] + biases[n][r]
                        for r in range(r_blocks)
                    ], axis=0))
                if near:
                    scores.append(raw[h * rows:(h + 1) * rows, len(ks) * BLK:] + near_bias[...])
                top = scores[0]
                for one in scores[1:]:
                    top = jnp.maximum(top, one)
                top = jnp.broadcast_to(jnp.max(top, axis=1, keepdims=True), (rows, HD))
                if not first:
                    before = top_ref[2 * step + h]
                    top = jnp.maximum(before, top)
                    factors.append(jnp.exp2((before - top) * rate))
                if not last:
                    top_ref[2 * step + h] = top
                rounded.append(jnp.concatenate(
                    [jnp.exp2((one - top) * rate).astype(jnp.bfloat16) for one in scores], axis=1
                ))
            both = jnp.dot(jnp.concatenate(rounded, axis=0), vals, preferred_element_type=jnp.float32)
            for h in range(2):
                numer = both[h * rows:(h + 1) * rows, 0:HD]
                denom = both[h * rows:(h + 1) * rows, HD:2 * HD]
                if not first:
                    numer = numer + factors[h] * acc_ref[2 * step + h, :, 0:HD]
                    denom = denom + factors[h] * acc_ref[2 * step + h, :, HD:2 * HD]
                if last:
                    att[:, ats[h]] = (numer / denom).astype(jnp.bfloat16)
                else:
                    acc_ref[2 * step + h, :, 0:HD] = numer
                    acc_ref[2 * step + h, :, HD:2 * HD] = denom

    for k in (1, 2, 3):
        answers[k].wait_recv()
    stage(True, False, (0, 1, 2, 3), False)
    for k in (6, 7, 4):
        answers[k].wait_recv()
    stage(False, False, (6, 7, 4), False)
    for kind in range(2):
        total = jnp.zeros((rows, HD), jnp.float32)
        for n in range(4):
            pltpu.make_async_copy(pbuf.at[0, 0], part.at[kind, n], s_recv.at[kind, n]).wait()
            total = total + part[kind, n].astype(jnp.float32)
        fresh[:, kind * HD:(kind + 1) * HD] = total.astype(jnp.bfloat16)
    answers[5].wait_recv()
    stage(False, True, (5,), True)

    for c in halves:
        h_other[c].wait_send()
        h_fwd[c].wait_send()
    for k in range(1, npool):
        ask[k].wait_send()
        answers[k].wait_send()
    for j in range(4):
        for i in range(2):
            mine = jnp.logical_and(4 * a + j == me, 2 * b + i == t)

            @pl.when(jnp.logical_not(mine))
            def _():
                remote(pbuf.at[j, i], part.at[x, t], s_send.at[j, i], s_recv.at[x, t], 4 * a + j, 2 * b + i).wait_send()


def fused(hidden_rows, kv_weight, queries, cache_table, retrieval, pattern):
    rows, depth = hidden_rows.shape
    cols = kv_weight.shape[1]
    blocks_dev, _, width = cache_table.shape
    dma = pltpu.SemaphoreType.DMA
    hbm = pl.BlockSpec(memory_space=pltpu.HBM)
    vmem = pl.BlockSpec(memory_space=pltpu.VMEM)
    bf = jnp.bfloat16
    return pl.pallas_call(
        kernel,
        out_shape=(
            pltpu.VMEM(queries.shape, bf),
            pltpu.VMEM((rows, width), bf),
        ),
        in_specs=[hbm] * 6,
        out_specs=(vmem, vmem),
        scratch_shapes=[
            pltpu.VMEM((4 * rows, depth), bf),
            pltpu.VMEM((depth, 2 * cols), bf),
            pltpu.VMEM((depth, cols), bf),
            pltpu.VMEM((4, 2, rows, HD), bf),
            pltpu.VMEM((2, 4, rows, HD), bf),
            pltpu.VMEM((8, 8, 128), jnp.int32),
            pltpu.VMEM((8, 8, 128), jnp.int32),
            pltpu.VMEM((8, BLK, width), bf),
            pltpu.VMEM((8, BLK, width), bf),
            pltpu.VMEM((queries.shape[1] // HD, rows, HD), jnp.float32),
            pltpu.VMEM((queries.shape[1] // HD, rows, 2 * HD), jnp.float32),
            pltpu.VMEM((rows, rows), jnp.float32),
            pltpu.VMEM(queries.shape, bf),
            pltpu.VMEM(cache_table.shape, bf),
            pltpu.SMEM(retrieval.shape, jnp.int32),
            pltpu.SMEM(pattern.shape, jnp.int32),
            dma((4, 2)), dma((2,)), dma((2,)), dma((2,)), dma((2, 2)), dma((2,)), dma((2,)),
            dma((8,)), dma((8,)), dma((8,)), dma((8,)), dma((2, 4)), dma((4, 2)), dma((5,)),
        ],
        compiler_params=pltpu.CompilerParams(
            collective_id=0, has_side_effects=True, vmem_limit_bytes=62 * 1024 * 1024
        ),
        name="blend",
    )(hidden_rows, kv_weight, queries, cache_table, retrieval, pattern)


def fits(mesh, hidden_rows, kv_weight, cache_table, retrieval):
    return (
        mesh.shape["pool"] == 8
        and mesh.shape["tp"] == 4
        and hidden_rows.shape[0] == 8 * BLK
        and kv_weight.shape[1] == 8 * HD
        and cache_table.shape[2] == 8 * HD
        and retrieval.shape[1] <= 8
    )


def solution(mesh):
    placed = (
        P("pool", "tp"),
        P("tp", "pool"),
        P("pool", "tp"),
        P("pool", None, "tp"),
        P("pool", None),
        P("pool", None, None),
    )

    def run(hidden_rows, kv_weight, queries, cache_table, retrieval, pattern):
        small = fits(mesh, hidden_rows, kv_weight, cache_table, retrieval)
        return jax.shard_map(
            fused if small else body,
            mesh=mesh,
            in_specs=placed,
            out_specs=(P("pool", "tp"), P("pool", "tp")),
            check_vma=False,
        )(hidden_rows, kv_weight, queries, cache_table, retrieval, pattern)

    return run
```

```python
import math

import jax
import jax.numpy as jnp
from jax import lax
from jax.experimental import pallas as pl
from jax.experimental.pallas import tpu as pltpu
from jax.sharding import PartitionSpec as P

HD = 128
QH = 32
KVH = 4
BLK = 128
RBLK = 64


def rows_by_keys(left, right):
    return lax.dot_general(
        left, right, (((1,), (1,)), ((), ())), preferred_element_type=jnp.float32
    )


def body(hidden_rows, kv_weight, queries, cache_table, retrieval, pattern):
    partial_kv = jnp.dot(
        hidden_rows,
        lax.all_gather(kv_weight, "pool", axis=1, tiled=True),
        preferred_element_type=jnp.float32,
    )
    fresh = lax.psum_scatter(partial_kv.astype(jnp.bfloat16), "tp", scatter_dimension=1, tiled=True)
    wanted = retrieval[0]
    blocks_dev = cache_table.shape[0]
    npool = lax.axis_size("pool")
    owners = wanted // blocks_dev
    local = wanted % blocks_dev
    hits = (owners[:, None] == jnp.arange(npool, dtype=jnp.int32)[None, :]).astype(jnp.int32)
    request = jnp.sum(hits * (local + 1)[:, None], axis=0)
    incoming = lax.all_to_all(
        request.reshape(npool, 1), "pool", split_axis=0, concat_axis=0, tiled=True
    ).reshape(npool)
    reply = jnp.zeros((npool,) + cache_table.shape[1:], jnp.bfloat16)
    for slot in range(blocks_dev):
        reply = jnp.where((incoming == slot + 1)[:, None, None], cache_table[slot][None], reply)
    arrived = lax.all_to_all(reply, "pool", split_axis=0, concat_axis=0, tiled=True)
    fetched = jnp.take(arrived, owners, axis=0)
    count = hidden_rows.shape[0]
    fetch_count = wanted.shape[0]
    group = QH // KVH
    scale = float(HD) ** (-0.5)
    local_heads = fresh.shape[1] // (2 * HD)
    width = fetched.shape[2]
    per_step = math.gcd(fetch_count, 8)
    steps_count = fetch_count // per_step
    grouped = fetched.reshape(steps_count, per_step * BLK, width)
    pat_steps = jnp.transpose(
        pattern[0].reshape(pattern.shape[1], steps_count, per_step), (1, 0, 2)
    )
    token_of_row = jnp.arange(count * group) // group
    block_of_row = token_of_row // RBLK
    row_blocks = block_of_row[:, None, None] == jnp.arange(pattern.shape[1])[None, :, None]
    near_mask = token_of_row[:, None] >= jnp.arange(count)[None, :]
    q_heads = queries.reshape(count, local_heads, group * HD)
    q_rows = q_heads[:, 0].reshape(count * group, HD)
    near_keys = fresh[:, 0:HD]
    near_vals = fresh[:, HD : 2 * HD]
    near_scores = rows_by_keys(q_rows, near_keys) * scale
    top = jnp.max(jnp.where(near_mask, near_scores, -1e30), axis=1)
    weights = jnp.where(near_mask, jnp.exp(near_scores - top[:, None]), 0.0)
    total = jnp.sum(weights, axis=1)
    numer = jnp.dot(weights.astype(jnp.bfloat16), near_vals, preferred_element_type=jnp.float32)

    def visit(carry, items):
        top_now, total_now, numer_now = carry
        block_rows, pat_now = items
        keys = block_rows[:, 0:HD]
        vals = block_rows[:, HD : 2 * HD]
        scores = rows_by_keys(q_rows, keys) * scale
        row_pat = jnp.any(row_blocks & (pat_now[None] != 0), axis=1)
        mask = jnp.repeat(row_pat, BLK, axis=1)
        top_new = jnp.maximum(top_now, jnp.max(jnp.where(mask, scores, -1e30), axis=1))
        weights_now = jnp.where(mask, jnp.exp(scores - top_new[:, None]), 0.0)
        factor = jnp.exp(top_now - top_new)
        total_new = total_now * factor + jnp.sum(weights_now, axis=1)
        numer_new = numer_now * factor[:, None] + jnp.dot(
            weights_now.astype(jnp.bfloat16), vals, preferred_element_type=jnp.float32
        )
        return ((top_new, total_new, numer_new), None)

    (top, total, numer), unused = lax.scan(visit, (top, total, numer), (grouped, pat_steps))
    results = (numer / total[:, None]).reshape(count, group * HD)
    attended = results.astype(jnp.bfloat16)
    return (attended, fresh)


MESH = pl.DeviceIdType.MESH


def kernel(hid, wgt, q_hbm, cache_hbm, retr_hbm, pat_hbm, att, fresh, hbuf, wbuf, wsrc, pbuf, part,
           msg_out, msg_in, reply, arrived, top_ref, acc_ref, near_bias, q_ref, cache, retr, pat,
           h_recv, p_send, x_send, f_send, w_recv, w_send, v_send, m_recv, m_send, a_recv, a_send,
           s_recv, s_send, load_sem):
    npool = 8
    blocks_dev = cache.shape[0]
    fetch = retr.shape[1]
    rows, depth = hid.shape
    half_rows, half_depth = rows // 2, depth // 2
    loads = [
        pltpu.make_async_copy(src, dst, load_sem.at[n])
        for n, (src, dst) in enumerate(((retr_hbm, retr), (cache_hbm, cache), (q_hbm, q_ref), (pat_hbm, pat), (wgt, wsrc)))
    ]
    loads[0].start()
    loads[4].start()
    me = lax.axis_index("pool")
    t = lax.axis_index("tp")
    z, x = lax.div(me, 2), lax.rem(me, 2)
    a, b = lax.div(z, 2), lax.rem(z, 2)
    y = lax.div(t, 2)
    pair = (2 * a + 1 - b) * 2 + x
    other = z * 2 + 1 - x
    far = (2 - a) * 2 + x

    def peer(k):
        pa = 1 - a if k & 4 else a
        pb = 1 - b if k & 2 else b
        return (2 * pa + pb) * 2 + (1 - x if k & 1 else x)

    def remote(src, dst, ssem, rsem, pool, tp=None):
        where = {"pool": pool} if tp is None else {"pool": pool, "tp": tp}
        return pltpu.make_async_remote_copy(
            src_ref=src, dst_ref=dst, send_sem=ssem, recv_sem=rsem, device_id=where, device_id_type=MESH
        )

    def rows_at(slot, count=1):
        return pl.ds(pl.multiple_of(slot * rows, rows), count * rows)

    def half_at(slot, c):
        return pl.ds(pl.multiple_of(slot * rows + c * half_rows, half_rows), half_rows)

    def cols_at(slot):
        return pl.ds(pl.multiple_of(slot * HD, HD), HD)

    own_slot = b * 2 + x
    pair_slot = (1 - b) * 2 + x
    halves = (0, 1)
    h_in = [hid.at[pl.ds(c * half_rows, half_rows)] for c in halves]
    w_in = [wgt.at[pl.ds(c * half_depth, half_depth)] for c in halves]
    h_part = [hbuf.at[half_at(own_slot, c)] for c in halves]
    w_part = [wsrc.at[pl.ds(c * half_depth, half_depth)] for c in halves]
    w_land = [wbuf.at[pl.ds(c * half_depth, half_depth), cols_at(b)] for c in halves]

    own_h = [pltpu.make_async_copy(h_in[c], hbuf.at[half_at(own_slot, c)], h_recv.at[own_slot, c]) for c in halves]
    for c in halves:
        own_h[c].start()

    @pl.when(a == b)
    def _():
        for c in halves:
            pltpu.make_async_copy(w_in[c], w_land[c], w_recv.at[b, c]).start()

    for n in (1, 3, 2):
        loads[n].start()
    barrier = pltpu.get_barrier_semaphore()
    for k in range(1, npool):
        pl.semaphore_signal(barrier, inc=1, device_id={"pool": peer(k)}, device_id_type=MESH)
    for sx in range(2):
        for k in range(1, 4):
            pl.semaphore_signal(
                barrier, inc=1,
                device_id={"pool": (2 * a + y) * 2 + sx, "tp": lax.rem(t + k, 4)}, device_id_type=MESH,
            )
    loads[0].wait()

    wanted = [retr[0, f] for f in range(fetch)]
    owners = [lax.div(v, blocks_dev) for v in wanted]
    locals_ = [lax.rem(v, blocks_dev) for v in wanted]

    def slot_at(owner):
        total = jnp.int32(0)
        for f in range(fetch):
            total = total + jnp.where(owners[f] == owner, locals_[f], 0)
        return total

    ask, answers = [None], [None]
    for k in range(1, npool):
        msg_out[k] = jnp.full((8, 128), slot_at(peer(k)), jnp.int32)
        ask.append(remote(msg_out.at[k], msg_in.at[k], m_send.at[k], m_recv.at[k], peer(k)))
    for c in halves:
        own_h[c].wait()
    loads[4].wait()
    pl.semaphore_wait(barrier, npool - 1 + jnp.where(y == b, 4, 8))

    h_pair = [remote(h_part[c], hbuf.at[half_at(own_slot, c)], p_send.at[c], h_recv.at[own_slot, c], pair) for c in halves]
    h_other = [remote(h_part[c], hbuf.at[half_at(own_slot, c)], x_send.at[c], h_recv.at[own_slot, c], other) for c in halves]
    h_fwd = [
        remote(hbuf.at[half_at(pair_slot, c)], hbuf.at[half_at(pair_slot, c)], f_send.at[c], h_recv.at[pair_slot, c], other)
        for c in halves
    ]
    w_far = [remote(w_part[c], w_land[c], w_send.at[c], w_recv.at[b, c], far) for c in halves]
    w_near = [remote(w_part[c], w_land[c], v_send.at[c], w_recv.at[b, c], pair) for c in halves]

    for k in range(1, npool):
        ask[k].start()
    for c in halves:
        h_pair[c].start()
    for c in halves:
        h_other[c].start()

    @pl.when(a != b)
    def _():
        for c in halves:
            w_far[c].start()

    def h_wait(slot, c):
        pltpu.make_async_copy(h_in[c], hbuf.at[half_at(slot, c)], h_recv.at[slot, c]).wait()

    for c in halves:
        h_pair[c].wait_send()

        @pl.when(a == b)
        def _():
            w_far[c].start()

        @pl.when(a != b)
        def _():
            w_near[c].start()

        h_wait(pair_slot, c)
        h_fwd[c].start()
        if c == 0:
            loads[1].wait()
            arrived[0] = cache[slot_at(me)]
            for k in range(1, npool):
                ask[k].wait_recv()
                reply[k] = cache[jnp.max(msg_in[k])]
                answers.append(remote(reply.at[k], arrived.at[k], a_send.at[k], a_recv.at[k], peer(k)))
    for c in halves:
        w_far[c].wait_send()

        @pl.when(a != b)
        def _():
            w_near[c].wait_send()

        for k in ((6, 7), (2, 3, 1, 4, 5))[c]:
            answers[k].start()

    def w_wait(c):
        for n in range(2):
            pltpu.make_async_copy(
                w_in[c], wbuf.at[pl.ds(c * half_depth, half_depth), pl.ds(n * HD, HD)], w_recv.at[n, c]
            ).wait()

    def product(zl, c):
        at = pl.ds(c * half_depth, half_depth)
        return jnp.dot(hbuf[rows_at(zl * 2, 2), at], wbuf[at, :], preferred_element_type=jnp.float32)

    def hand_out(zl, block):
        for sx in range(2):
            for i in range(2):
                j = zl * 2 + sx
                src = pbuf.at[j, i]
                src[...] = block[sx * rows:(sx + 1) * rows, i * HD:(i + 1) * HD].astype(jnp.bfloat16)
                mine = jnp.logical_and(4 * a + j == me, 2 * b + i == t)

                @pl.when(mine)
                def _():
                    pltpu.make_async_copy(src, part.at[x, t], s_recv.at[x, t]).start()

                @pl.when(jnp.logical_not(mine))
                def _():
                    remote(src, part.at[x, t], s_send.at[j, i], s_recv.at[x, t], 4 * a + j, 2 * b + i).start()

    for c in halves:
        h_wait(b * 2 + 1 - x, c)
    w_wait(0)
    first = product(b, 0)
    w_wait(1)
    hand_out(b, first + product(b, 1))
    for c in halves:
        h_wait((1 - b) * 2 + 1 - x, c)
    hand_out(1 - b, product(1 - b, 0) + product(1 - b, 1))

    token = lax.broadcasted_iota(jnp.int32, (rows, rows), 0)
    near_bias[...] = jnp.where(token >= lax.broadcasted_iota(jnp.int32, (rows, rows), 1), 0.0, -1e30)
    loads[2].wait()
    loads[3].wait()

    rate = float(HD) ** (-0.5) * math.log2(math.e)
    r_blocks = pat.shape[1]

    def bias_of(k, r):
        owner = me if k == 0 else peer(k)
        named = jnp.int32(0)
        for f in range(fetch):
            named = named + jnp.where(owners[f] == owner, pat[0, r, f], 0)
        return jnp.where(named != 0, jnp.float32(0.0), jnp.float32(-1e30))

    def stage(first, near, ks, last):
        biases = [[bias_of(k, r) for r in range(r_blocks)] for k in ks]

        @pl.loop(0, q_ref.shape[1] // (2 * HD), unroll=2)
        def _(step):
            ats = [pl.ds(pl.multiple_of(step * 2 * HD + h * HD, HD), HD) for h in range(2)]
            keys = [arrived[k, :, 0:HD] for k in ks]
            vals = [arrived[k, :, HD:2 * HD] for k in ks]
            if near:
                keys.append(fresh[:, 0:HD])
                vals.append(fresh[:, HD:2 * HD])
            keys = jnp.concatenate(keys, axis=0)
            vals = jnp.concatenate(vals, axis=0)
            vals = jnp.concatenate([vals, jnp.ones_like(vals)], axis=1)
            raw = rows_by_keys(jnp.concatenate([q_ref[:, at] for at in ats], axis=0), keys)
            rounded, factors = [], []
            for h in range(2):
                scores = []
                for n in range(len(ks)):
                    scores.append(jnp.concatenate([
                        raw[h * rows + r * RBLK:h * rows + (r + 1) * RBLK, n * BLK:(n + 1) * BLK] + biases[n][r]
                        for r in range(r_blocks)
                    ], axis=0))
                if near:
                    scores.append(raw[h * rows:(h + 1) * rows, len(ks) * BLK:] + near_bias[...])
                top = scores[0]
                for one in scores[1:]:
                    top = jnp.maximum(top, one)
                top = jnp.broadcast_to(jnp.max(top, axis=1, keepdims=True), (rows, HD))
                if not first:
                    before = top_ref[2 * step + h]
                    top = jnp.maximum(before, top)
                    factors.append(jnp.exp2((before - top) * rate))
                if not last:
                    top_ref[2 * step + h] = top
                rounded.append(jnp.concatenate(
                    [jnp.exp2((one - top) * rate).astype(jnp.bfloat16) for one in scores], axis=1
                ))
            both = jnp.dot(jnp.concatenate(rounded, axis=0), vals, preferred_element_type=jnp.float32)
            for h in range(2):
                numer = both[h * rows:(h + 1) * rows, 0:HD]
                denom = both[h * rows:(h + 1) * rows, HD:2 * HD]
                if not first:
                    numer = numer + factors[h] * acc_ref[2 * step + h, :, 0:HD]
                    denom = denom + factors[h] * acc_ref[2 * step + h, :, HD:2 * HD]
                if last:
                    att[:, ats[h]] = (numer / denom).astype(jnp.bfloat16)
                else:
                    acc_ref[2 * step + h, :, 0:HD] = numer
                    acc_ref[2 * step + h, :, HD:2 * HD] = denom

    for k in (1, 2, 3):
        answers[k].wait_recv()
    stage(True, False, (0, 1, 2, 3), False)
    for k in (6, 7, 4):
        answers[k].wait_recv()
    stage(False, False, (6, 7, 4), False)
    for kind in range(2):
        total = jnp.zeros((rows, HD), jnp.float32)
        for n in range(4):
            pltpu.make_async_copy(pbuf.at[0, 0], part.at[kind, n], s_recv.at[kind, n]).wait()
            total = total + part[kind, n].astype(jnp.float32)
        fresh[:, kind * HD:(kind + 1) * HD] = total.astype(jnp.bfloat16)
    answers[5].wait_recv()
    stage(False, True, (5,), True)

    for c in halves:
        h_other[c].wait_send()
        h_fwd[c].wait_send()
    for k in range(1, npool):
        ask[k].wait_send()
        answers[k].wait_send()
    for j in range(4):
        for i in range(2):
            mine = jnp.logical_and(4 * a + j == me, 2 * b + i == t)

            @pl.when(jnp.logical_not(mine))
            def _():
                remote(pbuf.at[j, i], part.at[x, t], s_send.at[j, i], s_recv.at[x, t], 4 * a + j, 2 * b + i).wait_send()


def fused(hidden_rows, kv_weight, queries, cache_table, retrieval, pattern):
    rows, depth = hidden_rows.shape
    cols = kv_weight.shape[1]
    blocks_dev, _, width = cache_table.shape
    dma = pltpu.SemaphoreType.DMA
    hbm = pl.BlockSpec(memory_space=pltpu.HBM)
    vmem = pl.BlockSpec(memory_space=pltpu.VMEM)
    bf = jnp.bfloat16
    return pl.pallas_call(
        kernel,
        out_shape=(
            pltpu.VMEM(queries.shape, bf),
            pltpu.VMEM((rows, width), bf),
        ),
        in_specs=[hbm] * 6,
        out_specs=(vmem, vmem),
        scratch_shapes=[
            pltpu.VMEM((4 * rows, depth), bf),
            pltpu.VMEM((depth, 2 * cols), bf),
            pltpu.VMEM((depth, cols), bf),
            pltpu.VMEM((4, 2, rows, HD), bf),
            pltpu.VMEM((2, 4, rows, HD), bf),
            pltpu.VMEM((8, 8, 128), jnp.int32),
            pltpu.VMEM((8, 8, 128), jnp.int32),
            pltpu.VMEM((8, BLK, width), bf),
            pltpu.VMEM((8, BLK, width), bf),
            pltpu.VMEM((queries.shape[1] // HD, rows, HD), jnp.float32),
            pltpu.VMEM((queries.shape[1] // HD, rows, 2 * HD), jnp.float32),
            pltpu.VMEM((rows, rows), jnp.float32),
            pltpu.VMEM(queries.shape, bf),
            pltpu.VMEM(cache_table.shape, bf),
            pltpu.SMEM(retrieval.shape, jnp.int32),
            pltpu.SMEM(pattern.shape, jnp.int32),
            dma((4, 2)), dma((2,)), dma((2,)), dma((2,)), dma((2, 2)), dma((2,)), dma((2,)),
            dma((8,)), dma((8,)), dma((8,)), dma((8,)), dma((2, 4)), dma((4, 2)), dma((5,)),
        ],
        compiler_params=pltpu.CompilerParams(
            collective_id=0, has_side_effects=True, vmem_limit_bytes=62 * 1024 * 1024
        ),
        name="blend",
    )(hidden_rows, kv_weight, queries, cache_table, retrieval, pattern)


def fits(mesh, hidden_rows, kv_weight, cache_table, retrieval):
    return (
        mesh.shape["pool"] == 8
        and mesh.shape["tp"] == 4
        and hidden_rows.shape[0] == 8 * BLK
        and kv_weight.shape[1] == 8 * HD
        and cache_table.shape[2] == 8 * HD
        and retrieval.shape[1] <= 8
    )


def solution(mesh):
    placed = (
        P("pool", "tp"),
        P("tp", "pool"),
        P("pool", "tp"),
        P("pool", None, "tp"),
        P("pool", None),
        P("pool", None, None),
    )

    def run(hidden_rows, kv_weight, queries, cache_table, retrieval, pattern):
        small = fits(mesh, hidden_rows, kv_weight, cache_table, retrieval)
        return jax.shard_map(
            fused if small else body,
            mesh=mesh,
            in_specs=placed,
            out_specs=(P("pool", "tp"), P("pool", "tp")),
            check_vma=False,
        )(hidden_rows, kv_weight, queries, cache_table, retrieval, pattern)

    return run
```
